32 devices in a mesh: dp: 8 (over y, x, core), tensor: 4 (over z).
Axes of the slice: x: 2, y: 2, z: 4, core: 2. Of those that a mesh axis runs over, the one named last changes fastest.
Arguments:
- resid_in: float32 [8192, 1536], P(('dp', 'tensor')), may hold values from -6 to 6
- in_weight: bfloat16 [2, 1536, 2, 3072], P(None, 'dp', None, 'tensor'), may hold values from -0.15625 to 0.15625
- out_weight: bfloat16 [2, 1536, 3072], P(None, 'dp', 'tensor'), may hold values from -0.109375 to 0.109375
- shared_weight: bfloat16 [2, 1536, 304], replicated, may hold values from -0.15625 to 0.15625
- small_params: float32 [2, 21392], replicated, may hold values from -12 to 3.5
- in_momentum: float32 [2, 1536, 2, 3072], P(None, 'dp', None, 'tensor'), may hold values from -256 to 256
- out_momentum: float32 [2, 1536, 3072], P(None, 'dp', 'tensor'), may hold values from -256 to 256
- shared_momentum: float32 [2, 1536, 304], replicated, may hold values from -256 to 256
- small_first: float32 [2, 21392], replicated, may hold values from -119.48181 to 119.48181
- small_second: float32 [2, 21392], replicated, may hold values from 38.78093 to 15512.371
- resid_grad: float32 [8192, 1536], P(('dp', 'tensor')), may hold values from -6 to 6
Outputs:
- resid_out: float32 [8192, 1536], P(('dp', 'tensor'))
- input_grad: float32 [8192, 1536], P(('dp', 'tensor'))
- small_grad: float32 [2, 21392], replicated
- small_second_new: float32 [2, 21392], replicated
- small_new: float32 [2, 21392], replicated
- in_momentum_new: float32 [2, 1536, 2, 3072], P(None, 'dp', None, 'tensor')
- in_weight_new: float32 [2, 1536, 2, 3072], P(None, 'dp', None, 'tensor')
- out_momentum_new: float32 [2, 1536, 3072], P(None, 'dp', 'tensor')
- out_weight_new: float32 [2, 1536, 3072], P(None, 'dp', 'tensor')
- shared_momentum_new: float32 [2, 1536, 304], replicated
- shared_weight_new: float32 [2, 1536, 304], replicated
The draws below stay inside these ranges and needn't reach their ends.
All inputs are finite; a program needn't handle non-finite values.
Results may differ from the reference program's by a relative error of at most 0.013.
Values may be sent and summed in bfloat16 or wider, within the bound.
A program may use at most 256 MiB of HBM per device.

```python
import jax
import jax.numpy as jnp
from jax import lax

D = 1536
INNER = 3072
HEADS = 48
STATE = 128
KERNEL = 4
SPAN = 256
LAYERS = 2
STEP = 10
SEQ_LEN = 1024
TOKENS = 8192
SSM_COLS = 304
NSMALL = 21392
N_DP = 8
N_TENSOR = 4


def gradient_scale():
    root = jnp.sqrt(jnp.float32(TOKENS))
    channel_count = (KERNEL + 2) * INNER + (KERNEL + 1) * 2 * STATE
    return jnp.concatenate([jnp.full((channel_count,), 0.3, jnp.float32), jnp.full((3 * HEADS,), 3.0, jnp.float32), jnp.full((D,), 0.3, jnp.float32)]) * root


def clipped_normal(key, shape):
    return jnp.clip(jax.random.normal(key, shape, jnp.float32), -4.0, 4.0)


def draw_small_params(key, part):
    key = jax.random.fold_in(key, 11)
    keys = jax.random.split(key, 9)
    channel = jnp.arange(INNER, dtype=jnp.float32) / (INNER - 1)
    conv_x = clipped_normal(keys[0], (LAYERS, KERNEL, INNER)) * (0.25 + 0.5 * channel)
    in_gain = jax.random.uniform(keys[8], (LAYERS, D), jnp.float32, 0.5, 1.5)
    conv_x_b = 0.3 * clipped_normal(keys[1], (LAYERS, INNER))
    norm_gain = jax.random.uniform(keys[2], (LAYERS, INNER), jnp.float32, 0.5, 1.5)
    conv_s = 0.4 * clipped_normal(keys[3], (LAYERS, KERNEL, 2 * STATE))
    conv_s_b = 0.3 * clipped_normal(keys[4], (LAYERS, 2 * STATE))
    a_log = jax.random.uniform(keys[5], (LAYERS, HEADS), jnp.float32, 0.0, 1.3862944)
    low_end = jnp.log(jnp.float32(0.25) / SEQ_LEN)
    high_end = jnp.log(jnp.float32(8.0) / SPAN)
    timestep = jnp.exp(jax.random.uniform(keys[6], (LAYERS, HEADS), jnp.float32, 0.0, 1.0) * (high_end - low_end) + low_end)
    dt_bias = timestep + jnp.log(-jnp.expm1(-timestep))
    skip = jax.random.uniform(keys[7], (LAYERS, HEADS), jnp.float32, 0.5, 1.5)
    return jnp.concatenate([conv_x.reshape(LAYERS, KERNEL * INNER), conv_x_b, norm_gain, conv_s.reshape(LAYERS, KERNEL * 2 * STATE), conv_s_b, a_log, dt_bias, skip, in_gain], 1)


def draw_small_first(key, part):
    key = jax.random.fold_in(key, 13)
    return 0.11 * clipped_normal(key, (LAYERS, NSMALL)) * gradient_scale()[None, :]


def draw_small_second(key, part):
    key = jax.random.fold_in(key, 15)
    factor = jax.random.uniform(key, (LAYERS, NSMALL), jnp.float32, 1.0, 4.0)
    scale = gradient_scale()[None, :]
    return 0.0526 * factor * scale * scale


def draw_resid_grad(key, part):
    key = jax.random.fold_in(key, 17)
    position = jnp.arange(TOKENS, dtype=jnp.float32)[:, None] / (TOKENS - 1)
    return clipped_normal(key, (TOKENS, D)) * (0.5 + position)


def strengthened(drawn, stream_key, source, target, shards_of, factor):
    owner, partner = [(jnp.arange(drawn.shape[dim]) // (drawn.shape[dim] // shards_of)).reshape([-1 if axis == dim else 1 for axis in range(drawn.ndim)]) for dim in (source, target)]
    chosen = jax.random.permutation(stream_key, shards_of)[partner]
    strong = (owner == chosen) | (owner == (partner + shards_of // 2) % shards_of)
    return jnp.where(strong, factor * drawn, drawn)


def block_levels(own_key, shape, cuts, low, largest):
    factor_of, own = 1.0, jax.random.fold_in(own_key, 6)
    for axis_at, parts in cuts:
        draws = jnp.exp(jax.random.uniform(jax.random.fold_in(own, axis_at), (parts,), jnp.float32, low / len(cuts), largest / len(cuts)))
        factor_of = factor_of * jnp.repeat(draws, shape[axis_at] // parts).reshape([-1 if axis == axis_at else 1 for axis in range(len(shape))])
    return factor_of


def gaussian(rng, shape, deviation, reach, cuts=(), kind=jnp.bfloat16):
    drawn = jax.random.normal(rng, shape, jnp.float32) * deviation
    if len(cuts) > 0:
        drawn = block_levels(rng, shape, cuts, -0.22, 0.18) * drawn
    return jnp.clip(drawn, min=-reach, max=reach).astype(kind)


def bell_draw_with(stream_key, dims, scale, bound, shards, heavy, held_as=jnp.bfloat16):
    entries = scale * jax.random.normal(stream_key, dims, jnp.float32)
    if shards:
        entries = entries * block_levels(stream_key, dims, shards, -0.22, 0.18)
    return jnp.clip(strengthened(entries, jax.random.fold_in(stream_key, 3), *heavy), -bound, bound).astype(held_as)


def setup_inputs(seed: int = 0) -> dict:
    arg_keys = jax.random.split(jax.random.key(seed), 12)
    resid_in = bell_draw_with(arg_keys[0], (TOKENS, D), 1.0, 6.0, ((0, 32),), (0, 1, 32, 2.75), jnp.float32)
    in_weight = gaussian(arg_keys[1], (LAYERS, D, 2, INNER), D ** -0.5, 0.15625, ((1, 8), (3, 4)))
    out_weight = gaussian(arg_keys[2], (LAYERS, D, INNER), INNER ** -0.5, 0.109375, ((1, 8), (2, 4)))
    shared_weight = gaussian(arg_keys[3], (LAYERS, D, SSM_COLS), D ** -0.5, 0.15625)
    small_params = draw_small_params(jax.random.fold_in(arg_keys[11], 71), 0)
    in_momentum = gaussian(arg_keys[5], (LAYERS, D, 2, INNER), (0.5 * TOKENS ** 0.5), 256.0, ((1, 8), (3, 4)), jnp.float32)
    out_momentum = gaussian(arg_keys[6], (LAYERS, D, INNER), (0.5 * TOKENS ** 0.5), 256.0, ((1, 8), (2, 4)), jnp.float32)
    shared_momentum = gaussian(arg_keys[7], (LAYERS, D, SSM_COLS), (0.5 * TOKENS ** 0.5), 256.0, (), jnp.float32)
    small_first = draw_small_first(jax.random.fold_in(arg_keys[11], 71), 0)
    small_second = draw_small_second(jax.random.fold_in(arg_keys[11], 71), 0)
    resid_grad = draw_resid_grad(jax.random.fold_in(arg_keys[11], 71), 0)
    return dict(resid_in=resid_in, in_weight=in_weight, out_weight=out_weight, shared_weight=shared_weight, small_params=small_params, in_momentum=in_momentum, out_momentum=out_momentum, shared_momentum=shared_momentum, small_first=small_first, small_second=small_second, resid_grad=resid_grad)


@jax.custom_vjp
def low(v):
    return lax.optimization_barrier(v.astype(jnp.bfloat16)).astype(jnp.float32)

@jax.custom_vjp
def low_back(v):
    return v

def low_keep(v):
    return (low(v), None)

def low_pass(kept, grad):
    return (grad,)

def back_keep(v):
    return (v, None)

def back_low(kept, grad):
    return (low(grad),)
low.defvjp(low_keep, low_pass)
low_back.defvjp(back_keep, back_low)
epsilon = 1e-05
highest = lax.Precision.HIGHEST
coef_first = 3.4445
coef_second = -4.775
coef_third = 2.0315
muon_decay = 0.95
muon_rate = 0.2
beta_first = 0.9
beta_second = 0.95
adam_rate = 0.2

def unpack(vector):
    amounts = (KERNEL * INNER, INNER, INNER, KERNEL * 2 * STATE, 2 * STATE, HEADS, HEADS, HEADS, D)
    pieces = []
    offset = 0
    for amount in amounts:
        pieces.append(vector[offset:offset + amount])
        offset = offset + amount
    return (pieces[0].reshape(KERNEL, INNER), pieces[1], pieces[2], pieces[3].reshape(KERNEL, 2 * STATE), pieces[4], pieces[5], pieces[6], pieces[7], pieces[8])

def causal_conv(values, weights, biases):
    length = values.shape[0]
    padded = jnp.concatenate([jnp.zeros((KERNEL - 1, values.shape[1]), jnp.float32), values], 0)
    result = jnp.zeros_like(values) + biases[None, :]
    for offset in range(KERNEL):
        result = result + weights[offset][None, :] * padded[offset:offset + length]
    return result

def span_step(carry_state, pieces):
    values, inputs, readout, log_decay, timestep = pieces
    length = values.shape[0]
    cumulative = jnp.cumsum(log_decay, axis=0)
    row_index = lax.broadcasted_iota(jnp.int32, (length, length), 0)
    col_index = lax.broadcasted_iota(jnp.int32, (length, length), 1)
    causal = (row_index >= col_index)[:, :, None]
    spread = jnp.where(causal, cumulative[:, None, :] - cumulative[None, :, :], 0.0)
    decay_mask = jnp.where(causal, jnp.exp(spread), 0.0)
    scores = jnp.dot(readout, inputs.T, precision=highest)
    mixing = scores[:, :, None] * decay_mask * timestep[None, :, :]
    inside = jnp.einsum('tsh,shp->thp', mixing, values, precision=highest)
    carried = jnp.einsum('tn,hnp->thp', readout, carry_state, precision=highest) * jnp.exp(cumulative)[:, :, None]
    tail_weight = jnp.exp(cumulative[-1][None, :] - cumulative) * timestep
    fresh_state = jnp.einsum('sn,shp->hnp', inputs, tail_weight[:, :, None] * values, precision=highest)
    new_state = jnp.exp(cumulative[-1])[:, None, None] * carry_state + fresh_state
    return (new_state, inside + carried)

def mixer_core(gate_in, x_in, bc_in, dt_raw, conv_x_w, conv_x_b, conv_s_w, conv_s_b, a_log, dt_bias, skip):
    length = x_in.shape[0]
    head_count = a_log.shape[0]
    head_width = x_in.shape[1] // head_count
    x_conv = jax.nn.silu(causal_conv(x_in, conv_x_w, conv_x_b))
    bc_conv = jax.nn.silu(causal_conv(bc_in, conv_s_w, conv_s_b))
    timestep = jax.nn.softplus(dt_raw + dt_bias[None, :])
    log_decay = -timestep * jnp.exp(a_log)[None, :]
    values = x_conv.reshape(length, head_count, head_width)
    blocks = length // SPAN
    pieces = (values.reshape(blocks, SPAN, head_count, head_width), bc_conv[:, :STATE].reshape(blocks, SPAN, STATE), bc_conv[:, STATE:].reshape(blocks, SPAN, STATE), log_decay.reshape(blocks, SPAN, head_count), timestep.reshape(blocks, SPAN, head_count))
    initial = jnp.zeros((head_count, STATE, head_width), jnp.float32)
    last_state, outputs = lax.scan(jax.checkpoint(span_step), initial, pieces)
    result = outputs.reshape(length, head_count, head_width) + skip[None, :, None] * values
    return result.reshape(length, head_count * head_width) * jax.nn.silu(gate_in)

def orthogonal(matrix):
    current = matrix / (jnp.sqrt(jnp.sum(matrix * matrix)) + 1e-07)
    for iteration in range(5):
        gram = jnp.dot(current, current.T, precision=highest)
        poly = coef_second * gram + coef_third * jnp.dot(gram, gram, precision=highest)
        current = coef_first * current + jnp.dot(poly, current, precision=highest)
    return current

def layer_forward(residual, in_w, out_w, shared_w, small):
    conv_x_w, conv_x_b, norm_gain, conv_s_w, conv_s_b, a_log, dt_bias, skip, in_gain = unpack(small)
    normed = low(residual * lax.rsqrt(lax.optimization_barrier(jnp.mean(residual * residual, -1, keepdims=True)) + epsilon) * in_gain)
    gate_x = low_back(jnp.einsum('td,dki->tki', normed, in_w, precision=highest))
    shared = jnp.dot(normed, shared_w, precision=highest)
    group_cols = INNER // N_TENSOR
    group_heads = HEADS // N_TENSOR
    outputs = []
    for group_index in range(N_TENSOR):
        shared_group = low_back(shared)
        col_lo = group_index * group_cols
        head_lo = group_index * group_heads
        outputs.append(mixer_core(gate_x[:, 0, col_lo:col_lo + group_cols], gate_x[:, 1, col_lo:col_lo + group_cols], shared_group[:, :2 * STATE], shared_group[:, 2 * STATE + head_lo:2 * STATE + head_lo + group_heads], conv_x_w[:, col_lo:col_lo + group_cols], conv_x_b[col_lo:col_lo + group_cols], conv_s_w, conv_s_b, a_log[head_lo:head_lo + group_heads], dt_bias[head_lo:head_lo + group_heads], skip[head_lo:head_lo + group_heads]))
    mixer_out = jnp.concatenate(outputs, 1)
    scaled = low(mixer_out * lax.rsqrt(lax.optimization_barrier(jnp.mean(mixer_out * mixer_out, -1, keepdims=True)) + epsilon) * norm_gain)
    branch = low_back(jnp.dot(scaled, out_w.T, precision=highest))
    return residual + branch

def column_update(momentum):
    group_cols = INNER // N_TENSOR
    blocks = momentum.reshape(D, N_TENSOR, group_cols).transpose(1, 2, 0)
    turned = lax.map(orthogonal, blocks)
    return turned.transpose(2, 0, 1).reshape(D, INNER) * (D / group_cols) ** 0.5

def reference(resid_in, in_weight, out_weight, shared_weight, small_params, in_momentum, out_momentum, shared_momentum, small_first, small_second, resid_grad):
    weights = (in_weight.astype(jnp.float32), out_weight.astype(jnp.float32), shared_weight.astype(jnp.float32), small_params)

    def forward(residual, params):
        in_all, out_all, shared_all, small_all = params
        for layer_number in range(LAYERS):
            residual = layer_forward(residual, in_all[layer_number], out_all[layer_number], shared_all[layer_number], small_all[layer_number])
        return residual
    sequences = resid_in.reshape(N_DP, SEQ_LEN, D)
    cotangents = resid_grad.reshape(N_DP, SEQ_LEN, D)

    def per_sequence(totals, pair):
        output, pullback = jax.vjp(forward, pair[0], weights)
        grad_resid, grad_params = pullback(pair[1])
        totals = jax.tree.map(lambda left, right: left + right, totals, grad_params)
        return (totals, (output, grad_resid))
    zero_totals = jax.tree.map(jnp.zeros_like, weights)
    totals, (outputs, grads) = lax.scan(per_sequence, zero_totals, (sequences, cotangents))
    grad_in, grad_out, grad_shared, small_grad = totals
    in_momentum_new = muon_decay * in_momentum + grad_in
    out_momentum_new = muon_decay * out_momentum + grad_out
    shared_momentum_new = muon_decay * shared_momentum + grad_shared
    in_updates = []
    out_updates = []
    shared_updates = []
    for layer_number in range(LAYERS):
        in_updates.append(jnp.stack([column_update(in_momentum_new[layer_number][:, 0, :]), column_update(in_momentum_new[layer_number][:, 1, :])], 1))
        out_updates.append(column_update(out_momentum_new[layer_number]))
        shared_updates.append(orthogonal(shared_momentum_new[layer_number].T).T * (D / SSM_COLS) ** 0.5)
    in_weight_new = weights[0] - muon_rate * jnp.stack(in_updates)
    out_weight_new = weights[1] - muon_rate * jnp.stack(out_updates)
    shared_weight_new = weights[2] - muon_rate * jnp.stack(shared_updates)
    first_new = beta_first * small_first + (1.0 - beta_first) * small_grad
    small_second_new = beta_second * small_second + (1.0 - beta_second) * small_grad * small_grad
    small_new = small_params - adam_rate * (first_new / (1.0 - beta_first ** STEP)) / (jnp.sqrt(small_second_new / (1.0 - beta_second ** STEP)) + 1e-08)
    return (outputs.reshape(TOKENS, D), grads.reshape(TOKENS, D), small_grad, small_second_new, small_new, in_momentum_new, in_weight_new, out_momentum_new, out_weight_new, shared_momentum_new, shared_weight_new)
```

```python
import functools

import jax
import jax.numpy as jnp
from jax import lax
from jax.experimental import pallas as pl
from jax.experimental.pallas import tpu as pltpu
from jax.sharding import PartitionSpec as P

D = 1536
INNER = 3072
HEADS = 48
STATE = 128
KERNEL = 4
SPAN = 256
LAYERS = 2
STEP = 10
SSM_COLS = 304
WIDTH = INNER // HEADS
LANES = 128
SHARED_COLS = 2 * STATE + LANES
HALO = 8

epsilon = 1e-05
highest = lax.Precision.HIGHEST
coef_first = 3.4445
coef_second = -4.775
coef_third = 2.0315
muon_decay = 0.95
muon_rate = 0.2
beta_first = 0.9
beta_second = 0.95
adam_rate = 0.2

MESH = pl.DeviceIdType.MESH
NN = (((1,), (0,)), ((), ()))
NT = (((1,), (1,)), ((), ()))
TN = (((0,), (0,)), ((), ()))
f32 = jnp.float32
bf16 = jnp.bfloat16


def dot(left, right, dims=NN):
    return lax.dot_general(left, right, dims, preferred_element_type=f32)


def dot_exact(left, right, dims=NN):
    return lax.dot_general(left, right, dims, precision=highest, preferred_element_type=f32)


def sigmoid(v):
    return 0.5 * jnp.tanh(0.5 * v) + 0.5


def softplus(v):
    small = jnp.exp(-jnp.abs(v))
    series = small * (1.0 - small * (0.5 - small * (1.0 / 3.0 - small * 0.25)))
    return jnp.maximum(v, 0.0) + jnp.where(small < 0.01, series, jnp.log(1.0 + small))


def steps_of(raw_in, ph_ref):
    raw = raw_in + ph_ref[1:2, :]
    timestep = softplus(raw)
    decay = -jnp.exp(ph_ref[0:1, :])
    log_decay = timestep * decay
    rows = lax.broadcasted_iota(jnp.int32, (SPAN, SPAN), 0)
    cols = lax.broadcasted_iota(jnp.int32, (SPAN, SPAN), 1)
    lower = jnp.where(rows >= cols, 1.0, 0.0).astype(f32)
    cumulative = dot_exact(lower, log_decay)
    return raw, timestep, decay, log_decay, cumulative, lower


def pair_of(table, pair, low_half):
    return jnp.where(low_half, table[:, 2 * pair : 2 * pair + 1], table[:, 2 * pair + 1 : 2 * pair + 2])


def conv_of(pad, lanes, weights, first):
    total = weights[4:5, lanes] + weights[0:1, lanes] * pad[first : first + SPAN, lanes]
    for tap in range(1, KERNEL):
        total = total + weights[tap : tap + 1, lanes] * pad[first + tap : first + tap + SPAN, lanes]
    return total


def head_sums(values, owner):
    high = values.astype(bf16)
    low = (values - high.astype(f32)).astype(bf16)
    return dot(jnp.concatenate([high, low], 1), owner)


def matmul_into(target, left, right, dims, width, piece):
    for at in range(0, width, piece):
        cols = slice(at, min(at + piece, width))
        mine = right[:, cols] if dims == NN else right[cols, :]
        target[:, cols] = dot(left, mine, dims).astype(target.dtype)


def forward_kernel(
    g_ref, w_ref, wo_ref, px_ref, ps_ref, ph_ref, proj_ref, yt_ref, p_ref, sq_ref, st_ref, state, xpad, spad, gained
):
    step = pl.program_id(0)
    columns = yt_ref.shape[1]
    pairs = columns // LANES

    @pl.when(step == 0)
    def _():
        state[...] = jnp.zeros_like(state)
        xpad[0:HALO, :] = jnp.zeros((HALO, columns), f32)
        spad[0:HALO, :] = jnp.zeros((HALO, 2 * STATE), f32)

    @pl.when(step > 0)
    def _():
        xpad[0:HALO, :] = xpad[SPAN : SPAN + HALO, :]
        spad[0:HALO, :] = spad[SPAN : SPAN + HALO, :]

    matmul_into(proj_ref, g_ref[...], w_ref, NN, 2 * columns + SHARED_COLS, 2 * LANES)
    xpad[HALO:, :] = proj_ref[:, columns : 2 * columns]
    spad[HALO:, :] = proj_ref[:, 2 * columns : 2 * columns + 2 * STATE]
    first = HALO - KERNEL + 1
    pre_s = conv_of(spad, slice(None), ps_ref, first)
    bc = pre_s * sigmoid(pre_s)
    b_low, c_low = bc[:, :STATE].astype(bf16), bc[:, STATE:].astype(bf16)
    raw, timestep, decay, log_decay, cumulative, lower = steps_of(proj_ref[:, 2 * columns + 2 * STATE :], ph_ref)
    turned = cumulative.T
    grown = jnp.exp(cumulative)
    tail = jnp.exp(cumulative[SPAN - 1 : SPAN, :] - cumulative)
    scores = dot(c_low, b_low, NT) * lower
    low_half = lax.broadcasted_iota(jnp.int32, (SPAN, LANES), 1) < WIDTH
    squares = jnp.zeros((SPAN, LANES), f32)
    half = SPAN // 2
    for pair in range(pairs):
        lanes = slice(pair * LANES, (pair + 1) * LANES)
        pre = conv_of(xpad, lanes, px_ref, first)
        xc = pre * sigmoid(pre)
        u = xc * pair_of(timestep, pair, low_half)
        u_low = u.astype(bf16)
        mine = [jnp.where(low_half == (side == 0), u_low, jnp.zeros_like(u_low)) for side in range(2)]
        inside = []
        for rows, count in ((slice(0, half), half), (slice(half, SPAN), SPAN)):
            both = jnp.zeros((half, LANES), f32)
            for side in range(2):
                head = 2 * pair + side
                spread = cumulative[rows, head : head + 1] - turned[head : head + 1, :count]
                mixing = (scores[rows, :count] * jnp.exp(jnp.minimum(spread, 0.0))).astype(bf16)
                both = both + dot(mixing, mine[side][:count])
            inside.append(both)
        held = state[:, lanes]
        held_low = held.astype(bf16)
        st_ref[0, :, lanes] = held_low
        grown_pair = pair_of(grown, pair, low_half)
        carried = dot(c_low, held_low) * grown_pair
        tail_u = (pair_of(tail, pair, low_half) * u).astype(bf16)
        state[:, lanes] = grown_pair[SPAN - 1 : SPAN, :] * held + dot(b_low, tail_u, TN)
        total = jnp.concatenate(inside, 0) + carried + px_ref[6:7, lanes] * xc
        yt_ref[:, lanes] = total
        gate = proj_ref[:, lanes]
        mixed = total * gate * sigmoid(gate)
        gained[:, lanes] = (mixed * px_ref[5:6, lanes]).astype(bf16)
        squares = squares + mixed * mixed
    sq_ref[0] = dot_exact(jnp.ones((8, LANES), f32), squares, NT)
    matmul_into(p_ref, gained[...], wo_ref, NT, D, 2 * LANES)


def backward_kernel(
    dr_ref,
    w_ref,
    wo_ref,
    gate_ref,
    x_ref,
    xh_ref,
    sh_ref,
    shh_ref,
    yt_ref,
    st_ref,
    rd_ref,
    px_ref,
    ps_ref,
    ph_ref,
    dall_ref,
    scaled_ref,
    p_ref,
    gx_ref,
    gs_ref,
    gh_ref,
    dstate,
    xpad,
    spad,
    dxpad,
    dspad,
    dsc,
):
    step = pl.program_id(0)
    steps = pl.num_programs(0)
    columns = x_ref.shape[1]
    pairs = columns // LANES

    @pl.when(step == 0)
    def _():
        dstate[...] = jnp.zeros_like(dstate)
        dxpad[SPAN:, :] = jnp.zeros((HALO, columns), f32)
        dspad[SPAN:, :] = jnp.zeros((HALO, 2 * STATE), f32)
        gx_ref[...] = jnp.zeros_like(gx_ref)
        gs_ref[...] = jnp.zeros_like(gs_ref)
        gh_ref[...] = jnp.zeros_like(gh_ref)

    @pl.when(step > 0)
    def _():
        dxpad[SPAN:, :] = dxpad[0:HALO, :]
        dspad[SPAN:, :] = dspad[0:HALO, :]

    matmul_into(dsc, dr_ref[...], wo_ref, NN, columns, 2 * LANES)
    before = jnp.where(step < steps - 1, 1.0, 0.0).astype(f32)
    xpad[0:HALO, :] = xh_ref[...] * before
    spad[0:HALO, :] = shh_ref[:, : 2 * STATE] * before
    xpad[HALO:, :] = x_ref[...]
    spad[HALO:, :] = sh_ref[:, : 2 * STATE]
    first = HALO - KERNEL + 1
    pre_s = conv_of(spad, slice(None), ps_ref, first)
    sig_s = sigmoid(pre_s)
    bc = pre_s * sig_s
    b_low, c_low = bc[:, :STATE].astype(bf16), bc[:, STATE:].astype(bf16)
    raw, timestep, decay, log_decay, cumulative, lower = steps_of(sh_ref[:, 2 * STATE :], ph_ref)
    turned = cumulative.T
    grown = jnp.exp(cumulative)
    tail = jnp.exp(cumulative[SPAN - 1 : SPAN, :] - cumulative)
    upper = lower.T
    scores = dot(b_low, c_low, NT) * upper
    low_half = lax.broadcasted_iota(jnp.int32, (SPAN, LANES), 1) < WIDTH
    inverse = rd_ref[:, 0:1]
    dots = rd_ref[:, 1:2] * (1.0 / INNER)
    head_row = lax.rem(lax.broadcasted_iota(jnp.int32, (2 * LANES, LANES), 0), LANES) // WIDTH
    head_col = lax.broadcasted_iota(jnp.int32, (2 * LANES, LANES), 1)

    half = SPAN // 2
    d_scores = [jnp.zeros((half, SPAN), f32), jnp.zeros((half, half), f32)]
    d_b = jnp.zeros((SPAN, STATE), f32)
    d_c = jnp.zeros((SPAN, STATE), f32)
    d_cum = jnp.zeros((SPAN, LANES), f32)
    d_step = jnp.zeros((SPAN, LANES), f32)
    d_last = jnp.zeros((8, LANES), f32)
    for pair in range(pairs):
        lanes = slice(pair * LANES, (pair + 1) * LANES)
        owner = jnp.where(head_row + 2 * pair == head_col, 1.0, 0.0).astype(bf16)
        pre = conv_of(xpad, lanes, px_ref, first)
        sig = sigmoid(pre)
        xc = pre * sig
        step_pair = pair_of(timestep, pair, low_half)
        u = xc * step_pair
        u_low = u.astype(bf16)
        gate = gate_ref[:, lanes]
        sig_gate = sigmoid(gate)
        silu = gate * sig_gate
        total = yt_ref[:, lanes]
        gain = px_ref[5:6, lanes]
        sn = total * silu * inverse
        scaled_ref[:, lanes] = (sn * gain).astype(bf16)
        d_scaled = dsc[:, lanes]
        gx_ref[5:6, lanes] += jnp.sum(d_scaled * sn, 0, keepdims=True)
        d_mixed = inverse * (d_scaled * gain - sn * dots)
        dall_ref[:, lanes] = (
            d_mixed * total * (sig_gate * (1.0 + gate * (1.0 - sig_gate)))
        ).astype(bf16)
        dy = d_mixed * silu
        skip = px_ref[6:7, lanes]
        gx_ref[6:7, lanes] += jnp.sum(dy * xc, 0, keepdims=True)
        dy_low = dy.astype(bf16)
        mine = [jnp.where(low_half == (side == 0), dy_low, jnp.zeros_like(dy_low)) for side in range(2)]
        du = []
        for block, start in ((0, 0), (1, half)):
            rows = slice(start, start + half)
            both = jnp.zeros((half, LANES), f32)
            for side in range(2):
                head = 2 * pair + side
                spread = turned[head : head + 1, start:] - cumulative[rows, head : head + 1]
                mask = jnp.exp(jnp.minimum(spread, 0.0))
                mixing = (scores[rows, start:] * mask).astype(bf16)
                both = both + dot(mixing, mine[side][start:])
                d_scores[block] = d_scores[block] + dot(u_low[rows], mine[side][start:], NT) * mask
            du.append(both)
        held_low = st_ref[0, :, lanes]
        grown_pair = pair_of(grown, pair, low_half)
        last_pair = grown_pair[SPAN - 1 : SPAN, :]
        d_after = dstate[:, lanes]
        d_after_low = d_after.astype(bf16)
        grown_dy = (grown_pair * dy).astype(bf16)
        d_c = d_c + dot(grown_dy, held_low, NT)
        tail_pair = pair_of(tail, pair, low_half)
        du_tail = tail_pair * dot(b_low, d_after_low)
        d_b = d_b + dot((tail_pair * u).astype(bf16), d_after_low, NT)
        dstate[:, lanes] = last_pair * d_after + dot(c_low, grown_dy, TN)
        du = jnp.concatenate(du, 0) + du_tail
        u_round = u_low.astype(f32)
        y = total - skip * xc
        d_cum = d_cum + head_sums(dy_low.astype(f32) * y - u_round * du, owner)
        d_step = d_step + head_sums(xc * du, owner)
        ends = jnp.sum(u_round * du_tail, 0, keepdims=True) + last_pair * jnp.sum(
            d_after * held_low.astype(f32), 0, keepdims=True
        )
        d_last = d_last + head_sums(jnp.broadcast_to(ends, (8, LANES)), owner)
        d_pre = (skip * dy + step_pair * du) * (sig * (1.0 + pre * (1.0 - sig)))
        dxpad[0:SPAN, lanes] = d_pre
        d_x = px_ref[KERNEL - 1 : KERNEL, lanes] * d_pre
        gx_ref[4:5, lanes] += jnp.sum(d_pre, 0, keepdims=True)
        for tap in range(KERNEL):
            gx_ref[tap : tap + 1, lanes] += jnp.sum(
                d_pre * xpad[first + tap : first + tap + SPAN, lanes], 0, keepdims=True
            )
            if tap < KERNEL - 1:
                ahead = KERNEL - 1 - tap
                d_x = d_x + px_ref[tap : tap + 1, lanes] * dxpad[ahead : ahead + SPAN, lanes]
        dall_ref[:, columns + pair * LANES : columns + (pair + 1) * LANES] = d_x.astype(bf16)
    d_log = dot_exact(upper, d_cum) + d_last[0:1, :]
    d_raw = (d_step + d_log * decay) * sigmoid(raw)
    gh_ref[0:1, :] += jnp.sum(d_log * log_decay, 0, keepdims=True)
    gh_ref[1:2, :] += jnp.sum(d_raw, 0, keepdims=True)
    d_scores = jnp.concatenate(
        [d_scores[0], jnp.concatenate([jnp.zeros((half, half), f32), d_scores[1]], 1)], 0
    )
    d_scores_low = (d_scores * upper).astype(bf16)
    d_b = d_b + dot(d_scores_low, c_low)
    d_c = d_c + dot(d_scores_low, b_low, TN)
    slope_s = sig_s * (1.0 + pre_s * (1.0 - sig_s))
    d_pre_s = jnp.concatenate([d_b, d_c], 1) * slope_s
    dspad[0:SPAN, :] = d_pre_s
    d_s = ps_ref[KERNEL - 1 : KERNEL, :] * d_pre_s
    gs_ref[4:5, :] += jnp.sum(d_pre_s, 0, keepdims=True)
    for tap in range(KERNEL):
        gs_ref[tap : tap + 1, :] += jnp.sum(
            d_pre_s * spad[first + tap : first + tap + SPAN, :], 0, keepdims=True
        )
        if tap < KERNEL - 1:
            ahead = KERNEL - 1 - tap
            d_s = d_s + ps_ref[tap : tap + 1, :] * dspad[ahead : ahead + SPAN, :]
    dall_ref[:, 2 * columns : 2 * columns + 2 * STATE] = d_s.astype(bf16)
    dall_ref[:, 2 * columns + 2 * STATE :] = d_raw.astype(bf16)
    matmul_into(p_ref, dall_ref[...], w_ref, NT, D, 2 * LANES)


def resident(shape):
    return pl.BlockSpec(shape, lambda i: (0, 0), pipeline_mode=pl.Buffered(1))


def mixer_forward(gathered, w_in, w_out, px, ps, ph):
    length, columns = gathered.shape[0], px.shape[1]
    spans = length // SPAN
    width = 2 * columns + SHARED_COLS
    here = lambda i: (i, 0)
    return pl.pallas_call(
        forward_kernel,
        grid=(spans,),
        in_specs=[
            pl.BlockSpec((SPAN, D), here),
            resident((D, width)),
            resident((D, columns)),
            resident((8, columns)),
            resident((8, 2 * STATE)),
            resident((8, LANES)),
        ],
        out_specs=[
            pl.BlockSpec((SPAN, width), here),
            pl.BlockSpec((SPAN, columns), here),
            pl.BlockSpec((SPAN, D), here),
            pl.BlockSpec((1, 8, SPAN), lambda i: (i, 0, 0)),
            pl.BlockSpec((1, STATE, columns), lambda i: (i, 0, 0)),
        ],
        out_shape=[
            jax.ShapeDtypeStruct((length, width), f32),
            jax.ShapeDtypeStruct((length, columns), f32),
            jax.ShapeDtypeStruct((length, D), bf16),
            jax.ShapeDtypeStruct((spans, 8, SPAN), f32),
            jax.ShapeDtypeStruct((spans, STATE, columns), bf16),
        ],
        scratch_shapes=[
            pltpu.VMEM((STATE, columns), f32),
            pltpu.VMEM((SPAN + HALO, columns), f32),
            pltpu.VMEM((SPAN + HALO, 2 * STATE), f32),
            pltpu.VMEM((SPAN, columns), bf16),
        ],
        compiler_params=pltpu.CompilerParams(vmem_limit_bytes=56 * 2**20),
        cost_estimate=pl.CostEstimate(flops=10 * 10**9, bytes_accessed=32 * 2**20, transcendentals=0),
    )(gathered, w_in, w_out, px, ps, ph)


def mixer_backward(d_rows, w_in, w_out, projected, total, states, rd, px, ps, ph):
    length, columns = total.shape
    spans = length // SPAN
    width = 2 * columns + SHARED_COLS
    here = lambda i: (spans - 1 - i, 0)
    blocks = SPAN // HALO
    halo = lambda i: jnp.maximum((spans - 1 - i) * blocks - 1, 0)
    tail_block = 2 * columns // SHARED_COLS
    return pl.pallas_call(
        backward_kernel,
        grid=(spans,),
        in_specs=[
            pl.BlockSpec((SPAN, D), here),
            resident((D, width)),
            resident((D, columns)),
            pl.BlockSpec((SPAN, columns), here),
            pl.BlockSpec((SPAN, columns), lambda i: (spans - 1 - i, 1)),
            pl.BlockSpec((HALO, columns), lambda i: (halo(i), 1)),
            pl.BlockSpec((SPAN, SHARED_COLS), lambda i: (spans - 1 - i, tail_block)),
            pl.BlockSpec((HALO, SHARED_COLS), lambda i: (halo(i), tail_block)),
            pl.BlockSpec((SPAN, columns), here),
            pl.BlockSpec((1, STATE, columns), lambda i: (spans - 1 - i, 0, 0)),
            pl.BlockSpec((SPAN, 2), here),
            resident((8, columns)),
            resident((8, 2 * STATE)),
            resident((8, LANES)),
        ],
        out_specs=[
            pl.BlockSpec((SPAN, width), here),
            pl.BlockSpec((SPAN, columns), here),
            pl.BlockSpec((SPAN, D), here),
            pl.BlockSpec((8, columns), lambda i: (0, 0)),
            pl.BlockSpec((8, 2 * STATE), lambda i: (0, 0)),
            pl.BlockSpec((8, LANES), lambda i: (0, 0)),
        ],
        out_shape=[
            jax.ShapeDtypeStruct((length, width), bf16),
            jax.ShapeDtypeStruct((length, columns), bf16),
            jax.ShapeDtypeStruct((length, D), bf16),
            jax.ShapeDtypeStruct((8, columns), f32),
            jax.ShapeDtypeStruct((8, 2 * STATE), f32),
            jax.ShapeDtypeStruct((8, LANES), f32),
        ],
        scratch_shapes=[
            pltpu.VMEM((STATE, columns), f32),
            pltpu.VMEM((SPAN + HALO, columns), f32),
            pltpu.VMEM((SPAN + HALO, 2 * STATE), f32),
            pltpu.VMEM((SPAN + HALO, columns), f32),
            pltpu.VMEM((SPAN + HALO, 2 * STATE), f32),
            pltpu.VMEM((SPAN, columns), f32),
        ],
        compiler_params=pltpu.CompilerParams(vmem_limit_bytes=56 * 2**20),
        cost_estimate=pl.CostEstimate(flops=16 * 10**9, bytes_accessed=48 * 2**20, transcendentals=0),
    )(
        d_rows,
        w_in,
        w_out,
        projected,
        projected,
        projected,
        projected,
        projected,
        total,
        states,
        rd,
        px,
        ps,
        ph,
    )


def kernels_fit():
    return lax.axis_size("tensor") == 4 and lax.axis_size("dp") == 8


def neighbours():
    index = lax.axis_index("dp")
    core = lax.rem(index, 2)
    across = lax.rem(lax.div(index, 2), 2)
    along = lax.div(index, 4)
    return index, core, index + 1 - 2 * core, index + 2 - 4 * across, index + 4 - 8 * along


def greet(others):
    barrier = pltpu.get_barrier_semaphore()
    for other in others:
        pl.semaphore_signal(barrier, inc=1, device_id=other, device_id_type=MESH)
    pl.semaphore_wait(barrier, len(others))


def remote(source, target, send_sem, recv_sem, slot, where):
    return pltpu.make_async_remote_copy(
        src_ref=source,
        dst_ref=target,
        send_sem=send_sem.at[slot],
        recv_sem=recv_sem.at[slot],
        device_id=where,
        device_id_type=MESH,
    )


class Line:
    def __init__(self, side):
        me = lax.axis_index("tensor")
        self.side = side
        self.me = me
        self.pos = me if side == 0 else 3 - me
        self.next = {"tensor": lax.rem(me + (1 if side == 0 else 3), 4)}

    def chunk(self, ahead):
        return self.me + ahead if self.side == 0 else self.me - ahead


def rows_at(ref, chunk, count):
    return ref.at[pl.ds(pl.multiple_of(chunk * count, count), count), :]


class LineCopy:
    def __init__(self, lines, source, place, local_sem, send_sem, recv_sem):
        self.lines, self.source, self.place = lines, source, place
        self.send_sem, self.recv_sem = send_sem, recv_sem
        self.own = pltpu.make_async_copy(source, place(lines[0].me), local_sem)

    def outgoing(self, line, time):
        place = self.place(line.chunk(-time))
        source = self.source if time == 0 else place
        return remote(source, place, self.send_sem, self.recv_sem, 3 * line.side + time, line.next)

    def start(self):
        for line in self.lines:

            @pl.when(line.pos < 3)
            def _(line=line):
                self.outgoing(line, 0).start()

        self.own.start()

    def step(self, time):
        for line in self.lines:

            @pl.when(line.pos >= time)
            def _(line=line):
                place = self.place(line.chunk(-time))
                slot = 3 * line.side + time - 1
                remote(place, place, self.send_sem, self.recv_sem, slot, line.next).wait_recv()

            if time < 3:

                @pl.when(jnp.logical_and(line.pos >= time, line.pos < 3))
                def _(line=line):
                    self.outgoing(line, time).start()

    def finish(self):
        for time in range(3):
            for line in self.lines:

                @pl.when(jnp.logical_and(line.pos >= time, line.pos < 3))
                def _(line=line):
                    self.outgoing(line, time).wait_send()

        self.own.wait()


class SquareCopy:
    def __init__(self, source, result, local_sem, send_sem, recv_sem):
        self.source, self.result = source, result
        self.send_sem, self.recv_sem = send_sem, recv_sem
        self.rows = source.shape[0]
        self.split = near_rows(self.rows)
        self.index, core, self.sibling, self.by_x, self.by_y = neighbours()
        self.own = pltpu.make_async_copy(source, self.place(self.index, None), local_sem)

    def place(self, owner, side):
        start, count = {None: (0, self.rows), 0: (0, self.split), 1: (self.split, self.rows - self.split)}[side]
        return self.result.at[pl.ds(pl.multiple_of(owner * self.rows + start, 16), count), :]

    def copy(self, slot):
        near, far = self.source.at[pl.ds(0, self.split), :], self.source.at[pl.ds(self.split, self.rows - self.split), :]
        by_x, by_y = self.by_x, self.by_y
        source, owner, side, where = {
            0: (near, self.index, 0, by_x),
            1: (far, self.index, 1, by_y),
            2: (far, self.index, 1, by_x),
            3: (near, self.index, 0, by_y),
            4: (None, by_x, 0, by_y),
            5: (None, by_y, 1, by_x),
            6: (self.source, self.index, None, self.sibling),
            7: (None, by_x, None, self.sibling),
            8: (None, by_y, None, self.sibling),
            9: (None, by_x + by_y - self.index, None, self.sibling),
        }[slot]
        target = self.place(owner, side)
        return remote(target if source is None else source, target, self.send_sem, self.recv_sem, slot, {"dp": where})

    def start(self):
        for slot in (0, 1, 2, 3, 6):
            self.copy(slot).start()
        self.own.start()

    def relay(self):
        self.copy(0).wait_recv()
        self.copy(4).start()
        self.copy(1).wait_recv()
        self.copy(5).start()

    def forward(self):
        self.copy(2).wait_recv()
        self.copy(7).start()
        self.copy(3).wait_recv()
        self.copy(8).start()

    def last(self):
        self.copy(4).wait_recv()
        self.copy(5).wait_recv()
        self.copy(9).start()

    def finish(self):
        for slot in range(6, 10):
            self.copy(slot).wait_recv()
        for slot in range(10):
            self.copy(slot).wait_send()
        self.own.wait()


def first_kernel(x_ref, w_ref, v_ref, ox_ref, ow_ref, ov_ref, *sems):
    lines = (Line(0), Line(1))
    rows = x_ref.shape[0]
    me = lax.axis_index("tensor")
    index, core, sibling, by_x, by_y = neighbours()
    greet([{"tensor": lax.rem(me + 1, 4)}, {"tensor": lax.rem(me + 3, 4)}, {"dp": sibling}, {"dp": by_x}, {"dp": by_y}])
    tokens = LineCopy(lines, x_ref, lambda chunk: rows_at(ox_ref, chunk, rows), *sems[:3])
    weights = [SquareCopy(w_ref, ow_ref, *sems[3:6]), SquareCopy(v_ref, ov_ref, *sems[6:])]
    tokens.start()
    for each in weights:
        each.start()
    for each in weights:
        each.relay()
    tokens.step(1)
    for each in weights:
        each.forward()
    tokens.step(2)
    for each in weights:
        each.last()
    tokens.step(3)
    for each in weights:
        each.finish()
    tokens.finish()


def gather_first(rows, w_rows, v_rows):
    if not kernels_fit():
        return (
            lax.all_gather(rows, "tensor", axis=0, tiled=True),
            lax.all_gather(w_rows, "dp", axis=0, tiled=True),
            lax.all_gather(v_rows, "dp", axis=0, tiled=True),
        )
    anywhere = pl.BlockSpec(memory_space=pl.ANY)
    larger = lambda v, times: jax.ShapeDtypeStruct((times * v.shape[0], v.shape[1]), v.dtype)
    sems = lambda count: [
        pltpu.SemaphoreType.DMA,
        pltpu.SemaphoreType.DMA((count,)),
        pltpu.SemaphoreType.DMA((count,)),
    ]
    return pl.pallas_call(
        first_kernel,
        out_shape=(larger(rows, 4), larger(w_rows, 8), larger(v_rows, 8)),
        in_specs=[anywhere] * 3,
        out_specs=(anywhere,) * 3,
        scratch_shapes=[*sems(6), *sems(10), *sems(10)],
        compiler_params=pltpu.CompilerParams(collective_id=6, has_side_effects=True),
        cost_estimate=pl.CostEstimate(flops=0, bytes_accessed=150 * 2**20, transcendentals=0),
    )(rows, w_rows, v_rows)


def gather_tokens(rows, small):
    if not kernels_fit():
        return lax.all_gather(rows, "tensor", axis=0, tiled=True), lax.all_gather(small, "tensor", axis=0)
    count, columns = rows.shape
    vmem = pl.BlockSpec(memory_space=pltpu.VMEM)
    anywhere = pl.BlockSpec(memory_space=pl.ANY)
    return pl.pallas_call(
        gather_kernel,
        out_shape=(
            jax.ShapeDtypeStruct((4 * count, columns), rows.dtype),
            jax.ShapeDtypeStruct((4, *small.shape), small.dtype),
        ),
        in_specs=[anywhere, vmem],
        out_specs=(anywhere, vmem),
        scratch_shapes=[
            pltpu.SemaphoreType.DMA,
            pltpu.SemaphoreType.DMA,
            pltpu.SemaphoreType.DMA((6,)),
            pltpu.SemaphoreType.DMA((6,)),
            pltpu.SemaphoreType.DMA((6,)),
            pltpu.SemaphoreType.DMA((6,)),
        ],
        compiler_params=pltpu.CompilerParams(collective_id=0, has_side_effects=True),
        cost_estimate=pl.CostEstimate(flops=0, bytes_accessed=150 * 2**20, transcendentals=0),
    )(rows, small)


class LineSum:
    def __init__(self, lines, p_ref, o_ref, came, send_sem, recv_sem, first_row=0):
        self.lines, self.p_ref, self.o_ref, self.came = lines, p_ref, o_ref, came
        self.send_sem, self.recv_sem = send_sem, recv_sem
        self.first_row, self.count = first_row, came.shape[1]
        self.rows = p_ref.shape[0] // 4

    def part(self, chunk):
        start = pl.multiple_of(chunk * self.rows + self.first_row, self.count)
        return self.p_ref.at[pl.ds(start, self.count), :]

    def copy(self, line, time, first):
        slot = 3 * line.side + time
        target = self.came.at[slot]
        source = self.part(line.chunk(3 - time)) if first else self.came.at[slot - 1]
        return remote(source, target, self.send_sem, self.recv_sem, slot, line.next)

    def start(self, times=(0, 1, 2)):
        for line in self.lines:

            @pl.when(line.pos == 0)
            def _(line=line):
                for time in times:
                    self.copy(line, time, True).start()

    def step(self, time):
        for line in self.lines:

            @pl.when(jnp.logical_and(line.pos > 0, line.pos <= time))
            def _(line=line):
                slot = 3 * line.side + time - 1
                place = self.came.at[slot]
                remote(place, place, self.send_sem, self.recv_sem, slot, line.next).wait_recv()

            if time < 3:

                @pl.when(jnp.logical_and(line.pos > 0, line.pos <= time))
                def _(line=line):
                    slot = 3 * line.side + time - 1
                    mine = self.part(line.chunk(3 - time))[...]
                    self.came[slot] = (self.came[slot].astype(f32) + mine.astype(f32)).astype(bf16)
                    self.copy(line, time, False).start()

    def own(self):
        place = pl.ds(self.first_row, self.count)
        self.o_ref[place, :] = self.part(self.lines[0].me)[...].astype(f32)
        for line in self.lines:

            @pl.when(line.pos > 0)
            def _(line=line):
                self.o_ref[place, :] += self.came[3 * line.side + 2].astype(f32)

    def finish(self):
        for line in self.lines:

            @pl.when(line.pos == 0)
            def _(line=line):
                for time in range(3):
                    self.copy(line, time, True).wait_send()

            for time in range(1, 3):

                @pl.when(jnp.logical_and(line.pos > 0, line.pos <= time))
                def _(line=line):
                    self.copy(line, time, False).wait_send()


class Pass:
    def __init__(self, lines, p_ref, o_ref, came, x_ref, ox_ref, sems, work):
        half = came.shape[2]
        self.work = work
        self.sums, self.copies = [], []
        for part in range(2):
            sum_send, sum_recv, copy_local, copy_send, copy_recv = sems[5 * part : 5 * part + 5]
            first_row = part * half
            self.sums.append(LineSum(lines, p_ref, o_ref, came.at[part], sum_send, sum_recv, first_row))
            place = lambda chunk, first_row=first_row: ox_ref.at[
                pl.ds(pl.multiple_of(chunk * 2 * half + first_row, half), half), :
            ]
            source = x_ref.at[pl.ds(first_row, half), :]
            self.copies.append(LineCopy(lines, source, place, copy_local, copy_send, copy_recv))

    def start(self):
        self.sums[0].start()
        self.sums[1].start((0,))

    def turn(self, part):
        self.sums[part].step(3)
        self.sums[part].own()
        self.work(part)
        self.copies[part].start()

    def between(self):
        self.sums[1].start((1, 2))
        self.sums[1].step(1)

    def across(self):
        self.copies[0].step(1)
        self.sums[1].step(2)
        self.copies[0].step(2)

    def last(self):
        self.copies[0].step(3)
        for time in range(1, 4):
            self.copies[1].step(time)

    def finish(self):
        for each in (*self.sums, *self.copies):
            each.finish()


def pass_sems():
    line = pltpu.SemaphoreType.DMA((6,))
    return [line, line, pltpu.SemaphoreType.DMA, line, line] * 2


def column_of(row, count):
    return jnp.broadcast_to(row, (LANES, count)).T[:, 0:1]


def forward_pass_kernel(
    p_any,
    q_ref,
    r_ref,
    gain_ref,
    or_ref,
    ob_ref,
    oi_ref,
    ox_ref,
    p_ref,
    normed,
    came,
    came_q,
    fetch_sem,
    small_send,
    small_recv,
    *sems,
):
    lines = (Line(0), Line(1))
    me = lax.axis_index("tensor")
    others = [{"tensor": lax.rem(me + ahead, 4)} for ahead in (1, 2, 3)]
    fetch = pltpu.make_async_copy(p_any, p_ref, fetch_sem)
    fetch.start()
    greet(others)
    small = [
        remote(q_ref.at[lax.rem(me + slot + 1, 4)], came_q.at[slot], small_send, small_recv, slot, other)
        for slot, other in enumerate(others)
    ]
    for copy in small:
        copy.start()
    count = r_ref.shape[0]
    half = count // 2

    def work(part):
        rows = slice(part * half, (part + 1) * half)
        branch = ob_ref[rows, :] * column_of(oi_ref[0:1, rows], half)
        ob_ref[rows, :] = branch
        fresh = r_ref[rows, :] + branch
        or_ref[rows, :] = fresh
        inverse = lax.rsqrt(jnp.mean(fresh * fresh, -1, keepdims=True) + epsilon)
        normed[rows, :] = (fresh * inverse * gain_ref[0:1, :]).astype(bf16)

    line_pass = Pass(lines, p_ref, ob_ref, came, normed, ox_ref, sems, work)
    fetch.wait()
    line_pass.start()
    for copy in small:
        copy.wait_recv()
    oi_ref[...] = lax.rsqrt((q_ref[me] + came_q[0] + came_q[1] + came_q[2]) * (1.0 / INNER) + epsilon)
    line_pass.sums[0].step(1)
    line_pass.sums[0].step(2)
    line_pass.turn(0)
    line_pass.between()
    line_pass.across()
    line_pass.turn(1)
    line_pass.last()
    line_pass.finish()
    for copy in small:
        copy.wait_send()


def forward_pass(partial, squares, residual, in_gain):
    count, columns = residual.shape
    if not kernels_fit():
        summed, side = scatter_tokens(partial, squares)
        scale = lax.rsqrt(side / INNER + epsilon)
        branch = summed * scale[0][:, None]
        fresh = residual + branch
        inverse = lax.rsqrt(jnp.mean(fresh * fresh, -1, keepdims=True) + epsilon)
        normed = (fresh * inverse * in_gain).astype(bf16)
        return fresh, branch, scale, lax.all_gather(normed, "tensor", axis=0, tiled=True)
    vmem = pl.BlockSpec(memory_space=pltpu.VMEM)
    anywhere = pl.BlockSpec(memory_space=pl.ANY)
    return pl.pallas_call(
        forward_pass_kernel,
        out_shape=(
            jax.ShapeDtypeStruct((count, columns), f32),
            jax.ShapeDtypeStruct((count, columns), f32),
            jax.ShapeDtypeStruct((8, count), f32),
            jax.ShapeDtypeStruct((4 * count, columns), bf16),
        ),
        in_specs=[anywhere, vmem, vmem, vmem],
        out_specs=(vmem, vmem, vmem, anywhere),
        scratch_shapes=[
            pltpu.VMEM(partial.shape, bf16),
            pltpu.VMEM((count, columns), bf16),
            pltpu.VMEM((2, 6, count // 2, columns), bf16),
            pltpu.VMEM((3, 8, count), f32),
            pltpu.SemaphoreType.DMA,
            pltpu.SemaphoreType.DMA((3,)),
            pltpu.SemaphoreType.DMA((3,)),
            *pass_sems(),
        ],
        compiler_params=pltpu.CompilerParams(
            collective_id=2, has_side_effects=True, vmem_limit_bytes=40 * 2**20
        ),
        cost_estimate=pl.CostEstimate(flops=0, bytes_accessed=250 * 2**20, transcendentals=0),
    )(partial, squares, residual, jnp.broadcast_to(in_gain[None], (8, columns)))


def scatter_kernel(
    p_ref,
    q_ref,
    x_ref,
    o_ref,
    oq_ref,
    ox_ref,
    rd_ref,
    came,
    came_q,
    send_sem,
    recv_sem,
    small_send,
    small_recv,
    local_sem,
    copy_send,
    copy_recv,
    scalars,
    rd_local,
    rd_send,
    rd_recv,
):
    lines = (Line(0), Line(1))
    me = lax.axis_index("tensor")
    others = [{"tensor": lax.rem(me + ahead, 4)} for ahead in (1, 2, 3)]
    greet(others)
    small = [
        remote(q_ref.at[lax.rem(me + slot + 1, 4)], came_q.at[slot], small_send, small_recv, slot, other)
        for slot, other in enumerate(others)
    ]
    for copy in small:
        copy.start()
    rows = x_ref.shape[0]
    place = lambda chunk: rows_at(ox_ref, chunk, rows)
    total = LineSum(lines, p_ref, o_ref, came, send_sem, recv_sem)
    streams = [LineCopy(lines, x_ref, place, local_sem, copy_send, copy_recv), total]
    for stream in streams:
        stream.start()
    for copy in small:
        copy.wait_recv()
    oq_ref[...] = q_ref[me] + came_q[0] + came_q[1] + came_q[2]
    for time in range(1, 4):
        for stream in streams:
            stream.step(time)
    total.own()
    inverse = lax.rsqrt(oq_ref[...] * (1.0 / INNER) + epsilon)
    products = x_ref[...].astype(f32) * o_ref[...]
    dots = dot_exact(jnp.ones((8, products.shape[1]), f32), products, NT) * inverse
    first_row = lax.broadcasted_iota(jnp.int32, scalars.shape, 0) == 0
    scalars[...] = jnp.where(first_row, inverse, dots)
    copies = [remote(scalars, rd_ref.at[me], rd_send, rd_recv, slot, other) for slot, other in enumerate(others)]
    copies.append(pltpu.make_async_copy(scalars, rd_ref.at[me], rd_local))
    for copy in copies:
        copy.start()
    for stream in streams:
        stream.finish()
    for copy in small:
        copy.wait_send()
    for copy in copies:
        copy.wait()


def scatter_tokens(partial, extra, rows=None):
    if not kernels_fit():
        total = lax.psum_scatter(partial, "tensor", scatter_dimension=0, tiled=True).astype(f32)
        flat = jnp.transpose(extra, (0, 2, 1)).reshape(partial.shape[0], 8)
        side = lax.psum_scatter(flat, "tensor", scatter_dimension=0, tiled=True).T
        if rows is None:
            return total, side
        inverse = lax.rsqrt(side / INNER + epsilon)
        dots = jnp.sum(rows.astype(f32) * total, -1)[None] * inverse
        scalars = jnp.concatenate([inverse[:1], dots[1:]])
        return (
            total,
            side,
            lax.all_gather(rows, "tensor", axis=0, tiled=True),
            lax.all_gather(scalars, "tensor", axis=0),
        )
    count, columns = partial.shape[0] // 4, partial.shape[1]
    vmem = pl.BlockSpec(memory_space=pltpu.VMEM)
    anywhere = pl.BlockSpec(memory_space=pl.ANY)
    return pl.pallas_call(
        scatter_kernel,
        out_shape=(
            jax.ShapeDtypeStruct((count, columns), f32),
            jax.ShapeDtypeStruct((8, count), f32),
            jax.ShapeDtypeStruct((4 * rows.shape[0], rows.shape[1]), rows.dtype),
            jax.ShapeDtypeStruct((4, 8, count), f32),
        ),
        in_specs=[vmem] * 3,
        out_specs=(vmem, vmem, anywhere, vmem),
        scratch_shapes=[
            pltpu.VMEM((6, count, columns), bf16),
            pltpu.VMEM((3, 8, count), f32),
            pltpu.SemaphoreType.DMA((6,)),
            pltpu.SemaphoreType.DMA((6,)),
            pltpu.SemaphoreType.DMA((3,)),
            pltpu.SemaphoreType.DMA((3,)),
            pltpu.SemaphoreType.DMA,
            pltpu.SemaphoreType.DMA((6,)),
            pltpu.SemaphoreType.DMA((6,)),
            pltpu.VMEM((8, count), f32),
            pltpu.SemaphoreType.DMA,
            pltpu.SemaphoreType.DMA((3,)),
            pltpu.SemaphoreType.DMA((3,)),
        ],
        compiler_params=pltpu.CompilerParams(
            collective_id=5, has_side_effects=True, vmem_limit_bytes=32 * 2**20
        ),
        cost_estimate=pl.CostEstimate(flops=0, bytes_accessed=150 * 2**20, transcendentals=0),
    )(partial, extra, rows)


def near_rows(rows):
    return -(-rows // 32) * 16


class SquareSum:
    def __init__(self, g_ref, sib, relay, came, send_sem, recv_sem):
        self.g_ref, self.sib, self.relay, self.came = g_ref, sib, relay, came
        self.send_sem, self.recv_sem = send_sem, recv_sem
        self.rows = sib.shape[1]
        self.index, self.core, self.sibling, self.by_x, self.by_y = neighbours()
        self.chip = lax.div(self.index, 2)
        self.chip_x, self.chip_y = lax.div(self.by_x, 2), lax.div(self.by_y, 2)
        self.chip_far = 3 - self.chip
        split = near_rows(self.rows)
        self.near = pl.ds(0, split)
        self.far = pl.ds(split, self.rows - split)

    def send(self, source, target, slot, where):
        return remote(source, target, self.send_sem, self.recv_sem, slot, {"dp": where})

    def to_sibling(self, chip):
        theirs = 2 * chip + 1 - self.core
        return self.send(rows_at(self.g_ref, theirs, self.rows), self.sib.at[chip], chip, self.sibling)

    def start(self):
        for chip in range(4):
            self.to_sibling(chip).start()

    def add(self, chip):
        self.sib[chip] = (
            self.sib[chip].astype(f32) + rows_at(self.g_ref, 2 * chip + self.core, self.rows)[...].astype(f32)
        ).astype(bf16)

    def copy(self, slot):
        sib, far, near_half, far_half = self.sib, self.chip_far, self.near, self.far
        source, target, where = {
            4: (sib.at[far, near_half, :], self.relay.at[near_half, :], self.by_x),
            5: (sib.at[far, far_half, :], self.relay.at[far_half, :], self.by_y),
            6: (sib.at[self.chip_x, near_half, :], self.came.at[0, near_half, :], self.by_x),
            7: (sib.at[self.chip_y, far_half, :], self.came.at[1, far_half, :], self.by_y),
            8: (sib.at[self.chip_x, far_half, :], self.came.at[0, far_half, :], self.by_x),
            9: (sib.at[self.chip_y, near_half, :], self.came.at[1, near_half, :], self.by_y),
        }[slot]
        return self.send(source, target, slot, where)

    def cores(self):
        for chip in range(4):
            self.to_sibling(chip).wait_recv()
        self.add(self.chip_far)
        self.copy(4).start()
        self.copy(5).start()
        self.add(self.chip_x)
        self.copy(6).start()
        self.add(self.chip_y)
        self.copy(7).start()

    def join(self):
        self.copy(4).wait_recv()
        near = (self.sib[self.chip_y, self.near, :].astype(f32) + self.relay[self.near, :].astype(f32)).astype(bf16)
        self.sib[self.chip_y, self.near, :] = near
        self.copy(9).start()
        self.copy(5).wait_recv()
        far = (self.sib[self.chip_x, self.far, :].astype(f32) + self.relay[self.far, :].astype(f32)).astype(bf16)
        self.sib[self.chip_x, self.far, :] = far
        self.copy(8).start()

    def finish(self):
        for slot in range(6, 10):
            self.copy(slot).wait_recv()
        own = rows_at(self.g_ref, self.index, self.rows)[...].astype(f32) + self.sib[self.chip].astype(f32)
        for slot in range(4, 10):
            self.copy(slot).wait_send()
        for chip in range(4):
            self.to_sibling(chip).wait_send()
        return own + (self.came[0].astype(f32) + self.came[1].astype(f32))


def exchange_kernel(
    p_any,
    x_any,
    d_any,
    dr_any,
    sc_any,
    mi_ref,
    mo_ref,
    *refs,
    follows,
):
    if follows:
        (l_ref, r_ref, gain_ref, b_ref, i_ref), refs = refs[:5], refs[5:]
    (o_ref, ni_ref, no_ref, slots_ref, os_ref), refs = refs[:5], refs[5:]
    if follows:
        (or_ref, og_ref, ox_ref, rd_ref), refs = refs[:4], refs[4:]
    (p_ref, x_ref, d_ref, dr_ref, sc_ref, g_ref, h_ref, s_ref, fetch_sem), refs = refs[:9], refs[9:]
    square, refs = refs[:15], refs[15:]
    lines = (Line(0), Line(1))
    me = lax.axis_index("tensor")
    index, core, sibling, by_x, by_y = neighbours()
    fetches = [
        pltpu.make_async_copy(source, target, fetch_sem.at[slot])
        for slot, (source, target) in enumerate(
            ((p_any, p_ref), (x_any, x_ref), (d_any, d_ref), (dr_any, dr_ref), (sc_any, sc_ref))
        )
    ]
    for fetch in fetches:
        fetch.start()
    greet([{"tensor": lax.rem(me + 1, 4)}, {"tensor": lax.rem(me + 3, 4)}, {"dp": sibling}, {"dp": by_x}, {"dp": by_y}])
    sums = [SquareSum(ref, *square[5 * at : 5 * at + 5]) for at, ref in enumerate((g_ref, h_ref, s_ref))]
    if follows:
        came, low_grad, scalars, rd_local, rd_send, rd_recv, *line_sems = refs
        half = o_ref.shape[0] // 2
        og_ref[...] = jnp.zeros_like(og_ref)

        def work(part):
            rows = slice(part * half, (part + 1) * half)
            d_normed = o_ref[rows, :]
            layer_in = l_ref[rows, :]
            inverse = lax.rsqrt(jnp.mean(layer_in * layer_in, -1, keepdims=True) + epsilon)
            scaled = layer_in * inverse
            og_ref[0:1, :] += jnp.sum(d_normed * scaled, 0, keepdims=True)
            d_scaled = d_normed * gain_ref[0:1, :]
            fresh = r_ref[rows, :] + inverse * (d_scaled - scaled * jnp.mean(d_scaled * scaled, -1, keepdims=True))
            or_ref[rows, :] = fresh
            low = fresh.astype(bf16)
            low_grad[rows, :] = low
            products = low.astype(f32) * b_ref[rows, :]
            dots = dot_exact(jnp.ones((8, products.shape[1]), f32), products, NT)
            first_row = lax.broadcasted_iota(jnp.int32, dots.shape, 0) == 0
            scalars[:, rows] = jnp.where(first_row, i_ref[:, rows], dots)

        line_pass = Pass(lines, p_ref, o_ref, came, low_grad, ox_ref, line_sems, work)
        total = line_pass.sums[0]
        small = LineCopy(lines, scalars, lambda chunk: rd_ref.at[chunk], rd_local, rd_send, rd_recv)
    else:
        total = LineSum(lines, p_ref, o_ref, *refs)
    fetches[0].wait()
    if follows:
        line_pass.start()
    else:
        total.start()
    for fetch in fetches[1:]:
        fetch.wait()
    width = mo_ref.shape[1]
    share = x_ref.shape[1] // 4

    def grads(chip):
        rows = slice(chip * share, (chip + 1) * share)
        left = x_ref[:, rows]
        for at in range(0, 2 * width, 2 * LANES):
            cols = slice(at, at + 2 * LANES)
            g_ref[rows, cols] = dot(left, d_ref[:, cols], TN).astype(bf16)
        sums[0].to_sibling(chip).start()
        left = dr_ref[:, rows]
        for at in range(0, width, 2 * LANES):
            cols = slice(at, at + 2 * LANES)
            h_ref[rows, cols] = dot(left, sc_ref[:, cols], TN).astype(bf16)
        sums[1].to_sibling(chip).start()

    grads(0)
    grads(1)
    total.step(1)
    grads(2)
    grads(3)
    heads = HEADS // 4
    to = lax.broadcasted_iota(jnp.int32, (LANES, LANES), 0)
    source = lax.broadcasted_iota(jnp.int32, (LANES, LANES), 1)
    moved = jnp.where(jnp.logical_and(to == source + me * heads, source < heads), 1.0, 0.0).astype(bf16)
    both = d_ref[:, 2 * width : 2 * width + 2 * STATE]
    steps = d_ref[:, 2 * width + 2 * STATE :]
    for at in range(0, s_ref.shape[1], 2 * LANES):
        cols = slice(at, at + 2 * LANES)
        s_ref[: 2 * STATE, cols] = dot(both, x_ref[:, cols], TN).astype(bf16)
        s_ref[2 * STATE :, cols] = dot(moved, dot(steps, x_ref[:, cols], TN).astype(bf16)).astype(bf16)
    sums[2].start()
    if follows:
        total.step(2)
    for each in sums:
        each.cores()
    if follows:
        line_pass.turn(0)
        line_pass.between()
    for each in sums:
        each.join()
    if follows:
        line_pass.across()
        line_pass.turn(1)
        small.start()
    else:
        total.step(2)
    in_grad = sums[0].finish()
    for side in range(2):
        fresh = muon_decay * mi_ref[side] + in_grad[:, side * width : (side + 1) * width]
        ni_ref[side] = fresh
        slots_ref[side] = fresh.astype(bf16)
    fresh = muon_decay * mo_ref[...] + sums[1].finish()
    no_ref[...] = fresh
    slots_ref[2] = fresh.astype(bf16)
    os_ref[...] = sums[2].finish()
    if follows:
        line_pass.last()
        for time in range(1, 4):
            small.step(time)
        line_pass.finish()
        small.finish()
    else:
        total.step(3)
        total.own()
        total.finish()


def exchange(partial, gathered, d_all, d_rows, scaled_low, in_momentum, out_momentum, following=None):
    rows, width = out_momentum.shape
    if not kernels_fit():
        heads = HEADS // lax.axis_size("tensor")
        in_grad = dot(gathered, d_all[:, : 2 * width], TN).astype(bf16)
        out_grad = dot(d_rows, scaled_low, TN).astype(bf16)
        shared_grad = dot(d_all[:, 2 * width :], gathered, TN).astype(bf16)
        steps_grad = lax.dynamic_update_slice_in_dim(
            jnp.zeros((LANES, D), bf16),
            shared_grad[2 * STATE : 2 * STATE + heads],
            lax.axis_index("tensor") * heads,
            0,
        )
        shared_grad = jnp.concatenate([shared_grad[: 2 * STATE], steps_grad], 0)
        add = lambda v: lax.psum_scatter(v, "dp", scatter_dimension=0, tiled=True).astype(f32)
        in_sum = add(in_grad)
        in_new = muon_decay * in_momentum + jnp.stack([in_sum[:, :width], in_sum[:, width:]])
        out_new = muon_decay * out_momentum + add(out_grad)
        d_normed = lax.psum_scatter(partial, "tensor", scatter_dimension=0, tiled=True).astype(f32)
        results = (
            d_normed,
            in_new,
            out_new,
            jnp.concatenate([in_new, out_new[None]]).astype(bf16),
            add(shared_grad),
        )
        if following is None:
            return results
        layer_in, grad_resid, in_gain, branch, scale = following
        grad_resid, d_in_gain = input_step(d_normed, layer_in, grad_resid, in_gain)
        d_branch = grad_resid.astype(bf16)
        dots = jnp.sum(d_branch.astype(f32) * branch, -1)
        scalars = jnp.concatenate([scale[:1], jnp.broadcast_to(dots[None], (7, dots.shape[0]))])
        return (
            *results,
            grad_resid,
            d_in_gain,
            lax.all_gather(d_branch, "tensor", axis=0, tiled=True),
            lax.all_gather(scalars, "tensor", axis=0),
        )
    count, columns = partial.shape[0] // 4, partial.shape[1]
    vmem = pl.BlockSpec(memory_space=pltpu.VMEM)
    anywhere = pl.BlockSpec(memory_space=pl.ANY)
    fetched = (partial, gathered, d_all, d_rows, scaled_low)
    square = []
    shapes = ((D, 2 * width), (D, width), (SHARED_COLS, D))
    for tall, wide in shapes:
        square += [
            pltpu.VMEM((4, tall // 8, wide), bf16),
            pltpu.VMEM((tall // 8, wide), bf16),
            pltpu.VMEM((2, tall // 8, wide), bf16),
            pltpu.SemaphoreType.DMA((10,)),
            pltpu.SemaphoreType.DMA((10,)),
        ]
    line = pltpu.SemaphoreType.DMA((6,))
    out_shape = [
        jax.ShapeDtypeStruct((count, columns), f32),
        jax.ShapeDtypeStruct((2, rows, width), f32),
        jax.ShapeDtypeStruct((rows, width), f32),
        jax.ShapeDtypeStruct((3, rows, width), bf16),
        jax.ShapeDtypeStruct((SHARED_COLS // 8, D), f32),
    ]
    out_specs = [vmem] * 5
    if following is None:
        more = ()
        scratch = [pltpu.VMEM((6, count, columns), bf16), line, line]
    else:
        layer_in, grad_resid, in_gain, branch, scale = following
        more = (layer_in, grad_resid, jnp.broadcast_to(in_gain[None], (8, columns)), branch, scale)
        out_shape += [
            jax.ShapeDtypeStruct((count, columns), f32),
            jax.ShapeDtypeStruct((8, columns), f32),
            jax.ShapeDtypeStruct((4 * count, columns), bf16),
            jax.ShapeDtypeStruct((4, 8, count), f32),
        ]
        out_specs += [vmem, vmem, anywhere, vmem]
        scratch = [
            pltpu.VMEM((2, 6, count // 2, columns), bf16),
            pltpu.VMEM((count, columns), bf16),
            pltpu.VMEM((8, count), f32),
            pltpu.SemaphoreType.DMA,
            line,
            line,
            *pass_sems(),
        ]
    results = pl.pallas_call(
        functools.partial(exchange_kernel, follows=following is not None),
        out_shape=tuple(out_shape),
        in_specs=[anywhere] * 5 + [vmem] * (2 + len(more)),
        out_specs=tuple(out_specs),
        scratch_shapes=[
            *[pltpu.VMEM(each.shape, bf16) for each in fetched],
            *[pltpu.VMEM(shape, bf16) for shape in shapes],
            pltpu.SemaphoreType.DMA((5,)),
            *square,
            *scratch,
        ],
        compiler_params=pltpu.CompilerParams(
            collective_id=3 if following is None else 7, has_side_effects=True, vmem_limit_bytes=62 * 2**20
        ),
        cost_estimate=pl.CostEstimate(flops=10**10, bytes_accessed=150 * 2**20, transcendentals=0),
    )(*fetched, in_momentum, out_momentum, *more)
    if following is None:
        return results
    return (*results[:6], results[6][0], *results[7:])


def input_step(d_normed, layer_in, grad_resid, in_gain):
    inverse = lax.rsqrt(jnp.mean(layer_in * layer_in, -1, keepdims=True) + epsilon)
    scaled_in = layer_in * inverse
    d_in_gain = jnp.sum(d_normed * scaled_in, 0)
    d_scaled_in = d_normed * in_gain
    grad_resid = grad_resid + inverse * (
        d_scaled_in - scaled_in * jnp.mean(d_scaled_in * scaled_in, -1, keepdims=True)
    )
    return grad_resid, d_in_gain


def tail_kernel(
    s_ref,
    v_ref,
    b_ref,
    os_ref,
    ov_ref,
    t_ref,
    whole,
    low,
    next_low,
    shifted,
    mine,
    came,
    vsum,
    vcame,
    send_sem,
    recv_sem,
    small_send,
    small_recv,
    block_send,
    block_recv,
    block_local,
):
    me = lax.axis_index("tensor")
    index, core, sibling, by_x, by_y = neighbours()
    beside = me + 1 - 2 * lax.rem(me, 2)
    beyond = lax.rem(me + 2, 4)
    others_dp = [lax.rem(index + ahead, 8) for ahead in range(1, 8)]
    greet([{"tensor": beside}, {"tensor": beyond}, *[{"dp": other} for other in others_dp]])
    blocks, rows = b_ref.shape[0], b_ref.shape[1]

    def block_to(owner):
        return pltpu.make_async_remote_copy(
            src_ref=b_ref.at[owner],
            dst_ref=whole.at[index],
            send_sem=block_send.at[owner],
            recv_sem=block_recv.at[index],
            device_id={"dp": owner},
            device_id_type=MESH,
        )

    for owner in range(blocks):

        @pl.when(index != owner)
        def _(owner=owner):
            block_to(owner).start()

        @pl.when(index == owner)
        def _(owner=owner):
            pltpu.make_async_copy(b_ref.at[owner], whole.at[owner], block_local.at[0]).start()

    @pl.when(index >= blocks)
    def _():
        for place in range(8):
            pltpu.make_async_copy(b_ref.at[place % blocks], whole.at[place], block_local.at[place]).start()

    mine[0] = s_ref[...].astype(bf16)
    first = remote(mine.at[0], came.at[0], send_sem, recv_sem, 0, {"tensor": beside})
    first.start()
    first.wait()
    mine[1] = (mine[0].astype(f32) + came[0].astype(f32)).astype(bf16)
    second = remote(mine.at[1], came.at[1], send_sem, recv_sem, 1, {"tensor": beyond})
    second.start()
    second.wait()
    os_ref[index] = (mine[1].astype(f32) + came[1].astype(f32)).astype(bf16)

    for owner in range(blocks):

        @pl.when(index == owner)
        def _(owner=owner):
            pltpu.make_async_copy(b_ref.at[owner], whole.at[owner], block_local.at[0]).wait()

    for sender in range(8):

        @pl.when(jnp.logical_and(index < blocks, index != sender))
        def _(sender=sender):
            place = whole.at[sender]
            remote(place, place, block_send, block_recv, sender, {"dp": sibling}).wait_recv()

    @pl.when(index >= blocks)
    def _():
        for place in range(8):
            pltpu.make_async_copy(b_ref.at[place % blocks], whole.at[place], block_local.at[place]).wait()

    half = s_ref.shape[0] // 2
    near, far, everything = pl.ds(0, half), pl.ds(half, half), pl.ds(0, 2 * half)

    def send(owner, part, slot, where):
        place = os_ref.at[owner, part, :]
        copy = remote(place, place, send_sem, recv_sem, slot, {"dp": where})
        copy.start()
        return copy

    def small(source, target, slot, where):
        copy = remote(source, target, small_send, small_recv, slot, where)
        copy.start()
        return copy

    vsum[0] = v_ref[...]
    pending = small(vsum.at[0], vcame.at[0], 0, {"dp": sibling})
    copies = [
        send(index, near, 2, by_x),
        send(index, far, 3, by_y),
        send(index, far, 4, by_x),
        send(index, near, 5, by_y),
        send(index, everything, 8, sibling),
    ]
    squares = jnp.zeros((1, 1), f32)
    for at in range(8):
        part = whole[at].astype(f32)
        squares = squares + jnp.sum(part * part)
    scale = 1.0 / (jnp.sqrt(squares) + 1e-07)
    for at in range(0, 8, 2):
        part = jnp.concatenate([whole[at], whole[at + 1]], 0).astype(f32) * scale
        low[:, at * rows : (at + 2) * rows] = part.T.astype(bf16)
    chains = [(low, next_low, shifted)]
    advance(chains, 0)
    pending.wait()
    vsum[1] = vsum[0] + vcame[0]
    pending = small(vsum.at[1], vcame.at[1], 1, {"dp": by_x})
    copies[0].wait_recv()
    copies.append(send(by_x, near, 6, by_y))
    copies[1].wait_recv()
    copies.append(send(by_y, far, 7, by_x))
    advance(chains, 1)
    pending.wait()
    vsum[2] = vsum[1] + vcame[1]
    pending = small(vsum.at[2], vcame.at[2], 2, {"dp": by_y})
    copies[2].wait_recv()
    copies.append(send(by_x, everything, 9, sibling))
    copies[3].wait_recv()
    copies.append(send(by_y, everything, 10, sibling))
    advance(chains, 0)
    pending.wait()
    ov_ref[me] = vsum[2] + vcame[2]
    pending = small(ov_ref.at[me], ov_ref.at[me], 3, {"tensor": beside})
    copies[5].wait_recv()
    copies[6].wait_recv()
    copies.append(send(by_x + by_y - index, everything, 11, sibling))
    advance(chains, 1)
    pending.wait()
    base = pl.ds(2 * lax.div(me, 2), 2)
    pending = small(ov_ref.at[base], ov_ref.at[base], 4, {"tensor": beyond})
    advance(chains, 0)
    for at in range(0, 8, 2):
        t_ref[at * rows : (at + 2) * rows, :] = next_low[:, at * rows : (at + 2) * rows].astype(f32).T.astype(bf16)
    pending.wait()
    for at in (4, 7, 8, 9):
        copies[at].wait_recv()
    for copy in copies:
        copy.wait_send()
    for owner in range(blocks):

        @pl.when(index != owner)
        def _(owner=owner):
            block_to(owner).wait_send()


def finish_blocks(shard, vector, blocks):
    rows, width = blocks.shape[1:]
    if not kernels_fit():
        count = lax.axis_size("dp")
        total = lax.psum(shard, "tensor").astype(bf16)
        padded = jnp.pad(blocks, ((0, count - blocks.shape[0]), (0, 0), (0, 0)))
        whole = lax.all_to_all(padded, "dp", split_axis=0, concat_axis=0, tiled=True)
        return (
            lax.all_gather(total, "dp", axis=0),
            lax.all_gather(lax.psum(vector, "dp"), "tensor", axis=0),
            orthogonal(whole.reshape(D, width), bf16),
        )
    vmem = pl.BlockSpec(memory_space=pltpu.VMEM)
    anywhere = pl.BlockSpec(memory_space=pl.ANY)
    return pl.pallas_call(
        tail_kernel,
        out_shape=(
            jax.ShapeDtypeStruct((8, *shard.shape), bf16),
            jax.ShapeDtypeStruct((4, *vector.shape), f32),
            jax.ShapeDtypeStruct((D, width), bf16),
        ),
        in_specs=[vmem, vmem, anywhere],
        out_specs=(vmem, vmem, vmem),
        scratch_shapes=[
            pltpu.VMEM((8, rows, width), bf16),
            pltpu.VMEM((width, D), bf16),
            pltpu.VMEM((width, D), bf16),
            pltpu.VMEM((width, width), bf16),
            pltpu.VMEM((2, *shard.shape), bf16),
            pltpu.VMEM((2, *shard.shape), bf16),
            pltpu.VMEM((3, *vector.shape), f32),
            pltpu.VMEM((3, *vector.shape), f32),
            pltpu.SemaphoreType.DMA((12,)),
            pltpu.SemaphoreType.DMA((12,)),
            pltpu.SemaphoreType.DMA((5,)),
            pltpu.SemaphoreType.DMA((5,)),
            pltpu.SemaphoreType.DMA((8,)),
            pltpu.SemaphoreType.DMA((8,)),
            pltpu.SemaphoreType.DMA((8,)),
        ],
        compiler_params=pltpu.CompilerParams(
            collective_id=4, has_side_effects=True, vmem_limit_bytes=56 * 2**20
        ),
        cost_estimate=pl.CostEstimate(flops=2 * 10**10, bytes_accessed=100 * 2**20, transcendentals=0),
    )(shard, vector, blocks)


def advance(chains, flip):
    poly_zero = coef_first + coef_second + coef_third
    poly_one = coef_second + 2.0 * coef_third

    def unit(at, count, size):
        rows = lax.broadcasted_iota(jnp.int32, (count, size), 0) + at
        return jnp.where(rows == lax.broadcasted_iota(jnp.int32, (count, size), 1), 1.0, 0.0).astype(f32)

    for *buffers, shifted in chains:
        source = buffers[flip]
        size = source.shape[0]
        for at in range(0, size, 256):
            count = min(256, size - at)
            gram = dot(source[at : at + count, :], source[...], NT)
            shifted[at : at + count, :] = (gram - unit(at, count, size)).astype(bf16)
    for *buffers, shifted in chains:
        source, target = buffers[flip], buffers[1 - flip]
        size = source.shape[0]
        for at in range(0, size, 256):
            count = min(256, size - at)
            mine = shifted[at : at + count, :]
            poly = (
                poly_zero * unit(at, count, size)
                + poly_one * mine.astype(f32)
                + coef_third * dot(mine, shifted[...])
            )
            target[at : at + count, :] = dot(poly.astype(bf16), source[...]).astype(bf16)


def iterate(chains):
    def twice(_, carry):
        advance(chains, 0)
        advance(chains, 1)
        return carry

    lax.fori_loop(0, 2, twice, 0)
    advance(chains, 0)


def orthogonal_kernel(m_ref, o_ref, low, next_low, shifted):
    turned = m_ref[...].astype(f32).T
    scale = 1.0 / (jnp.sqrt(jnp.sum(turned * turned)) + 1e-07)
    low[...] = (turned * scale).astype(bf16)
    iterate([(low, next_low, shifted)])
    o_ref[...] = next_low[...].astype(f32).T.astype(o_ref.dtype)


def shared_step_kernel(m_ref, w_ref, o_ref, low, next_low, shifted):
    for layer in range(LAYERS):
        momentum = m_ref[layer]
        scale = 1.0 / (jnp.sqrt(jnp.sum(momentum * momentum)) + 1e-07)
        low[layer, :SSM_COLS, :] = (momentum * scale).astype(bf16)
        low[layer, SSM_COLS:, :] = jnp.zeros((low.shape[1] - SSM_COLS, D), bf16)
    iterate([(low.at[layer], next_low.at[layer], shifted.at[layer]) for layer in range(LAYERS)])
    rate = muon_rate * (D / SSM_COLS) ** 0.5
    for layer in range(LAYERS):
        o_ref[layer] = w_ref[layer].astype(f32) - rate * next_low[layer, :SSM_COLS, :].astype(f32)


def shared_step(momentum, weight):
    vmem = pl.BlockSpec(memory_space=pltpu.VMEM)
    padded = -(-SSM_COLS // LANES) * LANES
    return pl.pallas_call(
        shared_step_kernel,
        out_shape=jax.ShapeDtypeStruct(momentum.shape, f32),
        in_specs=[vmem, vmem],
        out_specs=vmem,
        scratch_shapes=[
            pltpu.VMEM((LAYERS, padded, D), bf16),
            pltpu.VMEM((LAYERS, padded, D), bf16),
            pltpu.VMEM((LAYERS, padded, padded), bf16),
        ],
        compiler_params=pltpu.CompilerParams(vmem_limit_bytes=56 * 2**20),
        cost_estimate=pl.CostEstimate(
            flops=20 * padded * padded * (2 * D + padded), bytes_accessed=12 * D * padded, transcendentals=0
        ),
    )(momentum, weight)


def orthogonal(matrix, dtype):
    length, size = matrix.shape
    vmem = pl.BlockSpec(memory_space=pltpu.VMEM)
    return pl.pallas_call(
        orthogonal_kernel,
        out_shape=jax.ShapeDtypeStruct((length, size), dtype),
        in_specs=[vmem],
        out_specs=vmem,
        scratch_shapes=[
            pltpu.VMEM((size, length), bf16),
            pltpu.VMEM((size, length), bf16),
            pltpu.VMEM((size, size), bf16),
        ],
        compiler_params=pltpu.CompilerParams(vmem_limit_bytes=56 * 2**20),
        cost_estimate=pl.CostEstimate(
            flops=10 * size * size * (2 * length + size), bytes_accessed=6 * size * length, transcendentals=0
        ),
    )(matrix)


def body(
    resid_in,
    in_weight,
    out_weight,
    shared_weight,
    small_params,
    in_momentum,
    out_momentum,
    shared_momentum,
    small_first,
    small_second,
    resid_grad,
):
    tensor_index = lax.axis_index("tensor")
    tensor_count = lax.axis_size("tensor")
    local_cols = in_weight.shape[3]
    local_heads = HEADS // tensor_count
    col_start = tensor_index * local_cols
    head_start = tensor_index * local_heads
    shard_rows = in_weight.shape[1]
    own_tokens = resid_in.shape[0]
    length = own_tokens * tensor_count

    row_start = lax.axis_index("dp") * shard_rows
    channels = small_params[:, : (KERNEL + 2) * INNER].reshape(LAYERS, KERNEL + 2, INNER)
    channels = lax.dynamic_slice_in_dim(channels, col_start, local_cols, 2)
    states_at = (KERNEL + 2) * INNER
    heads_at = states_at + (KERNEL + 1) * 2 * STATE
    by_state = small_params[:, states_at:heads_at].reshape(LAYERS, KERNEL + 1, 2 * STATE)
    by_head = small_params[:, heads_at : heads_at + 3 * HEADS].reshape(LAYERS, 3, HEADS)
    by_head = lax.dynamic_slice_in_dim(by_head, head_start, local_heads, 2)
    in_gains = small_params[:, heads_at + 3 * HEADS :]
    skips = jnp.repeat(by_head[:, 2:], WIDTH, axis=2)
    px_all = jnp.concatenate([channels, skips, jnp.zeros((LAYERS, 1, local_cols), f32)], 1)
    ps_all = jnp.pad(by_state, ((0, 0), (0, 8 - KERNEL - 1), (0, 0)))
    ph_all = jnp.pad(by_head[:, :2], ((0, 0), (0, 6), (0, LANES - local_heads)))

    w_in, w_out = [], []
    for layer in range(LAYERS):
        shared_rows = lax.dynamic_slice_in_dim(shared_weight[layer], row_start, shard_rows, 0)
        steps_weight = lax.dynamic_slice_in_dim(shared_rows, 2 * STATE + head_start, local_heads, 1)
        w_rows = jnp.concatenate(
            [
                in_weight[layer, :, 0],
                in_weight[layer, :, 1],
                shared_rows[:, : 2 * STATE],
                jnp.pad(steps_weight, ((0, 0), (0, LANES - local_heads))),
            ],
            1,
        )
        w_in.append(w_rows)
        w_out.append(out_weight[layer])
    in_momentum_planes = jnp.transpose(in_momentum, (0, 2, 1, 3))

    residual = resid_in
    inverse_in = lax.rsqrt(jnp.mean(residual * residual, -1, keepdims=True) + epsilon)
    normed_low = (residual * inverse_in * in_gains[0]).astype(bf16)
    gathered, w_in[0], w_out[0] = gather_first(normed_low, w_in[0], w_out[0])
    held = lax.optimization_barrier((gathered, *w_in[1:], *w_out[1:]))
    gathered = held[0]
    for later in range(1, LAYERS):
        w_in[later] = lax.all_gather(held[later], "dp", axis=0, tiled=True)
        w_out[later] = lax.all_gather(held[LAYERS - 1 + later], "dp", axis=0, tiled=True)
    saved = []
    branches = [None] * LAYERS
    for layer in range(LAYERS):
        projected, total, partial, squares, states = mixer_forward(
            gathered, w_in[layer], w_out[layer], px_all[layer], ps_all[layer], ph_all[layer]
        )
        saved.append((residual, gathered, projected, total, states))
        squares = squares[:, 0, :].reshape(tensor_count, 1, own_tokens)
        squares = jnp.broadcast_to(squares, (tensor_count, 8, own_tokens))
        if layer < LAYERS - 1:
            residual, branch, scale, gathered = forward_pass(partial, squares, residual, in_gains[layer + 1])
            branches[layer] = (branch, scale)
    summed, square_sum, d_rows, rd = scatter_tokens(partial, squares, resid_grad.astype(bf16))
    residual = residual + summed * lax.rsqrt(square_sum[0] / INNER + epsilon)[:, None]

    grad_resid = resid_grad
    in_new = [None] * LAYERS
    out_new = [None] * LAYERS
    slots = [None] * LAYERS
    shared_shards = [None] * LAYERS
    small_grads = [None] * LAYERS
    for layer in reversed(range(LAYERS)):
        layer_in, gathered, projected, total, states = saved[layer]
        rd = jnp.transpose(rd[:, :2], (0, 2, 1)).reshape(length, 2)
        d_all, scaled_low, partial, grad_x, grad_s, grad_h = mixer_backward(
            d_rows, w_in[layer], w_out[layer], projected, total, states, rd, px_all[layer], ps_all[layer], ph_all[layer]
        )
        following = None
        if layer > 0:
            following = (layer_in, grad_resid, in_gains[layer], *branches[layer - 1])
        results = exchange(
            partial, gathered, d_all, d_rows, scaled_low, in_momentum_planes[layer], out_momentum[layer], following
        )
        d_normed, in_new[layer], out_new[layer], slots[layer], shared_shards[layer] = results[:5]
        if layer > 0:
            grad_resid, d_in_gain, d_rows, rd = results[5:]
        else:
            grad_resid, d_in_gain = input_step(d_normed, layer_in, grad_resid, in_gains[layer])
        small_grads[layer] = jnp.concatenate([grad_x, grad_s, grad_h, d_in_gain.reshape(8, D // 8)], 1)

    in_momentum_new = jnp.transpose(jnp.stack(in_new), (0, 2, 1, 3))
    out_momentum_new = jnp.stack(out_new)
    block_count = 3 * LAYERS
    dp_count = lax.axis_size("dp")
    shared_total, vectors, turned = finish_blocks(
        jnp.concatenate(shared_shards, 0), jnp.concatenate(small_grads, 1), jnp.concatenate(slots, 0)
    )
    turned = turned.reshape(dp_count, shard_rows, local_cols)
    returned = lax.all_to_all(turned, "dp", split_axis=0, concat_axis=0, tiled=True)[:block_count]
    scale = muon_rate * (D / local_cols) ** 0.5
    updates = returned.astype(f32).reshape(LAYERS, 3, shard_rows, local_cols) * scale
    in_weight_new = in_weight.astype(f32) - jnp.transpose(updates[:, :2], (0, 2, 1, 3))
    out_weight_new = out_weight.astype(f32) - updates[:, 2]

    share = SHARED_COLS // dp_count
    shared_total = shared_total.reshape(dp_count, LAYERS, share, D)
    shared_total = jnp.transpose(shared_total, (1, 0, 2, 3)).reshape(LAYERS, SHARED_COLS, D)[:, :SSM_COLS]
    turned_momentum = muon_decay * jnp.transpose(shared_momentum, (0, 2, 1)) + shared_total.astype(f32)
    shared_momentum_new = jnp.transpose(turned_momentum, (0, 2, 1))
    shared_weight_new = jnp.transpose(
        shared_step(turned_momentum, jnp.transpose(shared_weight, (0, 2, 1))), (0, 2, 1)
    )
    small_rows = []
    for layer in range(LAYERS):
        width = local_cols + 2 * STATE + LANES + D // 8
        mine = vectors[:, :, layer * width : (layer + 1) * width]
        channel_grads = jnp.transpose(mine[:, :7, :local_cols], (1, 0, 2)).reshape(7, INNER)
        head_grads = jnp.transpose(mine[:, :2, local_cols + 2 * STATE :][:, :, :local_heads], (1, 0, 2))
        common = jnp.sum(mine, 0)
        state_grads = common[: KERNEL + 1, local_cols : local_cols + 2 * STATE]
        small_rows.append(
            jnp.concatenate(
                [
                    channel_grads[: KERNEL + 2].reshape(-1),
                    state_grads.reshape(-1),
                    head_grads.reshape(-1),
                    channel_grads[6].reshape(HEADS, WIDTH).sum(1),
                    common[:, local_cols + 2 * STATE + LANES :].reshape(-1),
                ]
            )
        )
    small_grad = jnp.stack(small_rows)
    first_new = beta_first * small_first + (1.0 - beta_first) * small_grad
    small_second_new = beta_second * small_second + (1.0 - beta_second) * small_grad * small_grad
    small_new = small_params - adam_rate * (first_new / (1.0 - beta_first**STEP)) / (
        jnp.sqrt(small_second_new / (1.0 - beta_second**STEP)) + 1e-08
    )
    return (
        residual,
        grad_resid,
        small_grad,
        small_second_new,
        small_new,
        in_momentum_new,
        in_weight_new,
        out_momentum_new,
        out_weight_new,
        shared_momentum_new,
        shared_weight_new,
    )


def solution(mesh):
    placed = (
        P(("dp", "tensor"), None),
        P(None, "dp", None, "tensor"),
        P(None, "dp", "tensor"),
        P(),
        P(),
        P(None, "dp", None, "tensor"),
        P(None, "dp", "tensor"),
        P(),
        P(),
        P(),
        P(("dp", "tensor"), None),
    )
    return jax.shard_map(
        body,
        mesh=mesh,
        in_specs=placed,
        out_specs=(
            P(("dp", "tensor"), None),
            P(("dp", "tensor"), None),
            P(),
            P(),
            P(),
            P(None, "dp", None, "tensor"),
            P(None, "dp", None, "tensor"),
            P(None, "dp", "tensor"),
            P(None, "dp", "tensor"),
            P(),
            P(),
        ),
        check_vma=False,
    )
```

```python
import functools

import jax
import jax.numpy as jnp
from jax import lax
from jax.experimental import pallas as pl
from jax.experimental.pallas import tpu as pltpu
from jax.sharding import PartitionSpec as P

D = 1536
INNER = 3072
HEADS = 48
STATE = 128
KERNEL = 4
SPAN = 256
LAYERS = 2
STEP = 10
SSM_COLS = 304
WIDTH = INNER // HEADS
LANES = 128
SHARED_COLS = 2 * STATE + LANES
HALO = 8

epsilon = 1e-05
highest = lax.Precision.HIGHEST
coef_first = 3.4445
coef_second = -4.775
coef_third = 2.0315
muon_decay = 0.95
muon_rate = 0.2
beta_first = 0.9
beta_second = 0.95
adam_rate = 0.2

MESH = pl.DeviceIdType.MESH
NN = (((1,), (0,)), ((), ()))
NT = (((1,), (1,)), ((), ()))
TN = (((0,), (0,)), ((), ()))
f32 = jnp.float32
bf16 = jnp.bfloat16


def dot(left, right, dims=NN):
    return lax.dot_general(left, right, dims, preferred_element_type=f32)


def dot_exact(left, right, dims=NN):
    return lax.dot_general(left, right, dims, precision=highest, preferred_element_type=f32)


def sigmoid(v):
    return 0.5 * jnp.tanh(0.5 * v) + 0.5


def softplus(v):
    small = jnp.exp(-jnp.abs(v))
    series = small * (1.0 - small * (0.5 - small * (1.0 / 3.0 - small * 0.25)))
    return jnp.maximum(v, 0.0) + jnp.where(small < 0.01, series, jnp.log(1.0 + small))


def steps_of(raw_in, ph_ref):
    raw = raw_in + ph_ref[1:2, :]
    timestep = softplus(raw)
    decay = -jnp.exp(ph_ref[0:1, :])
    log_decay = timestep * decay
    rows = lax.broadcasted_iota(jnp.int32, (SPAN, SPAN), 0)
    cols = lax.broadcasted_iota(jnp.int32, (SPAN, SPAN), 1)
    lower = jnp.where(rows >= cols, 1.0, 0.0).astype(f32)
    cumulative = dot_exact(lower, log_decay)
    return raw, timestep, decay, log_decay, cumulative, lower


def spread_heads(table, columns):
    high = table.astype(bf16)
    low = (table - high.astype(f32)).astype(bf16)
    head = lax.rem(lax.broadcasted_iota(jnp.int32, (2 * LANES, columns), 0), LANES)
    owned = head == lax.broadcasted_iota(jnp.int32, (2 * LANES, columns), 1) // WIDTH
    return dot(jnp.concatenate([high, low], 1), jnp.where(owned, 1.0, 0.0).astype(bf16))


def conv_of(pad, lanes, weights, first):
    total = weights[4:5, lanes] + weights[0:1, lanes] * pad[first : first + SPAN, lanes]
    for tap in range(1, KERNEL):
        total = total + weights[tap : tap + 1, lanes] * pad[first + tap : first + tap + SPAN, lanes]
    return total


def head_sums(values, owner):
    high = values.astype(bf16)
    low = (values - high.astype(f32)).astype(bf16)
    return dot(jnp.concatenate([high, low], 1), owner)


def matmul_into(target, left, right, dims, width, piece):
    for at in range(0, width, piece):
        cols = slice(at, min(at + piece, width))
        mine = right[:, cols] if dims == NN else right[cols, :]
        target[:, cols] = dot(left, mine, dims).astype(target.dtype)


def forward_kernel(
    g_ref, w_ref, wo_ref, px_ref, ps_ref, ph_ref, proj_ref, yt_ref, p_ref, sq_ref, st_ref, state, xpad, spad, gained
):
    step = pl.program_id(0)
    columns = yt_ref.shape[1]
    pairs = columns // LANES

    @pl.when(step == 0)
    def _():
        state[...] = jnp.zeros_like(state)
        xpad[0:HALO, :] = jnp.zeros((HALO, columns), f32)
        spad[0:HALO, :] = jnp.zeros((HALO, 2 * STATE), f32)

    @pl.when(step > 0)
    def _():
        xpad[0:HALO, :] = xpad[SPAN : SPAN + HALO, :]
        spad[0:HALO, :] = spad[SPAN : SPAN + HALO, :]

    matmul_into(proj_ref, g_ref[...], w_ref, NN, 2 * columns + SHARED_COLS, 2 * LANES)
    xpad[HALO:, :] = proj_ref[:, columns : 2 * columns]
    spad[HALO:, :] = proj_ref[:, 2 * columns : 2 * columns + 2 * STATE]
    first = HALO - KERNEL + 1
    pre_s = conv_of(spad, slice(None), ps_ref, first)
    bc = pre_s * sigmoid(pre_s)
    b_low, c_low = bc[:, :STATE].astype(bf16), bc[:, STATE:].astype(bf16)
    raw, timestep, decay, log_decay, cumulative, lower = steps_of(proj_ref[:, 2 * columns + 2 * STATE :], ph_ref)
    turned = cumulative.T
    grown = jnp.exp(cumulative)
    tail = jnp.exp(cumulative[SPAN - 1 : SPAN, :] - cumulative)
    scores = dot(c_low, b_low, NT) * lower
    wide_step, wide_grown, wide_tail = (spread_heads(each, columns) for each in (timestep, grown, tail))
    low_half = lax.broadcasted_iota(jnp.int32, (SPAN, LANES), 1) < WIDTH
    squares = jnp.zeros((SPAN, LANES), f32)
    half = SPAN // 2
    for pair in range(pairs):
        lanes = slice(pair * LANES, (pair + 1) * LANES)
        pre = conv_of(xpad, lanes, px_ref, first)
        xc = pre * sigmoid(pre)
        u = xc * wide_step[:, lanes]
        u_low = u.astype(bf16)
        mine = [jnp.where(low_half == (side == 0), u_low, jnp.zeros_like(u_low)) for side in range(2)]
        inside = []
        for rows, count in ((slice(0, half), half), (slice(half, SPAN), SPAN)):
            mixing = []
            for side in range(2):
                head = 2 * pair + side
                spread = cumulative[rows, head : head + 1] - turned[head : head + 1, :count]
                mixing.append((scores[rows, :count] * jnp.exp(jnp.minimum(spread, 0.0))).astype(bf16))
            inside.append(dot(jnp.concatenate(mixing, 1), jnp.concatenate([mine[0][:count], mine[1][:count]], 0)))
        held = state[:, lanes]
        held_low = held.astype(bf16)
        st_ref[0, :, lanes] = held_low
        grown_pair = wide_grown[:, lanes]
        carried = dot(c_low, held_low) * grown_pair
        tail_u = (wide_tail[:, lanes] * u).astype(bf16)
        state[:, lanes] = grown_pair[SPAN - 1 : SPAN, :] * held + dot(b_low, tail_u, TN)
        total = jnp.concatenate(inside, 0) + carried + px_ref[6:7, lanes] * xc
        yt_ref[:, lanes] = total
        gate = proj_ref[:, lanes]
        mixed = total * gate * sigmoid(gate)
        gained[:, lanes] = (mixed * px_ref[5:6, lanes]).astype(bf16)
        squares = squares + mixed * mixed
    sq_ref[0] = dot_exact(jnp.ones((8, LANES), f32), squares, NT)
    matmul_into(p_ref, gained[...], wo_ref, NT, D, 2 * LANES)


def backward_kernel(
    dr_ref,
    w_ref,
    wo_ref,
    gate_ref,
    x_ref,
    xh_ref,
    sh_ref,
    shh_ref,
    yt_ref,
    st_ref,
    rd_ref,
    px_ref,
    ps_ref,
    ph_ref,
    dall_ref,
    scaled_ref,
    p_ref,
    gx_ref,
    gs_ref,
    gh_ref,
    dstate,
    xpad,
    spad,
    dxpad,
    dspad,
    dsc,
):
    step = pl.program_id(0)
    steps = pl.num_programs(0)
    columns = x_ref.shape[1]
    pairs = columns // LANES

    @pl.when(step == 0)
    def _():
        dstate[...] = jnp.zeros_like(dstate)
        dxpad[SPAN:, :] = jnp.zeros((HALO, columns), f32)
        dspad[SPAN:, :] = jnp.zeros((HALO, 2 * STATE), f32)
        gx_ref[...] = jnp.zeros_like(gx_ref)
        gs_ref[...] = jnp.zeros_like(gs_ref)
        gh_ref[...] = jnp.zeros_like(gh_ref)

    @pl.when(step > 0)
    def _():
        dxpad[SPAN:, :] = dxpad[0:HALO, :]
        dspad[SPAN:, :] = dspad[0:HALO, :]

    matmul_into(dsc, dr_ref[...], wo_ref, NN, columns, 2 * LANES)
    before = jnp.where(step < steps - 1, 1.0, 0.0).astype(f32)
    xpad[0:HALO, :] = xh_ref[...] * before
    spad[0:HALO, :] = shh_ref[:, : 2 * STATE] * before
    xpad[HALO:, :] = x_ref[...]
    spad[HALO:, :] = sh_ref[:, : 2 * STATE]
    first = HALO - KERNEL + 1
    pre_s = conv_of(spad, slice(None), ps_ref, first)
    sig_s = sigmoid(pre_s)
    bc = pre_s * sig_s
    b_low, c_low = bc[:, :STATE].astype(bf16), bc[:, STATE:].astype(bf16)
    raw, timestep, decay, log_decay, cumulative, lower = steps_of(sh_ref[:, 2 * STATE :], ph_ref)
    turned = cumulative.T
    grown = jnp.exp(cumulative)
    tail = jnp.exp(cumulative[SPAN - 1 : SPAN, :] - cumulative)
    upper = lower.T
    scores = dot(b_low, c_low, NT) * upper
    wide_step, wide_grown, wide_tail = (spread_heads(each, columns) for each in (timestep, grown, tail))
    low_half = lax.broadcasted_iota(jnp.int32, (SPAN, LANES), 1) < WIDTH
    inverse = rd_ref[:, 0:1]
    dots = rd_ref[:, 1:2] * (1.0 / INNER)
    head_row = lax.rem(lax.broadcasted_iota(jnp.int32, (2 * LANES, LANES), 0), LANES) // WIDTH
    head_col = lax.broadcasted_iota(jnp.int32, (2 * LANES, LANES), 1)

    half = SPAN // 2
    d_scores = [jnp.zeros((half, SPAN), f32), jnp.zeros((half, half), f32)]
    d_b = jnp.zeros((SPAN, STATE), f32)
    d_c = jnp.zeros((SPAN, STATE), f32)
    d_cum = jnp.zeros((SPAN, LANES), f32)
    d_step = jnp.zeros((SPAN, LANES), f32)
    d_last = jnp.zeros((8, LANES), f32)
    for pair in range(pairs):
        lanes = slice(pair * LANES, (pair + 1) * LANES)
        owner = jnp.where(head_row + 2 * pair == head_col, 1.0, 0.0).astype(bf16)
        pre = conv_of(xpad, lanes, px_ref, first)
        sig = sigmoid(pre)
        xc = pre * sig
        step_pair = wide_step[:, lanes]
        u = xc * step_pair
        u_low = u.astype(bf16)
        gate = gate_ref[:, lanes]
        sig_gate = sigmoid(gate)
        silu = gate * sig_gate
        total = yt_ref[:, lanes]
        gain = px_ref[5:6, lanes]
        sn = total * silu * inverse
        scaled_ref[:, lanes] = (sn * gain).astype(bf16)
        d_scaled = dsc[:, lanes]
        gx_ref[5:6, lanes] += jnp.sum(d_scaled * sn, 0, keepdims=True)
        d_mixed = inverse * (d_scaled * gain - sn * dots)
        dall_ref[:, lanes] = (
            d_mixed * total * (sig_gate * (1.0 + gate * (1.0 - sig_gate)))
        ).astype(bf16)
        dy = d_mixed * silu
        skip = px_ref[6:7, lanes]
        gx_ref[6:7, lanes] += jnp.sum(dy * xc, 0, keepdims=True)
        dy_low = dy.astype(bf16)
        mine = [jnp.where(low_half == (side == 0), dy_low, jnp.zeros_like(dy_low)) for side in range(2)]
        du = []
        for block, start in ((0, 0), (1, half)):
            rows = slice(start, start + half)
            mixing = []
            for side in range(2):
                head = 2 * pair + side
                spread = turned[head : head + 1, start:] - cumulative[rows, head : head + 1]
                mask = jnp.exp(jnp.minimum(spread, 0.0))
                mixing.append((scores[rows, start:] * mask).astype(bf16))
                d_scores[block] = d_scores[block] + dot(u_low[rows], mine[side][start:], NT) * mask
            du.append(dot(jnp.concatenate(mixing, 1), jnp.concatenate([mine[0][start:], mine[1][start:]], 0)))
        held_low = st_ref[0, :, lanes]
        grown_pair = wide_grown[:, lanes]
        last_pair = grown_pair[SPAN - 1 : SPAN, :]
        d_after = dstate[:, lanes]
        d_after_low = d_after.astype(bf16)
        grown_dy = (grown_pair * dy).astype(bf16)
        d_c = d_c + dot(grown_dy, held_low, NT)
        tail_pair = wide_tail[:, lanes]
        du_tail = tail_pair * dot(b_low, d_after_low)
        d_b = d_b + dot((tail_pair * u).astype(bf16), d_after_low, NT)
        dstate[:, lanes] = last_pair * d_after + dot(c_low, grown_dy, TN)
        du = jnp.concatenate(du, 0) + du_tail
        u_round = u_low.astype(f32)
        y = total - skip * xc
        d_cum = d_cum + head_sums(dy_low.astype(f32) * y - u_round * du, owner)
        d_step = d_step + head_sums(xc * du, owner)
        ends = jnp.sum(u_round * du_tail, 0, keepdims=True) + last_pair * jnp.sum(
            d_after * held_low.astype(f32), 0, keepdims=True
        )
        d_last = d_last + head_sums(jnp.broadcast_to(ends, (8, LANES)), owner)
        d_pre = (skip * dy + step_pair * du) * (sig * (1.0 + pre * (1.0 - sig)))
        dxpad[0:SPAN, lanes] = d_pre
        d_x = px_ref[KERNEL - 1 : KERNEL, lanes] * d_pre
        gx_ref[4:5, lanes] += jnp.sum(d_pre, 0, keepdims=True)
        for tap in range(KERNEL):
            gx_ref[tap : tap + 1, lanes] += jnp.sum(
                d_pre * xpad[first + tap : first + tap + SPAN, lanes], 0, keepdims=True
            )
            if tap < KERNEL - 1:
                ahead = KERNEL - 1 - tap
                d_x = d_x + px_ref[tap : tap + 1, lanes] * dxpad[ahead : ahead + SPAN, lanes]
        dall_ref[:, columns + pair * LANES : columns + (pair + 1) * LANES] = d_x.astype(bf16)
    d_log = dot_exact(upper, d_cum) + d_last[0:1, :]
    d_raw = (d_step + d_log * decay) * sigmoid(raw)
    gh_ref[0:1, :] += jnp.sum(d_log * log_decay, 0, keepdims=True)
    gh_ref[1:2, :] += jnp.sum(d_raw, 0, keepdims=True)
    d_scores = jnp.concatenate(
        [d_scores[0], jnp.concatenate([jnp.zeros((half, half), f32), d_scores[1]], 1)], 0
    )
    d_scores_low = (d_scores * upper).astype(bf16)
    d_b = d_b + dot(d_scores_low, c_low)
    d_c = d_c + dot(d_scores_low, b_low, TN)
    slope_s = sig_s * (1.0 + pre_s * (1.0 - sig_s))
    d_pre_s = jnp.concatenate([d_b, d_c], 1) * slope_s
    dspad[0:SPAN, :] = d_pre_s
    d_s = ps_ref[KERNEL - 1 : KERNEL, :] * d_pre_s
    gs_ref[4:5, :] += jnp.sum(d_pre_s, 0, keepdims=True)
    for tap in range(KERNEL):
        gs_ref[tap : tap + 1, :] += jnp.sum(
            d_pre_s * spad[first + tap : first + tap + SPAN, :], 0, keepdims=True
        )
        if tap < KERNEL - 1:
            ahead = KERNEL - 1 - tap
            d_s = d_s + ps_ref[tap : tap + 1, :] * dspad[ahead : ahead + SPAN, :]
    dall_ref[:, 2 * columns : 2 * columns + 2 * STATE] = d_s.astype(bf16)
    dall_ref[:, 2 * columns + 2 * STATE :] = d_raw.astype(bf16)
    matmul_into(p_ref, dall_ref[...], w_ref, NT, D, 2 * LANES)


def resident(shape):
    return pl.BlockSpec(shape, lambda i: (0, 0), pipeline_mode=pl.Buffered(1))


def mixer_forward(gathered, w_in, w_out, px, ps, ph):
    length, columns = gathered.shape[0], px.shape[1]
    spans = length // SPAN
    width = 2 * columns + SHARED_COLS
    here = lambda i: (i, 0)
    return pl.pallas_call(
        forward_kernel,
        grid=(spans,),
        in_specs=[
            pl.BlockSpec((SPAN, D), here),
            resident((D, width)),
            resident((D, columns)),
            resident((8, columns)),
            resident((8, 2 * STATE)),
            resident((8, LANES)),
        ],
        out_specs=[
            pl.BlockSpec((SPAN, width), here),
            pl.BlockSpec((SPAN, columns), here),
            pl.BlockSpec((SPAN, D), here),
            pl.BlockSpec((1, 8, SPAN), lambda i: (i, 0, 0)),
            pl.BlockSpec((1, STATE, columns), lambda i: (i, 0, 0)),
        ],
        out_shape=[
            jax.ShapeDtypeStruct((length, width), f32),
            jax.ShapeDtypeStruct((length, columns), f32),
            jax.ShapeDtypeStruct((length, D), bf16),
            jax.ShapeDtypeStruct((spans, 8, SPAN), f32),
            jax.ShapeDtypeStruct((spans, STATE, columns), bf16),
        ],
        scratch_shapes=[
            pltpu.VMEM((STATE, columns), f32),
            pltpu.VMEM((SPAN + HALO, columns), f32),
            pltpu.VMEM((SPAN + HALO, 2 * STATE), f32),
            pltpu.VMEM((SPAN, columns), bf16),
        ],
        compiler_params=pltpu.CompilerParams(vmem_limit_bytes=56 * 2**20),
        cost_estimate=pl.CostEstimate(flops=10 * 10**9, bytes_accessed=32 * 2**20, transcendentals=0),
    )(gathered, w_in, w_out, px, ps, ph)


def mixer_backward(d_rows, w_in, w_out, projected, total, states, rd, px, ps, ph):
    length, columns = total.shape
    spans = length // SPAN
    width = 2 * columns + SHARED_COLS
    here = lambda i: (spans - 1 - i, 0)
    blocks = SPAN // HALO
    halo = lambda i: jnp.maximum((spans - 1 - i) * blocks - 1, 0)
    tail_block = 2 * columns // SHARED_COLS
    return pl.pallas_call(
        backward_kernel,
        grid=(spans,),
        in_specs=[
            pl.BlockSpec((SPAN, D), here),
            resident((D, width)),
            resident((D, columns)),
            pl.BlockSpec((SPAN, columns), here),
            pl.BlockSpec((SPAN, columns), lambda i: (spans - 1 - i, 1)),
            pl.BlockSpec((HALO, columns), lambda i: (halo(i), 1)),
            pl.BlockSpec((SPAN, SHARED_COLS), lambda i: (spans - 1 - i, tail_block)),
            pl.BlockSpec((HALO, SHARED_COLS), lambda i: (halo(i), tail_block)),
            pl.BlockSpec((SPAN, columns), here),
            pl.BlockSpec((1, STATE, columns), lambda i: (spans - 1 - i, 0, 0)),
            pl.BlockSpec((SPAN, 2), here),
            resident((8, columns)),
            resident((8, 2 * STATE)),
            resident((8, LANES)),
        ],
        out_specs=[
            pl.BlockSpec((SPAN, width), here),
            pl.BlockSpec((SPAN, columns), here),
            pl.BlockSpec((SPAN, D), here),
            pl.BlockSpec((8, columns), lambda i: (0, 0)),
            pl.BlockSpec((8, 2 * STATE), lambda i: (0, 0)),
            pl.BlockSpec((8, LANES), lambda i: (0, 0)),
        ],
        out_shape=[
            jax.ShapeDtypeStruct((length, width), bf16),
            jax.ShapeDtypeStruct((length, columns), bf16),
            jax.ShapeDtypeStruct((length, D), bf16),
            jax.ShapeDtypeStruct((8, columns), f32),
            jax.ShapeDtypeStruct((8, 2 * STATE), f32),
            jax.ShapeDtypeStruct((8, LANES), f32),
        ],
        scratch_shapes=[
            pltpu.VMEM((STATE, columns), f32),
            pltpu.VMEM((SPAN + HALO, columns), f32),
            pltpu.VMEM((SPAN + HALO, 2 * STATE), f32),
            pltpu.VMEM((SPAN + HALO, columns), f32),
            pltpu.VMEM((SPAN + HALO, 2 * STATE), f32),
            pltpu.VMEM((SPAN, columns), f32),
        ],
        compiler_params=pltpu.CompilerParams(vmem_limit_bytes=56 * 2**20),
        cost_estimate=pl.CostEstimate(flops=16 * 10**9, bytes_accessed=48 * 2**20, transcendentals=0),
    )(
        d_rows,
        w_in,
        w_out,
        projected,
        projected,
        projected,
        projected,
        projected,
        total,
        states,
        rd,
        px,
        ps,
        ph,
    )


def kernels_fit():
    return lax.axis_size("tensor") == 4 and lax.axis_size("dp") == 8


def neighbours():
    index = lax.axis_index("dp")
    core = lax.rem(index, 2)
    across = lax.rem(lax.div(index, 2), 2)
    along = lax.div(index, 4)
    return index, core, index + 1 - 2 * core, index + 2 - 4 * across, index + 4 - 8 * along


def greet(others):
    barrier = pltpu.get_barrier_semaphore()
    for other in others:
        pl.semaphore_signal(barrier, inc=1, device_id=other, device_id_type=MESH)
    pl.semaphore_wait(barrier, len(others))


def remote(source, target, send_sem, recv_sem, slot, where):
    return pltpu.make_async_remote_copy(
        src_ref=source,
        dst_ref=target,
        send_sem=send_sem.at[slot],
        recv_sem=recv_sem.at[slot],
        device_id=where,
        device_id_type=MESH,
    )


class Line:
    def __init__(self, side):
        me = lax.axis_index("tensor")
        self.side = side
        self.me = me
        self.pos = me if side == 0 else 3 - me
        self.next = {"tensor": lax.rem(me + (1 if side == 0 else 3), 4)}

    def chunk(self, ahead):
        return self.me + ahead if self.side == 0 else self.me - ahead


def rows_at(ref, chunk, count):
    return ref.at[pl.ds(pl.multiple_of(chunk * count, count), count), :]


class LineCopy:
    def __init__(self, lines, source, place, local_sem, send_sem, recv_sem):
        self.lines, self.source, self.place = lines, source, place
        self.send_sem, self.recv_sem = send_sem, recv_sem
        self.own = pltpu.make_async_copy(source, place(lines[0].me), local_sem)

    def outgoing(self, line, time):
        place = self.place(line.chunk(-time))
        source = self.source if time == 0 else place
        return remote(source, place, self.send_sem, self.recv_sem, 3 * line.side + time, line.next)

    def start(self):
        for line in self.lines:

            @pl.when(line.pos < 3)
            def _(line=line):
                self.outgoing(line, 0).start()

        self.own.start()

    def step(self, time):
        for line in self.lines:

            @pl.when(line.pos >= time)
            def _(line=line):
                place = self.place(line.chunk(-time))
                slot = 3 * line.side + time - 1
                remote(place, place, self.send_sem, self.recv_sem, slot, line.next).wait_recv()

            if time < 3:

                @pl.when(jnp.logical_and(line.pos >= time, line.pos < 3))
                def _(line=line):
                    self.outgoing(line, time).start()

    def finish(self):
        for time in range(3):
            for line in self.lines:

                @pl.when(jnp.logical_and(line.pos >= time, line.pos < 3))
                def _(line=line):
                    self.outgoing(line, time).wait_send()

        self.own.wait()


class SquareCopy:
    def __init__(self, source, result, local_sem, send_sem, recv_sem):
        self.source, self.result = source, result
        self.send_sem, self.recv_sem = send_sem, recv_sem
        self.rows = source.shape[0]
        self.split = near_rows(self.rows)
        self.index, core, self.sibling, self.by_x, self.by_y = neighbours()
        self.own = pltpu.make_async_copy(source, self.place(self.index, None), local_sem)

    def place(self, owner, side):
        start, count = {None: (0, self.rows), 0: (0, self.split), 1: (self.split, self.rows - self.split)}[side]
        return self.result.at[pl.ds(pl.multiple_of(owner * self.rows + start, 16), count), :]

    def copy(self, slot):
        near, far = self.source.at[pl.ds(0, self.split), :], self.source.at[pl.ds(self.split, self.rows - self.split), :]
        by_x, by_y = self.by_x, self.by_y
        source, owner, side, where = {
            0: (near, self.index, 0, by_x),
            1: (far, self.index, 1, by_y),
            2: (far, self.index, 1, by_x),
            3: (near, self.index, 0, by_y),
            4: (None, by_x, 0, by_y),
            5: (None, by_y, 1, by_x),
            6: (self.source, self.index, None, self.sibling),
            7: (None, by_x, None, self.sibling),
            8: (None, by_y, None, self.sibling),
            9: (None, by_x + by_y - self.index, None, self.sibling),
        }[slot]
        target = self.place(owner, side)
        return remote(target if source is None else source, target, self.send_sem, self.recv_sem, slot, {"dp": where})

    def start(self):
        for slot in (0, 1, 2, 3, 6):
            self.copy(slot).start()
        self.own.start()

    def relay(self):
        self.copy(0).wait_recv()
        self.copy(4).start()
        self.copy(1).wait_recv()
        self.copy(5).start()

    def forward(self):
        self.copy(2).wait_recv()
        self.copy(7).start()
        self.copy(3).wait_recv()
        self.copy(8).start()

    def last(self):
        self.copy(4).wait_recv()
        self.copy(5).wait_recv()
        self.copy(9).start()

    def finish(self):
        for slot in range(6, 10):
            self.copy(slot).wait_recv()
        for slot in range(10):
            self.copy(slot).wait_send()
        self.own.wait()


def first_kernel(x_ref, w_ref, v_ref, ox_ref, ow_ref, ov_ref, *sems):
    lines = (Line(0), Line(1))
    rows = x_ref.shape[0]
    me = lax.axis_index("tensor")
    index, core, sibling, by_x, by_y = neighbours()
    greet([{"tensor": lax.rem(me + 1, 4)}, {"tensor": lax.rem(me + 3, 4)}, {"dp": sibling}, {"dp": by_x}, {"dp": by_y}])
    tokens = LineCopy(lines, x_ref, lambda chunk: rows_at(ox_ref, chunk, rows), *sems[:3])
    weights = [SquareCopy(w_ref, ow_ref, *sems[3:6]), SquareCopy(v_ref, ov_ref, *sems[6:])]
    tokens.start()
    for each in weights:
        each.start()
    for each in weights:
        each.relay()
    tokens.step(1)
    for each in weights:
        each.forward()
    tokens.step(2)
    for each in weights:
        each.last()
    tokens.step(3)
    for each in weights:
        each.finish()
    tokens.finish()


def gather_first(rows, w_rows, v_rows):
    if not kernels_fit():
        return (
            lax.all_gather(rows, "tensor", axis=0, tiled=True),
            lax.all_gather(w_rows, "dp", axis=0, tiled=True),
            lax.all_gather(v_rows, "dp", axis=0, tiled=True),
        )
    anywhere = pl.BlockSpec(memory_space=pl.ANY)
    larger = lambda v, times: jax.ShapeDtypeStruct((times * v.shape[0], v.shape[1]), v.dtype)
    sems = lambda count: [
        pltpu.SemaphoreType.DMA,
        pltpu.SemaphoreType.DMA((count,)),
        pltpu.SemaphoreType.DMA((count,)),
    ]
    return pl.pallas_call(
        first_kernel,
        out_shape=(larger(rows, 4), larger(w_rows, 8), larger(v_rows, 8)),
        in_specs=[anywhere] * 3,
        out_specs=(anywhere,) * 3,
        scratch_shapes=[*sems(6), *sems(10), *sems(10)],
        compiler_params=pltpu.CompilerParams(collective_id=6, has_side_effects=True),
        cost_estimate=pl.CostEstimate(flops=0, bytes_accessed=150 * 2**20, transcendentals=0),
    )(rows, w_rows, v_rows)


def gather_tokens(rows, small):
    if not kernels_fit():
        return lax.all_gather(rows, "tensor", axis=0, tiled=True), lax.all_gather(small, "tensor", axis=0)
    count, columns = rows.shape
    vmem = pl.BlockSpec(memory_space=pltpu.VMEM)
    anywhere = pl.BlockSpec(memory_space=pl.ANY)
    return pl.pallas_call(
        gather_kernel,
        out_shape=(
            jax.ShapeDtypeStruct((4 * count, columns), rows.dtype),
            jax.ShapeDtypeStruct((4, *small.shape), small.dtype),
        ),
        in_specs=[anywhere, vmem],
        out_specs=(anywhere, vmem),
        scratch_shapes=[
            pltpu.SemaphoreType.DMA,
            pltpu.SemaphoreType.DMA,
            pltpu.SemaphoreType.DMA((6,)),
            pltpu.SemaphoreType.DMA((6,)),
            pltpu.SemaphoreType.DMA((6,)),
            pltpu.SemaphoreType.DMA((6,)),
        ],
        compiler_params=pltpu.CompilerParams(collective_id=0, has_side_effects=True),
        cost_estimate=pl.CostEstimate(flops=0, bytes_accessed=150 * 2**20, transcendentals=0),
    )(rows, small)


class LineSum:
    def __init__(self, lines, p_ref, o_ref, came, send_sem, recv_sem, first_row=0):
        self.lines, self.p_ref, self.o_ref, self.came = lines, p_ref, o_ref, came
        self.send_sem, self.recv_sem = send_sem, recv_sem
        self.first_row, self.count = first_row, came.shape[1]
        self.rows = p_ref.shape[0] // 4

    def part(self, chunk):
        start = pl.multiple_of(chunk * self.rows + self.first_row, self.count)
        return self.p_ref.at[pl.ds(start, self.count), :]

    def copy(self, line, time, first):
        slot = 3 * line.side + time
        target = self.came.at[slot]
        source = self.part(line.chunk(3 - time)) if first else self.came.at[slot - 1]
        return remote(source, target, self.send_sem, self.recv_sem, slot, line.next)

    def start(self, times=(0, 1, 2)):
        for line in self.lines:

            @pl.when(line.pos == 0)
            def _(line=line):
                for time in times:
                    self.copy(line, time, True).start()

    def step(self, time):
        for line in self.lines:

            @pl.when(jnp.logical_and(line.pos > 0, line.pos <= time))
            def _(line=line):
                slot = 3 * line.side + time - 1
                place = self.came.at[slot]
                remote(place, place, self.send_sem, self.recv_sem, slot, line.next).wait_recv()

            if time < 3:

                @pl.when(jnp.logical_and(line.pos > 0, line.pos <= time))
                def _(line=line):
                    slot = 3 * line.side + time - 1
                    mine = self.part(line.chunk(3 - time))[...]
                    self.came[slot] = (self.came[slot].astype(f32) + mine.astype(f32)).astype(bf16)
                    self.copy(line, time, False).start()

    def own(self):
        place = pl.ds(self.first_row, self.count)
        self.o_ref[place, :] = self.part(self.lines[0].me)[...].astype(f32)
        for line in self.lines:

            @pl.when(line.pos > 0)
            def _(line=line):
                self.o_ref[place, :] += self.came[3 * line.side + 2].astype(f32)

    def finish(self):
        for line in self.lines:

            @pl.when(line.pos == 0)
            def _(line=line):
                for time in range(3):
                    self.copy(line, time, True).wait_send()

            for time in range(1, 3):

                @pl.when(jnp.logical_and(line.pos > 0, line.pos <= time))
                def _(line=line):
                    self.copy(line, time, False).wait_send()


class Pass:
    def __init__(self, lines, p_ref, o_ref, came, x_ref, ox_ref, sems, work):
        half = came.shape[2]
        self.work = work
        self.sums, self.copies = [], []
        for part in range(2):
            sum_send, sum_recv, copy_local, copy_send, copy_recv = sems[5 * part : 5 * part + 5]
            first_row = part * half
            self.sums.append(LineSum(lines, p_ref, o_ref, came.at[part], sum_send, sum_recv, first_row))
            place = lambda chunk, first_row=first_row: ox_ref.at[
                pl.ds(pl.multiple_of(chunk * 2 * half + first_row, half), half), :
            ]
            source = x_ref.at[pl.ds(first_row, half), :]
            self.copies.append(LineCopy(lines, source, place, copy_local, copy_send, copy_recv))

    def start(self):
        self.sums[0].start()
        self.sums[1].start((0,))

    def turn(self, part):
        self.sums[part].step(3)
        self.sums[part].own()
        self.work(part)
        self.copies[part].start()

    def between(self):
        self.sums[1].start((1, 2))
        self.sums[1].step(1)

    def across(self):
        self.copies[0].step(1)
        self.sums[1].step(2)
        self.copies[0].step(2)

    def last(self):
        self.copies[0].step(3)
        for time in range(1, 4):
            self.copies[1].step(time)

    def finish(self):
        for each in (*self.sums, *self.copies):
            each.finish()


def pass_sems():
    line = pltpu.SemaphoreType.DMA((6,))
    return [line, line, pltpu.SemaphoreType.DMA, line, line] * 2


def column_of(row, count):
    return jnp.broadcast_to(row, (LANES, count)).T[:, 0:1]


def forward_pass_kernel(
    p_any,
    q_ref,
    r_ref,
    gain_ref,
    or_ref,
    ob_ref,
    oi_ref,
    ox_ref,
    p_ref,
    normed,
    came,
    came_q,
    fetch_sem,
    small_send,
    small_recv,
    *sems,
):
    lines = (Line(0), Line(1))
    me = lax.axis_index("tensor")
    others = [{"tensor": lax.rem(me + ahead, 4)} for ahead in (1, 2, 3)]
    fetch = pltpu.make_async_copy(p_any, p_ref, fetch_sem)
    fetch.start()
    greet(others)
    small = [
        remote(q_ref.at[lax.rem(me + slot + 1, 4)], came_q.at[slot], small_send, small_recv, slot, other)
        for slot, other in enumerate(others)
    ]
    for copy in small:
        copy.start()
    count = r_ref.shape[0]
    half = count // 2

    def work(part):
        rows = slice(part * half, (part + 1) * half)
        branch = ob_ref[rows, :] * column_of(oi_ref[0:1, rows], half)
        ob_ref[rows, :] = branch
        fresh = r_ref[rows, :] + branch
        or_ref[rows, :] = fresh
        inverse = lax.rsqrt(jnp.mean(fresh * fresh, -1, keepdims=True) + epsilon)
        normed[rows, :] = (fresh * inverse * gain_ref[0:1, :]).astype(bf16)

    line_pass = Pass(lines, p_ref, ob_ref, came, normed, ox_ref, sems, work)
    fetch.wait()
    line_pass.start()
    for copy in small:
        copy.wait_recv()
    oi_ref[...] = lax.rsqrt((q_ref[me] + came_q[0] + came_q[1] + came_q[2]) * (1.0 / INNER) + epsilon)
    line_pass.sums[0].step(1)
    line_pass.sums[0].step(2)
    line_pass.turn(0)
    line_pass.between()
    line_pass.across()
    line_pass.turn(1)
    line_pass.last()
    line_pass.finish()
    for copy in small:
        copy.wait_send()


def forward_pass(partial, squares, residual, in_gain):
    count, columns = residual.shape
    if not kernels_fit():
        summed, scale = plain_scatter(partial, squares)
        branch = summed * scale[0][:, None]
        fresh = residual + branch
        inverse = lax.rsqrt(jnp.mean(fresh * fresh, -1, keepdims=True) + epsilon)
        normed = (fresh * inverse * in_gain).astype(bf16)
        return fresh, branch, scale, lax.all_gather(normed, "tensor", axis=0, tiled=True)
    vmem = pl.BlockSpec(memory_space=pltpu.VMEM)
    anywhere = pl.BlockSpec(memory_space=pl.ANY)
    return pl.pallas_call(
        forward_pass_kernel,
        out_shape=(
            jax.ShapeDtypeStruct((count, columns), f32),
            jax.ShapeDtypeStruct((count, columns), f32),
            jax.ShapeDtypeStruct((8, count), f32),
            jax.ShapeDtypeStruct((4 * count, columns), bf16),
        ),
        in_specs=[anywhere, vmem, vmem, vmem],
        out_specs=(vmem, vmem, vmem, anywhere),
        scratch_shapes=[
            pltpu.VMEM(partial.shape, bf16),
            pltpu.VMEM((count, columns), bf16),
            pltpu.VMEM((2, 6, count // 2, columns), bf16),
            pltpu.VMEM((3, 8, count), f32),
            pltpu.SemaphoreType.DMA,
            pltpu.SemaphoreType.DMA((3,)),
            pltpu.SemaphoreType.DMA((3,)),
            *pass_sems(),
        ],
        compiler_params=pltpu.CompilerParams(
            collective_id=2, has_side_effects=True, vmem_limit_bytes=40 * 2**20
        ),
        cost_estimate=pl.CostEstimate(flops=0, bytes_accessed=250 * 2**20, transcendentals=0),
    )(partial, squares, residual, jnp.broadcast_to(in_gain[None], (8, columns)))


def scatter_kernel(
    p_ref,
    q_ref,
    x_ref,
    r_ref,
    or_ref,
    ox_ref,
    rd_ref,
    o_ref,
    oq_ref,
    came,
    came_q,
    send_sem,
    recv_sem,
    small_send,
    small_recv,
    local_sem,
    copy_send,
    copy_recv,
    scalars,
    rd_local,
    rd_send,
    rd_recv,
):
    lines = (Line(0), Line(1))
    me = lax.axis_index("tensor")
    others = [{"tensor": lax.rem(me + ahead, 4)} for ahead in (1, 2, 3)]
    greet(others)
    small = [
        remote(q_ref.at[lax.rem(me + slot + 1, 4)], came_q.at[slot], small_send, small_recv, slot, other)
        for slot, other in enumerate(others)
    ]
    for copy in small:
        copy.start()
    rows = x_ref.shape[0]
    place = lambda chunk: rows_at(ox_ref, chunk, rows)
    total = LineSum(lines, p_ref, o_ref, came, send_sem, recv_sem)
    streams = [LineCopy(lines, x_ref, place, local_sem, copy_send, copy_recv), total]
    for stream in streams:
        stream.start()
    for copy in small:
        copy.wait_recv()
    oq_ref[...] = q_ref[me] + came_q[0] + came_q[1] + came_q[2]
    for time in range(1, 4):
        for stream in streams:
            stream.step(time)
    total.own()
    inverse = lax.rsqrt(oq_ref[...] * (1.0 / INNER) + epsilon)
    products = x_ref[...].astype(f32) * o_ref[...]
    dots = dot_exact(jnp.ones((8, products.shape[1]), f32), products, NT) * inverse
    first_row = lax.broadcasted_iota(jnp.int32, scalars.shape, 0) == 0
    scalars[...] = jnp.where(first_row, inverse, dots)
    copies = [remote(scalars, rd_ref.at[me], rd_send, rd_recv, slot, other) for slot, other in enumerate(others)]
    copies.append(pltpu.make_async_copy(scalars, rd_ref.at[me], rd_local))
    for copy in copies:
        copy.start()
    or_ref[...] = r_ref[...] + o_ref[...] * column_of(inverse[0:1, :], rows)
    for stream in streams:
        stream.finish()
    for copy in small:
        copy.wait_send()
    for copy in copies:
        copy.wait()


def plain_scatter(partial, extra):
    total = lax.psum_scatter(partial, "tensor", scatter_dimension=0, tiled=True).astype(f32)
    flat = jnp.transpose(extra, (0, 2, 1)).reshape(partial.shape[0], 8)
    side = lax.psum_scatter(flat, "tensor", scatter_dimension=0, tiled=True).T
    return total, lax.rsqrt(side / INNER + epsilon)


def last_scatter(partial, extra, rows, residual):
    if not kernels_fit():
        total, inverse = plain_scatter(partial, extra)
        dots = jnp.sum(rows.astype(f32) * total, -1)[None] * inverse
        scalars = jnp.concatenate([inverse[:1], dots[1:]])
        return (
            residual + total * inverse[0][:, None],
            lax.all_gather(rows, "tensor", axis=0, tiled=True),
            lax.all_gather(scalars, "tensor", axis=0),
        )
    count, columns = partial.shape[0] // 4, partial.shape[1]
    vmem = pl.BlockSpec(memory_space=pltpu.VMEM)
    anywhere = pl.BlockSpec(memory_space=pl.ANY)
    return pl.pallas_call(
        scatter_kernel,
        out_shape=(
            jax.ShapeDtypeStruct((count, columns), f32),
            jax.ShapeDtypeStruct((4 * rows.shape[0], rows.shape[1]), rows.dtype),
            jax.ShapeDtypeStruct((4, 8, count), f32),
        ),
        in_specs=[vmem] * 4,
        out_specs=(vmem, anywhere, vmem),
        scratch_shapes=[
            pltpu.VMEM((count, columns), f32),
            pltpu.VMEM((8, count), f32),
            pltpu.VMEM((6, count, columns), bf16),
            pltpu.VMEM((3, 8, count), f32),
            pltpu.SemaphoreType.DMA((6,)),
            pltpu.SemaphoreType.DMA((6,)),
            pltpu.SemaphoreType.DMA((3,)),
            pltpu.SemaphoreType.DMA((3,)),
            pltpu.SemaphoreType.DMA,
            pltpu.SemaphoreType.DMA((6,)),
            pltpu.SemaphoreType.DMA((6,)),
            pltpu.VMEM((8, count), f32),
            pltpu.SemaphoreType.DMA,
            pltpu.SemaphoreType.DMA((3,)),
            pltpu.SemaphoreType.DMA((3,)),
        ],
        compiler_params=pltpu.CompilerParams(
            collective_id=5, has_side_effects=True, vmem_limit_bytes=32 * 2**20
        ),
        cost_estimate=pl.CostEstimate(flops=0, bytes_accessed=150 * 2**20, transcendentals=0),
    )(partial, extra, rows, residual)


def near_rows(rows):
    return -(-rows // 32) * 16


class SquareSum:
    def __init__(self, g_ref, sib, relay, came, send_sem, recv_sem):
        self.g_ref, self.sib, self.relay, self.came = g_ref, sib, relay, came
        self.send_sem, self.recv_sem = send_sem, recv_sem
        self.rows = sib.shape[1]
        self.index, self.core, self.sibling, self.by_x, self.by_y = neighbours()
        self.chip = lax.div(self.index, 2)
        self.chip_x, self.chip_y = lax.div(self.by_x, 2), lax.div(self.by_y, 2)
        self.chip_far = 3 - self.chip
        split = near_rows(self.rows)
        self.near = pl.ds(0, split)
        self.far = pl.ds(split, self.rows - split)

    def send(self, source, target, slot, where):
        return remote(source, target, self.send_sem, self.recv_sem, slot, {"dp": where})

    def to_sibling(self, chip):
        theirs = 2 * chip + 1 - self.core
        return self.send(rows_at(self.g_ref, theirs, self.rows), self.sib.at[chip], chip, self.sibling)

    def start(self):
        for chip in range(4):
            self.to_sibling(chip).start()

    def add(self, chip):
        self.sib[chip] = (
            self.sib[chip].astype(f32) + rows_at(self.g_ref, 2 * chip + self.core, self.rows)[...].astype(f32)
        ).astype(bf16)

    def copy(self, slot):
        sib, far, near_half, far_half = self.sib, self.chip_far, self.near, self.far
        source, target, where = {
            4: (sib.at[far, near_half, :], self.relay.at[near_half, :], self.by_x),
            5: (sib.at[far, far_half, :], self.relay.at[far_half, :], self.by_y),
            6: (sib.at[self.chip_x, near_half, :], self.came.at[0, near_half, :], self.by_x),
            7: (sib.at[self.chip_y, far_half, :], self.came.at[1, far_half, :], self.by_y),
            8: (sib.at[self.chip_x, far_half, :], self.came.at[0, far_half, :], self.by_x),
            9: (sib.at[self.chip_y, near_half, :], self.came.at[1, near_half, :], self.by_y),
        }[slot]
        return self.send(source, target, slot, where)

    def cores(self):
        for chip in range(4):
            self.to_sibling(chip).wait_recv()
        self.add(self.chip_far)
        self.copy(4).start()
        self.copy(5).start()
        self.add(self.chip_x)
        self.copy(6).start()
        self.add(self.chip_y)
        self.copy(7).start()

    def join(self):
        self.copy(4).wait_recv()
        near = (self.sib[self.chip_y, self.near, :].astype(f32) + self.relay[self.near, :].astype(f32)).astype(bf16)
        self.sib[self.chip_y, self.near, :] = near
        self.copy(9).start()
        self.copy(5).wait_recv()
        far = (self.sib[self.chip_x, self.far, :].astype(f32) + self.relay[self.far, :].astype(f32)).astype(bf16)
        self.sib[self.chip_x, self.far, :] = far
        self.copy(8).start()

    def finish(self):
        for slot in range(6, 10):
            self.copy(slot).wait_recv()
        own = rows_at(self.g_ref, self.index, self.rows)[...].astype(f32) + self.sib[self.chip].astype(f32)
        for slot in range(4, 10):
            self.copy(slot).wait_send()
        for chip in range(4):
            self.to_sibling(chip).wait_send()
        return own + (self.came[0].astype(f32) + self.came[1].astype(f32))


def exchange_kernel(
    p_any,
    x_any,
    d_any,
    dr_any,
    sc_any,
    mi_ref,
    mo_ref,
    l_ref,
    r_ref,
    gain_ref,
    *refs,
    gathers,
):
    if gathers:
        (b_ref, i_ref), refs = refs[:2], refs[2:]
    (ni_ref, no_ref, slots_ref, os_ref, or_ref, og_ref), refs = refs[:6], refs[6:]
    if gathers:
        (ox_ref, rd_ref), refs = refs[:2], refs[2:]
    o_ref, refs = refs[0], refs[1:]
    (p_ref, x_ref, d_ref, dr_ref, sc_ref, g_ref, h_ref, s_ref, fetch_sem), refs = refs[:9], refs[9:]
    square, refs = refs[:15], refs[15:]
    lines = (Line(0), Line(1))
    me = lax.axis_index("tensor")
    index, core, sibling, by_x, by_y = neighbours()
    fetches = [
        pltpu.make_async_copy(source, target, fetch_sem.at[slot])
        for slot, (source, target) in enumerate(
            ((p_any, p_ref), (x_any, x_ref), (d_any, d_ref), (dr_any, dr_ref), (sc_any, sc_ref))
        )
    ]
    for fetch in fetches:
        fetch.start()
    greet([{"tensor": lax.rem(me + 1, 4)}, {"tensor": lax.rem(me + 3, 4)}, {"dp": sibling}, {"dp": by_x}, {"dp": by_y}])
    sums = [SquareSum(ref, *square[5 * at : 5 * at + 5]) for at, ref in enumerate((g_ref, h_ref, s_ref))]
    og_ref[...] = jnp.zeros_like(og_ref)
    half = o_ref.shape[0] // 2

    def input_part(rows):
        d_normed = o_ref[rows, :]
        layer_in = l_ref[rows, :]
        inverse = lax.rsqrt(jnp.mean(layer_in * layer_in, -1, keepdims=True) + epsilon)
        scaled = layer_in * inverse
        og_ref[0:1, :] += jnp.sum(d_normed * scaled, 0, keepdims=True)
        d_scaled = d_normed * gain_ref[0:1, :]
        fresh = r_ref[rows, :] + inverse * (d_scaled - scaled * jnp.mean(d_scaled * scaled, -1, keepdims=True))
        or_ref[rows, :] = fresh
        return fresh

    if gathers:
        came, low_grad, scalars, rd_local, rd_send, rd_recv, *line_sems = refs

        def work(part):
            rows = slice(part * half, (part + 1) * half)
            low = input_part(rows).astype(bf16)
            low_grad[rows, :] = low
            products = low.astype(f32) * b_ref[rows, :]
            dots = dot_exact(jnp.ones((8, products.shape[1]), f32), products, NT)
            first_row = lax.broadcasted_iota(jnp.int32, dots.shape, 0) == 0
            scalars[:, rows] = jnp.where(first_row, i_ref[:, rows], dots)

        line_pass = Pass(lines, p_ref, o_ref, came, low_grad, ox_ref, line_sems, work)
        total = line_pass.sums[0]
        small = LineCopy(lines, scalars, lambda chunk: rd_ref.at[chunk], rd_local, rd_send, rd_recv)
    else:
        total = LineSum(lines, p_ref, o_ref, *refs)
    fetches[0].wait()
    if gathers:
        line_pass.start()
    else:
        total.start()
    for fetch in fetches[1:]:
        fetch.wait()
    width = mo_ref.shape[1]
    share = x_ref.shape[1] // 4

    def grads(chip):
        rows = slice(chip * share, (chip + 1) * share)
        left = x_ref[:, rows]
        for at in range(0, 2 * width, 2 * LANES):
            cols = slice(at, at + 2 * LANES)
            g_ref[rows, cols] = dot(left, d_ref[:, cols], TN).astype(bf16)
        sums[0].to_sibling(chip).start()
        left = dr_ref[:, rows]
        for at in range(0, width, 2 * LANES):
            cols = slice(at, at + 2 * LANES)
            h_ref[rows, cols] = dot(left, sc_ref[:, cols], TN).astype(bf16)
        sums[1].to_sibling(chip).start()

    grads(0)
    grads(1)
    if gathers:
        total.step(1)
    grads(2)
    grads(3)
    heads = HEADS // 4
    to = lax.broadcasted_iota(jnp.int32, (LANES, LANES), 0)
    source = lax.broadcasted_iota(jnp.int32, (LANES, LANES), 1)
    moved = jnp.where(jnp.logical_and(to == source + me * heads, source < heads), 1.0, 0.0).astype(bf16)
    both = d_ref[:, 2 * width : 2 * width + 2 * STATE]
    steps = d_ref[:, 2 * width + 2 * STATE :]
    for at in range(0, s_ref.shape[1], 2 * LANES):
        cols = slice(at, at + 2 * LANES)
        s_ref[: 2 * STATE, cols] = dot(both, x_ref[:, cols], TN).astype(bf16)
        s_ref[2 * STATE :, cols] = dot(moved, dot(steps, x_ref[:, cols], TN).astype(bf16)).astype(bf16)
    sums[2].start()
    if gathers:
        total.step(2)
    for each in sums:
        each.cores()
    if gathers:
        line_pass.turn(0)
        line_pass.between()
    else:
        total.step(1)
    for each in sums:
        each.join()
    if gathers:
        line_pass.across()
        line_pass.turn(1)
        small.start()
    else:
        total.step(2)
    in_grad = sums[0].finish()
    for side in range(2):
        fresh = muon_decay * mi_ref[side] + in_grad[:, side * width : (side + 1) * width]
        ni_ref[side] = fresh
        slots_ref[side] = fresh.astype(bf16)
    fresh = muon_decay * mo_ref[...] + sums[1].finish()
    no_ref[...] = fresh
    slots_ref[2] = fresh.astype(bf16)
    os_ref[...] = sums[2].finish()
    if gathers:
        line_pass.last()
        for time in range(1, 4):
            small.step(time)
        line_pass.finish()
        small.finish()
    else:
        total.step(3)
        total.own()
        for part in range(2):
            input_part(slice(part * half, (part + 1) * half))
        total.finish()


def exchange(
    partial, gathered, d_all, d_rows, scaled_low, in_momentum, out_momentum, layer_in, grad_resid, in_gain, below=None
):
    rows, width = out_momentum.shape
    if not kernels_fit():
        heads = HEADS // lax.axis_size("tensor")
        in_grad = dot(gathered, d_all[:, : 2 * width], TN).astype(bf16)
        out_grad = dot(d_rows, scaled_low, TN).astype(bf16)
        shared_grad = dot(d_all[:, 2 * width :], gathered, TN).astype(bf16)
        steps_grad = lax.dynamic_update_slice_in_dim(
            jnp.zeros((LANES, D), bf16),
            shared_grad[2 * STATE : 2 * STATE + heads],
            lax.axis_index("tensor") * heads,
            0,
        )
        shared_grad = jnp.concatenate([shared_grad[: 2 * STATE], steps_grad], 0)
        add = lambda v: lax.psum_scatter(v, "dp", scatter_dimension=0, tiled=True).astype(f32)
        in_sum = add(in_grad)
        in_new = muon_decay * in_momentum + jnp.stack([in_sum[:, :width], in_sum[:, width:]])
        out_new = muon_decay * out_momentum + add(out_grad)
        d_normed = lax.psum_scatter(partial, "tensor", scatter_dimension=0, tiled=True).astype(f32)
        grad_resid, d_in_gain = input_step(d_normed, layer_in, grad_resid, in_gain)
        results = (
            in_new,
            out_new,
            jnp.concatenate([in_new, out_new[None]]).astype(bf16),
            add(shared_grad),
            grad_resid,
            d_in_gain,
        )
        if below is None:
            return results
        branch, scale = below
        d_branch = grad_resid.astype(bf16)
        dots = jnp.sum(d_branch.astype(f32) * branch, -1)
        scalars = jnp.concatenate([scale[:1], jnp.broadcast_to(dots[None], (7, dots.shape[0]))])
        return (
            *results,
            lax.all_gather(d_branch, "tensor", axis=0, tiled=True),
            lax.all_gather(scalars, "tensor", axis=0),
        )
    count, columns = partial.shape[0] // 4, partial.shape[1]
    vmem = pl.BlockSpec(memory_space=pltpu.VMEM)
    anywhere = pl.BlockSpec(memory_space=pl.ANY)
    fetched = (partial, gathered, d_all, d_rows, scaled_low)
    square = []
    shapes = ((D, 2 * width), (D, width), (SHARED_COLS, D))
    for tall, wide in shapes:
        square += [
            pltpu.VMEM((4, tall // 8, wide), bf16),
            pltpu.VMEM((tall // 8, wide), bf16),
            pltpu.VMEM((2, tall // 8, wide), bf16),
            pltpu.SemaphoreType.DMA((10,)),
            pltpu.SemaphoreType.DMA((10,)),
        ]
    line = pltpu.SemaphoreType.DMA((6,))
    out_shape = [
        jax.ShapeDtypeStruct((2, rows, width), f32),
        jax.ShapeDtypeStruct((rows, width), f32),
        jax.ShapeDtypeStruct((3, rows, width), bf16),
        jax.ShapeDtypeStruct((SHARED_COLS // 8, D), f32),
        jax.ShapeDtypeStruct((count, columns), f32),
        jax.ShapeDtypeStruct((8, columns), f32),
    ]
    out_specs = [vmem] * 6
    operands = [*fetched, in_momentum, out_momentum, layer_in, grad_resid, jnp.broadcast_to(in_gain[None], (8, columns))]
    if below is None:
        scratch = [pltpu.VMEM((6, count, columns), bf16), line, line]
    else:
        operands += below
        out_shape += [
            jax.ShapeDtypeStruct((4 * count, columns), bf16),
            jax.ShapeDtypeStruct((4, 8, count), f32),
        ]
        out_specs += [anywhere, vmem]
        scratch = [
            pltpu.VMEM((2, 6, count // 2, columns), bf16),
            pltpu.VMEM((count, columns), bf16),
            pltpu.VMEM((8, count), f32),
            pltpu.SemaphoreType.DMA,
            line,
            line,
            *pass_sems(),
        ]
    results = pl.pallas_call(
        functools.partial(exchange_kernel, gathers=below is not None),
        out_shape=tuple(out_shape),
        in_specs=[anywhere] * 5 + [vmem] * (len(operands) - 5),
        out_specs=tuple(out_specs),
        scratch_shapes=[
            pltpu.VMEM((count, columns), f32),
            *[pltpu.VMEM(each.shape, bf16) for each in fetched],
            *[pltpu.VMEM(shape, bf16) for shape in shapes],
            pltpu.SemaphoreType.DMA((5,)),
            *square,
            *scratch,
        ],
        compiler_params=pltpu.CompilerParams(
            collective_id=3 if below is None else 7, has_side_effects=True, vmem_limit_bytes=62 * 2**20
        ),
        cost_estimate=pl.CostEstimate(flops=10**10, bytes_accessed=150 * 2**20, transcendentals=0),
    )(*operands)
    return (*results[:5], results[5][0], *results[6:])


def input_step(d_normed, layer_in, grad_resid, in_gain):
    inverse = lax.rsqrt(jnp.mean(layer_in * layer_in, -1, keepdims=True) + epsilon)
    scaled_in = layer_in * inverse
    d_in_gain = jnp.sum(d_normed * scaled_in, 0)
    d_scaled_in = d_normed * in_gain
    grad_resid = grad_resid + inverse * (
        d_scaled_in - scaled_in * jnp.mean(d_scaled_in * scaled_in, -1, keepdims=True)
    )
    return grad_resid, d_in_gain


def tail_kernel(
    s_ref,
    v_ref,
    b_ref,
    os_ref,
    ov_ref,
    t_ref,
    whole,
    low,
    next_low,
    shifted,
    mine,
    came,
    vsum,
    vcame,
    send_sem,
    recv_sem,
    small_send,
    small_recv,
    block_send,
    block_recv,
    block_local,
):
    me = lax.axis_index("tensor")
    index, core, sibling, by_x, by_y = neighbours()
    beside = me + 1 - 2 * lax.rem(me, 2)
    beyond = lax.rem(me + 2, 4)
    others_dp = [lax.rem(index + ahead, 8) for ahead in range(1, 8)]
    greet([{"tensor": beside}, {"tensor": beyond}, *[{"dp": other} for other in others_dp]])
    blocks, rows = b_ref.shape[0], b_ref.shape[1]

    def block_to(owner):
        return pltpu.make_async_remote_copy(
            src_ref=b_ref.at[owner],
            dst_ref=whole.at[index],
            send_sem=block_send.at[owner],
            recv_sem=block_recv.at[index],
            device_id={"dp": owner},
            device_id_type=MESH,
        )

    for owner in range(blocks):

        @pl.when(index != owner)
        def _(owner=owner):
            block_to(owner).start()

        @pl.when(index == owner)
        def _(owner=owner):
            pltpu.make_async_copy(b_ref.at[owner], whole.at[owner], block_local.at[0]).start()

    @pl.when(index >= blocks)
    def _():
        for place in range(8):
            pltpu.make_async_copy(b_ref.at[place % blocks], whole.at[place], block_local.at[place]).start()

    mine[0] = s_ref[...].astype(bf16)
    first = remote(mine.at[0], came.at[0], send_sem, recv_sem, 0, {"tensor": beside})
    first.start()
    first.wait()
    mine[1] = (mine[0].astype(f32) + came[0].astype(f32)).astype(bf16)
    second = remote(mine.at[1], came.at[1], send_sem, recv_sem, 1, {"tensor": beyond})
    second.start()
    second.wait()
    os_ref[index] = (mine[1].astype(f32) + came[1].astype(f32)).astype(bf16)

    for owner in range(blocks):

        @pl.when(index == owner)
        def _(owner=owner):
            pltpu.make_async_copy(b_ref.at[owner], whole.at[owner], block_local.at[0]).wait()

    for sender in range(8):

        @pl.when(jnp.logical_and(index < blocks, index != sender))
        def _(sender=sender):
            place = whole.at[sender]
            remote(place, place, block_send, block_recv, sender, {"dp": sibling}).wait_recv()

    @pl.when(index >= blocks)
    def _():
        for place in range(8):
            pltpu.make_async_copy(b_ref.at[place % blocks], whole.at[place], block_local.at[place]).wait()

    half = s_ref.shape[0] // 2
    near, far, everything = pl.ds(0, half), pl.ds(half, half), pl.ds(0, 2 * half)

    def send(owner, part, slot, where):
        place = os_ref.at[owner, part, :]
        copy = remote(place, place, send_sem, recv_sem, slot, {"dp": where})
        copy.start()
        return copy

    def small(source, target, slot, where):
        copy = remote(source, target, small_send, small_recv, slot, where)
        copy.start()
        return copy

    vsum[0] = v_ref[...]
    pending = small(vsum.at[0], vcame.at[0], 0, {"dp": sibling})
    copies = [
        send(index, near, 2, by_x),
        send(index, far, 3, by_y),
        send(index, far, 4, by_x),
        send(index, near, 5, by_y),
        send(index, everything, 8, sibling),
    ]
    squares = jnp.zeros((1, 1), f32)
    for at in range(8):
        part = whole[at].astype(f32)
        squares = squares + jnp.sum(part * part)
    scale = 1.0 / (jnp.sqrt(squares) + 1e-07)
    for at in range(0, 8, 2):
        part = jnp.concatenate([whole[at], whole[at + 1]], 0).astype(f32) * scale
        low[:, at * rows : (at + 2) * rows] = part.T.astype(bf16)
    chains = [(low, next_low, shifted)]
    advance(chains, 0)
    pending.wait()
    vsum[1] = vsum[0] + vcame[0]
    pending = small(vsum.at[1], vcame.at[1], 1, {"dp": by_x})
    copies[0].wait_recv()
    copies.append(send(by_x, near, 6, by_y))
    copies[1].wait_recv()
    copies.append(send(by_y, far, 7, by_x))
    advance(chains, 1)
    pending.wait()
    vsum[2] = vsum[1] + vcame[1]
    pending = small(vsum.at[2], vcame.at[2], 2, {"dp": by_y})
    copies[2].wait_recv()
    copies.append(send(by_x, everything, 9, sibling))
    copies[3].wait_recv()
    copies.append(send(by_y, everything, 10, sibling))
    advance(chains, 0)
    pending.wait()
    ov_ref[me] = vsum[2] + vcame[2]
    pending = small(ov_ref.at[me], ov_ref.at[me], 3, {"tensor": beside})
    copies[5].wait_recv()
    copies[6].wait_recv()
    copies.append(send(by_x + by_y - index, everything, 11, sibling))
    advance(chains, 1)
    pending.wait()
    base = pl.ds(2 * lax.div(me, 2), 2)
    pending = small(ov_ref.at[base], ov_ref.at[base], 4, {"tensor": beyond})
    advance(chains, 0)
    for at in range(0, 8, 2):
        t_ref[at * rows : (at + 2) * rows, :] = next_low[:, at * rows : (at + 2) * rows].astype(f32).T.astype(bf16)
    pending.wait()
    for at in (4, 7, 8, 9):
        copies[at].wait_recv()
    for copy in copies:
        copy.wait_send()
    for owner in range(blocks):

        @pl.when(index != owner)
        def _(owner=owner):
            block_to(owner).wait_send()


def finish_blocks(shard, vector, blocks):
    rows, width = blocks.shape[1:]
    if not kernels_fit():
        count = lax.axis_size("dp")
        total = lax.psum(shard, "tensor").astype(bf16)
        padded = jnp.pad(blocks, ((0, count - blocks.shape[0]), (0, 0), (0, 0)))
        whole = lax.all_to_all(padded, "dp", split_axis=0, concat_axis=0, tiled=True)
        return (
            lax.all_gather(total, "dp", axis=0),
            lax.all_gather(lax.psum(vector, "dp"), "tensor", axis=0),
            orthogonal(whole.reshape(D, width), bf16),
        )
    vmem = pl.BlockSpec(memory_space=pltpu.VMEM)
    anywhere = pl.BlockSpec(memory_space=pl.ANY)
    return pl.pallas_call(
        tail_kernel,
        out_shape=(
            jax.ShapeDtypeStruct((8, *shard.shape), bf16),
            jax.ShapeDtypeStruct((4, *vector.shape), f32),
            jax.ShapeDtypeStruct((D, width), bf16),
        ),
        in_specs=[vmem, vmem, anywhere],
        out_specs=(vmem, vmem, vmem),
        scratch_shapes=[
            pltpu.VMEM((8, rows, width), bf16),
            pltpu.VMEM((width, D), bf16),
            pltpu.VMEM((width, D), bf16),
            pltpu.VMEM((width, width), bf16),
            pltpu.VMEM((2, *shard.shape), bf16),
            pltpu.VMEM((2, *shard.shape), bf16),
            pltpu.VMEM((3, *vector.shape), f32),
            pltpu.VMEM((3, *vector.shape), f32),
            pltpu.SemaphoreType.DMA((12,)),
            pltpu.SemaphoreType.DMA((12,)),
            pltpu.SemaphoreType.DMA((5,)),
            pltpu.SemaphoreType.DMA((5,)),
            pltpu.SemaphoreType.DMA((8,)),
            pltpu.SemaphoreType.DMA((8,)),
            pltpu.SemaphoreType.DMA((8,)),
        ],
        compiler_params=pltpu.CompilerParams(
            collective_id=4, has_side_effects=True, vmem_limit_bytes=56 * 2**20
        ),
        cost_estimate=pl.CostEstimate(flops=2 * 10**10, bytes_accessed=100 * 2**20, transcendentals=0),
    )(shard, vector, blocks)


def advance(chains, flip):
    poly_zero = coef_first + coef_second + coef_third
    poly_one = coef_second + 2.0 * coef_third

    def unit(at, count, size):
        rows = lax.broadcasted_iota(jnp.int32, (count, size), 0) + at
        return jnp.where(rows == lax.broadcasted_iota(jnp.int32, (count, size), 1), 1.0, 0.0).astype(f32)

    for *buffers, shifted in chains:
        source = buffers[flip]
        size = source.shape[0]
        for at in range(0, size, 256):
            count = min(256, size - at)
            gram = dot(source[at : at + count, :], source[...], NT)
            shifted[at : at + count, :] = (gram - unit(at, count, size)).astype(bf16)
    for *buffers, shifted in chains:
        source, target = buffers[flip], buffers[1 - flip]
        size = source.shape[0]
        for at in range(0, size, 256):
            count = min(256, size - at)
            mine = shifted[at : at + count, :]
            poly = (
                poly_zero * unit(at, count, size)
                + poly_one * mine.astype(f32)
                + coef_third * dot(mine, shifted[...])
            )
            target[at : at + count, :] = dot(poly.astype(bf16), source[...]).astype(bf16)


def iterate(chains):
    def twice(_, carry):
        advance(chains, 0)
        advance(chains, 1)
        return carry

    lax.fori_loop(0, 2, twice, 0)
    advance(chains, 0)


def orthogonal_kernel(m_ref, o_ref, low, next_low, shifted):
    turned = m_ref[...].astype(f32).T
    scale = 1.0 / (jnp.sqrt(jnp.sum(turned * turned)) + 1e-07)
    low[...] = (turned * scale).astype(bf16)
    iterate([(low, next_low, shifted)])
    o_ref[...] = next_low[...].astype(f32).T.astype(o_ref.dtype)


def shared_step_kernel(m_ref, w_ref, o_ref, low, next_low, shifted):
    for layer in range(LAYERS):
        momentum = m_ref[layer]
        scale = 1.0 / (jnp.sqrt(jnp.sum(momentum * momentum)) + 1e-07)
        low[layer, :SSM_COLS, :] = (momentum * scale).astype(bf16)
        low[layer, SSM_COLS:, :] = jnp.zeros((low.shape[1] - SSM_COLS, D), bf16)
    iterate([(low.at[layer], next_low.at[layer], shifted.at[layer]) for layer in range(LAYERS)])
    rate = muon_rate * (D / SSM_COLS) ** 0.5
    for layer in range(LAYERS):
        o_ref[layer] = w_ref[layer].astype(f32) - rate * next_low[layer, :SSM_COLS, :].astype(f32)


def shared_pair_kernel(m_ref, w_ref, o_ref, low, next_low, shifted, both, send_sem, recv_sem):
    index, core, sibling, by_x, by_y = neighbours()
    greet([{"dp": sibling}])
    momentum = m_ref[core]
    scale = 1.0 / (jnp.sqrt(jnp.sum(momentum * momentum)) + 1e-07)
    low[:SSM_COLS, :] = (momentum * scale).astype(bf16)
    low[SSM_COLS:, :] = jnp.zeros((low.shape[0] - SSM_COLS, D), bf16)
    iterate([(low, next_low, shifted)])
    both[core] = next_low[...]
    copy = remote(both.at[core], both.at[core], send_sem, recv_sem, 0, {"dp": sibling})
    copy.start()
    copy.wait()
    rate = muon_rate * (D / SSM_COLS) ** 0.5
    for layer in range(2):
        o_ref[layer] = w_ref[layer].astype(f32) - rate * both[layer, :SSM_COLS, :].astype(f32)


def shared_step(momentum, weight):
    vmem = pl.BlockSpec(memory_space=pltpu.VMEM)
    padded = -(-SSM_COLS // LANES) * LANES
    pair = kernels_fit() and LAYERS == 2
    if pair:
        scratch = [
            pltpu.VMEM((padded, D), bf16),
            pltpu.VMEM((padded, D), bf16),
            pltpu.VMEM((padded, padded), bf16),
            pltpu.VMEM((2, padded, D), bf16),
            pltpu.SemaphoreType.DMA((1,)),
            pltpu.SemaphoreType.DMA((1,)),
        ]
        params = pltpu.CompilerParams(collective_id=0, has_side_effects=True, vmem_limit_bytes=56 * 2**20)
    else:
        scratch = [
            pltpu.VMEM((LAYERS, padded, D), bf16),
            pltpu.VMEM((LAYERS, padded, D), bf16),
            pltpu.VMEM((LAYERS, padded, padded), bf16),
        ]
        params = pltpu.CompilerParams(vmem_limit_bytes=56 * 2**20)
    return pl.pallas_call(
        shared_pair_kernel if pair else shared_step_kernel,
        out_shape=jax.ShapeDtypeStruct(momentum.shape, f32),
        in_specs=[vmem, vmem],
        out_specs=vmem,
        scratch_shapes=scratch,
        compiler_params=params,
        cost_estimate=pl.CostEstimate(
            flops=20 * padded * padded * (2 * D + padded), bytes_accessed=12 * D * padded, transcendentals=0
        ),
    )(momentum, weight)


def orthogonal(matrix, dtype):
    length, size = matrix.shape
    vmem = pl.BlockSpec(memory_space=pltpu.VMEM)
    return pl.pallas_call(
        orthogonal_kernel,
        out_shape=jax.ShapeDtypeStruct((length, size), dtype),
        in_specs=[vmem],
        out_specs=vmem,
        scratch_shapes=[
            pltpu.VMEM((size, length), bf16),
            pltpu.VMEM((size, length), bf16),
            pltpu.VMEM((size, size), bf16),
        ],
        compiler_params=pltpu.CompilerParams(vmem_limit_bytes=56 * 2**20),
        cost_estimate=pl.CostEstimate(
            flops=10 * size * size * (2 * length + size), bytes_accessed=6 * size * length, transcendentals=0
        ),
    )(matrix)


def body(
    resid_in,
    in_weight,
    out_weight,
    shared_weight,
    small_params,
    in_momentum,
    out_momentum,
    shared_momentum,
    small_first,
    small_second,
    resid_grad,
):
    tensor_index = lax.axis_index("tensor")
    tensor_count = lax.axis_size("tensor")
    local_cols = in_weight.shape[3]
    local_heads = HEADS // tensor_count
    col_start = tensor_index * local_cols
    head_start = tensor_index * local_heads
    shard_rows = in_weight.shape[1]
    own_tokens = resid_in.shape[0]
    length = own_tokens * tensor_count

    row_start = lax.axis_index("dp") * shard_rows
    channels = small_params[:, : (KERNEL + 2) * INNER].reshape(LAYERS, KERNEL + 2, INNER)
    channels = lax.dynamic_slice_in_dim(channels, col_start, local_cols, 2)
    states_at = (KERNEL + 2) * INNER
    heads_at = states_at + (KERNEL + 1) * 2 * STATE
    by_state = small_params[:, states_at:heads_at].reshape(LAYERS, KERNEL + 1, 2 * STATE)
    by_head = small_params[:, heads_at : heads_at + 3 * HEADS].reshape(LAYERS, 3, HEADS)
    by_head = lax.dynamic_slice_in_dim(by_head, head_start, local_heads, 2)
    in_gains = small_params[:, heads_at + 3 * HEADS :]
    skips = jnp.repeat(by_head[:, 2:], WIDTH, axis=2)
    px_all = jnp.concatenate([channels, skips, jnp.zeros((LAYERS, 1, local_cols), f32)], 1)
    ps_all = jnp.pad(by_state, ((0, 0), (0, 8 - KERNEL - 1), (0, 0)))
    ph_all = jnp.pad(by_head[:, :2], ((0, 0), (0, 6), (0, LANES - local_heads)))

    w_in, w_out = [], []
    for layer in range(LAYERS):
        shared_rows = lax.dynamic_slice_in_dim(shared_weight[layer], row_start, shard_rows, 0)
        steps_weight = lax.dynamic_slice_in_dim(shared_rows, 2 * STATE + head_start, local_heads, 1)
        w_rows = jnp.concatenate(
            [
                in_weight[layer, :, 0],
                in_weight[layer, :, 1],
                shared_rows[:, : 2 * STATE],
                jnp.pad(steps_weight, ((0, 0), (0, LANES - local_heads))),
            ],
            1,
        )
        w_in.append(w_rows)
        w_out.append(out_weight[layer])
    in_momentum_planes = jnp.transpose(in_momentum, (0, 2, 1, 3))

    residual = resid_in
    inverse_in = lax.rsqrt(jnp.mean(residual * residual, -1, keepdims=True) + epsilon)
    normed_low = (residual * inverse_in * in_gains[0]).astype(bf16)
    gathered, w_in[0], w_out[0] = gather_first(normed_low, w_in[0], w_out[0])
    held = lax.optimization_barrier((gathered, *w_in[1:], *w_out[1:]))
    gathered = held[0]
    for later in range(1, LAYERS):
        w_in[later] = lax.all_gather(held[later], "dp", axis=0, tiled=True)
        w_out[later] = lax.all_gather(held[LAYERS - 1 + later], "dp", axis=0, tiled=True)
    saved = []
    branches = [None] * LAYERS
    for layer in range(LAYERS):
        projected, total, partial, squares, states = mixer_forward(
            gathered, w_in[layer], w_out[layer], px_all[layer], ps_all[layer], ph_all[layer]
        )
        saved.append((residual, gathered, projected, total, states))
        squares = squares[:, 0, :].reshape(tensor_count, 1, own_tokens)
        squares = jnp.broadcast_to(squares, (tensor_count, 8, own_tokens))
        if layer < LAYERS - 1:
            residual, branch, scale, gathered = forward_pass(partial, squares, residual, in_gains[layer + 1])
            branches[layer] = (branch, scale)
    residual, d_rows, rd = last_scatter(partial, squares, resid_grad.astype(bf16), residual)

    grad_resid = resid_grad
    in_new = [None] * LAYERS
    out_new = [None] * LAYERS
    slots = [None] * LAYERS
    shared_shards = [None] * LAYERS
    small_grads = [None] * LAYERS
    for layer in reversed(range(LAYERS)):
        layer_in, gathered, projected, total, states = saved[layer]
        rd = jnp.transpose(rd[:, :2], (0, 2, 1)).reshape(length, 2)
        d_all, scaled_low, partial, grad_x, grad_s, grad_h = mixer_backward(
            d_rows, w_in[layer], w_out[layer], projected, total, states, rd, px_all[layer], ps_all[layer], ph_all[layer]
        )
        results = exchange(
            partial,
            gathered,
            d_all,
            d_rows,
            scaled_low,
            in_momentum_planes[layer],
            out_momentum[layer],
            layer_in,
            grad_resid,
            in_gains[layer],
            branches[layer - 1] if layer > 0 else None,
        )
        in_new[layer], out_new[layer], slots[layer], shared_shards[layer], grad_resid, d_in_gain = results[:6]
        if layer > 0:
            d_rows, rd = results[6:]
        small_grads[layer] = jnp.concatenate([grad_x, grad_s, grad_h, d_in_gain.reshape(8, D // 8)], 1)

    in_momentum_new = jnp.transpose(jnp.stack(in_new), (0, 2, 1, 3))
    out_momentum_new = jnp.stack(out_new)
    block_count = 3 * LAYERS
    dp_count = lax.axis_size("dp")
    shared_total, vectors, turned = finish_blocks(
        jnp.concatenate(shared_shards, 0), jnp.concatenate(small_grads, 1), jnp.concatenate(slots, 0)
    )
    turned = turned.reshape(dp_count, shard_rows, local_cols)
    returned = lax.all_to_all(turned, "dp", split_axis=0, concat_axis=0, tiled=True)[:block_count]
    scale = muon_rate * (D / local_cols) ** 0.5
    updates = returned.astype(f32).reshape(LAYERS, 3, shard_rows, local_cols) * scale
    in_weight_new = in_weight.astype(f32) - jnp.transpose(updates[:, :2], (0, 2, 1, 3))
    out_weight_new = out_weight.astype(f32) - updates[:, 2]

    share = SHARED_COLS // dp_count
    shared_total = shared_total.reshape(dp_count, LAYERS, share, D)
    shared_total = jnp.transpose(shared_total, (1, 0, 2, 3)).reshape(LAYERS, SHARED_COLS, D)[:, :SSM_COLS]
    turned_momentum = muon_decay * jnp.transpose(shared_momentum, (0, 2, 1)) + shared_total.astype(f32)
    shared_momentum_new = jnp.transpose(turned_momentum, (0, 2, 1))
    shared_weight_new = jnp.transpose(
        shared_step(turned_momentum, jnp.transpose(shared_weight, (0, 2, 1))), (0, 2, 1)
    )
    small_rows = []
    for layer in range(LAYERS):
        width = local_cols + 2 * STATE + LANES + D // 8
        mine = vectors[:, :, layer * width : (layer + 1) * width]
        channel_grads = jnp.transpose(mine[:, :7, :local_cols], (1, 0, 2)).reshape(7, INNER)
        head_grads = jnp.transpose(mine[:, :2, local_cols + 2 * STATE :][:, :, :local_heads], (1, 0, 2))
        common = jnp.sum(mine, 0)
        state_grads = common[: KERNEL + 1, local_cols : local_cols + 2 * STATE]
        small_rows.append(
            jnp.concatenate(
                [
                    channel_grads[: KERNEL + 2].reshape(-1),
                    state_grads.reshape(-1),
                    head_grads.reshape(-1),
                    channel_grads[6].reshape(HEADS, WIDTH).sum(1),
                    common[:, local_cols + 2 * STATE + LANES :].reshape(-1),
                ]
            )
        )
    small_grad = jnp.stack(small_rows)
    first_new = beta_first * small_first + (1.0 - beta_first) * small_grad
    small_second_new = beta_second * small_second + (1.0 - beta_second) * small_grad * small_grad
    small_new = small_params - adam_rate * (first_new / (1.0 - beta_first**STEP)) / (
        jnp.sqrt(small_second_new / (1.0 - beta_second**STEP)) + 1e-08
    )
    return (
        residual,
        grad_resid,
        small_grad,
        small_second_new,
        small_new,
        in_momentum_new,
        in_weight_new,
        out_momentum_new,
        out_weight_new,
        shared_momentum_new,
        shared_weight_new,
    )


def solution(mesh):
    placed = (
        P(("dp", "tensor"), None),
        P(None, "dp", None, "tensor"),
        P(None, "dp", "tensor"),
        P(),
        P(),
        P(None, "dp", None, "tensor"),
        P(None, "dp", "tensor"),
        P(),
        P(),
        P(),
        P(("dp", "tensor"), None),
    )
    return jax.shard_map(
        body,
        mesh=mesh,
        in_specs=placed,
        out_specs=(
            P(("dp", "tensor"), None),
            P(("dp", "tensor"), None),
            P(),
            P(),
            P(),
            P(None, "dp", None, "tensor"),
            P(None, "dp", None, "tensor"),
            P(None, "dp", "tensor"),
            P(None, "dp", "tensor"),
            P(),
            P(),
        ),
        check_vma=False,
    )
```

```python
import functools

import jax
import jax.numpy as jnp
from jax import lax
from jax.experimental import pallas as pl
from jax.experimental.pallas import tpu as pltpu
from jax.sharding import PartitionSpec as P

D = 1536
INNER = 3072
HEADS = 48
STATE = 128
KERNEL = 4
SPAN = 256
LAYERS = 2
STEP = 10
SSM_COLS = 304
WIDTH = INNER // HEADS
LANES = 128
SHARED_COLS = 2 * STATE + LANES
HALO = 8

epsilon = 1e-05
highest = lax.Precision.HIGHEST
coef_first = 3.4445
coef_second = -4.775
coef_third = 2.0315
muon_decay = 0.95
muon_rate = 0.2
beta_first = 0.9
beta_second = 0.95
adam_rate = 0.2

MESH = pl.DeviceIdType.MESH
NN = (((1,), (0,)), ((), ()))
NT = (((1,), (1,)), ((), ()))
TN = (((0,), (0,)), ((), ()))
f32 = jnp.float32
bf16 = jnp.bfloat16


def dot(left, right, dims=NN):
    return lax.dot_general(left, right, dims, preferred_element_type=f32)


def dot_exact(left, right, dims=NN):
    return lax.dot_general(left, right, dims, precision=highest, preferred_element_type=f32)


def sigmoid(v):
    return 0.5 * jnp.tanh(0.5 * v) + 0.5


def softplus(v):
    small = jnp.exp(-jnp.abs(v))
    series = small * (1.0 - small * (0.5 - small * (1.0 / 3.0 - small * 0.25)))
    return jnp.maximum(v, 0.0) + jnp.where(small < 0.01, series, jnp.log(1.0 + small))


def steps_of(raw_in, ph_ref):
    raw = raw_in + ph_ref[1:2, :]
    timestep = softplus(raw)
    decay = -jnp.exp(ph_ref[0:1, :])
    log_decay = timestep * decay
    rows = lax.broadcasted_iota(jnp.int32, (SPAN, SPAN), 0)
    cols = lax.broadcasted_iota(jnp.int32, (SPAN, SPAN), 1)
    lower = jnp.where(rows >= cols, 1.0, 0.0).astype(f32)
    cumulative = dot_exact(lower, log_decay)
    return raw, timestep, decay, log_decay, cumulative, lower


def spread_heads(table, columns):
    high = table.astype(bf16)
    low = (table - high.astype(f32)).astype(bf16)
    head = lax.rem(lax.broadcasted_iota(jnp.int32, (2 * LANES, columns), 0), LANES)
    owned = head == lax.broadcasted_iota(jnp.int32, (2 * LANES, columns), 1) // WIDTH
    return dot(jnp.concatenate([high, low], 1), jnp.where(owned, 1.0, 0.0).astype(bf16))


def conv_of(pad, lanes, weights, first):
    total = weights[4:5, lanes] + weights[0:1, lanes] * pad[first : first + SPAN, lanes]
    for tap in range(1, KERNEL):
        total = total + weights[tap : tap + 1, lanes] * pad[first + tap : first + tap + SPAN, lanes]
    return total


def head_sums(values, owner):
    high = values.astype(bf16)
    low = (values - high.astype(f32)).astype(bf16)
    return dot(jnp.concatenate([high, low], 1), owner)


def matmul_into(target, left, right, dims, width, piece, first=0):
    for at in range(first, width, piece):
        cols = slice(at, min(at + piece, width))
        mine = right[:, cols] if dims == NN else right[cols, :]
        target[:, cols] = dot(left, mine, dims).astype(target.dtype)


def forward_kernel(
    g_ref, w_ref, wo_ref, px_ref, ps_ref, ph_ref, proj_ref, yt_ref, p_ref, sq_ref, st_ref, state, xpad, spad, gained
):
    step = pl.program_id(0)
    spans = pl.num_programs(0) - 1
    columns = yt_ref.shape[1]
    here, there = lax.rem(step, 2), lax.rem(step + 1, 2)

    @pl.when(step == 0)
    def _():
        state[...] = jnp.zeros_like(state)
        xpad[0:HALO, :] = jnp.zeros((HALO, columns), f32)
        spad[0:HALO, :] = jnp.zeros((HALO, 2 * STATE), f32)
        gained[there] = jnp.zeros((SPAN, columns), bf16)

    @pl.when(step > 0)
    def _():
        xpad[0:HALO, :] = xpad[SPAN : SPAN + HALO, :]
        spad[0:HALO, :] = spad[SPAN : SPAN + HALO, :]

    @pl.when(step < spans)
    def _():
        forward_span(
            g_ref, w_ref, wo_ref, px_ref, ps_ref, ph_ref, proj_ref, yt_ref, p_ref, sq_ref, st_ref, state, xpad, spad, gained, here, there
        )

    @pl.when(step == spans)
    def _():
        matmul_into(p_ref, gained[there], wo_ref, NT, D, 2 * LANES)


def forward_span(
    g_ref, w_ref, wo_ref, px_ref, ps_ref, ph_ref, proj_ref, yt_ref, p_ref, sq_ref, st_ref, state, xpad, spad, gained, here, there
):
    columns = yt_ref.shape[1]
    pairs = columns // LANES
    matmul_into(proj_ref, g_ref[...], w_ref, NN, 2 * columns + SHARED_COLS, 2 * LANES)
    xpad[HALO:, :] = proj_ref[:, columns : 2 * columns]
    spad[HALO:, :] = proj_ref[:, 2 * columns : 2 * columns + 2 * STATE]
    first = HALO - KERNEL + 1
    pre_s = conv_of(spad, slice(None), ps_ref, first)
    bc = pre_s * sigmoid(pre_s)
    b_low, c_low = bc[:, :STATE].astype(bf16), bc[:, STATE:].astype(bf16)
    raw, timestep, decay, log_decay, cumulative, lower = steps_of(proj_ref[:, 2 * columns + 2 * STATE :], ph_ref)
    turned = cumulative.T
    grown = jnp.exp(cumulative)
    tail = jnp.exp(cumulative[SPAN - 1 : SPAN, :] - cumulative)
    scores = dot(c_low, b_low, NT) * lower
    wide_step, wide_grown, wide_tail = (spread_heads(each, columns) for each in (timestep, grown, tail))
    low_half = lax.broadcasted_iota(jnp.int32, (SPAN, LANES), 1) < WIDTH
    squares = jnp.zeros((SPAN, LANES), f32)
    half = SPAN // 2
    for pair in range(pairs):
        matmul_into(p_ref, gained[there], wo_ref, NT, (pair + 1) * D // pairs, 2 * LANES, pair * D // pairs)
        lanes = slice(pair * LANES, (pair + 1) * LANES)
        pre = conv_of(xpad, lanes, px_ref, first)
        xc = pre * sigmoid(pre)
        u = xc * wide_step[:, lanes]
        u_low = u.astype(bf16)
        mine = [jnp.where(low_half == (side == 0), u_low, jnp.zeros_like(u_low)) for side in range(2)]
        inside = []
        for rows, count in ((slice(0, half), half), (slice(half, SPAN), SPAN)):
            mixing = []
            for side in range(2):
                head = 2 * pair + side
                spread = cumulative[rows, head : head + 1] - turned[head : head + 1, :count]
                mixing.append((scores[rows, :count] * jnp.exp(jnp.minimum(spread, 0.0))).astype(bf16))
            inside.append(dot(jnp.concatenate(mixing, 1), jnp.concatenate([mine[0][:count], mine[1][:count]], 0)))
        held = state[:, lanes]
        held_low = held.astype(bf16)
        st_ref[0, :, lanes] = held_low
        grown_pair = wide_grown[:, lanes]
        carried = dot(c_low, held_low) * grown_pair
        tail_u = (wide_tail[:, lanes] * u).astype(bf16)
        state[:, lanes] = grown_pair[SPAN - 1 : SPAN, :] * held + dot(b_low, tail_u, TN)
        total = jnp.concatenate(inside, 0) + carried + px_ref[6:7, lanes] * xc
        yt_ref[:, lanes] = total
        gate = proj_ref[:, lanes]
        mixed = total * gate * sigmoid(gate)
        gained[here, :, lanes] = (mixed * px_ref[5:6, lanes]).astype(bf16)
        squares = squares + mixed * mixed
    sq_ref[0] = dot_exact(jnp.ones((8, LANES), f32), squares, NT)


def backward_kernel(
    dr_ref,
    w_ref,
    wo_ref,
    gate_ref,
    x_ref,
    xh_ref,
    sh_ref,
    shh_ref,
    yt_ref,
    st_ref,
    rd_ref,
    px_ref,
    ps_ref,
    ph_ref,
    dall_ref,
    scaled_ref,
    p_ref,
    gx_ref,
    gs_ref,
    gh_ref,
    dstate,
    xpad,
    spad,
    dxpad,
    dspad,
    dsc,
    held_all,
):
    step = pl.program_id(0)
    steps = pl.num_programs(0) - 1
    columns = x_ref.shape[1]
    here, there = lax.rem(step, 2), lax.rem(step + 1, 2)

    @pl.when(step == 0)
    def _():
        dstate[...] = jnp.zeros_like(dstate)
        dxpad[SPAN:, :] = jnp.zeros((HALO, columns), f32)
        dspad[SPAN:, :] = jnp.zeros((HALO, 2 * STATE), f32)
        gx_ref[...] = jnp.zeros_like(gx_ref)
        gs_ref[...] = jnp.zeros_like(gs_ref)
        gh_ref[...] = jnp.zeros_like(gh_ref)
        held_all[there] = jnp.zeros(dall_ref.shape, bf16)

    @pl.when(step > 0)
    def _():
        dxpad[SPAN:, :] = dxpad[0:HALO, :]
        dspad[SPAN:, :] = dspad[0:HALO, :]

    @pl.when(step < steps)
    def _():
        backward_span(
            dr_ref,
            w_ref,
            wo_ref,
            gate_ref,
            x_ref,
            xh_ref,
            sh_ref,
            shh_ref,
            yt_ref,
            st_ref,
            rd_ref,
            px_ref,
            ps_ref,
            ph_ref,
            dall_ref,
            scaled_ref,
            p_ref,
            gx_ref,
            gs_ref,
            gh_ref,
            dstate,
            xpad,
            spad,
            dxpad,
            dspad,
            dsc,
            held_all,
            step,
            steps,
            here,
            there,
        )

    @pl.when(step == steps)
    def _():
        matmul_into(p_ref, held_all[there], w_ref, NT, D, 2 * LANES)


def backward_span(
    dr_ref,
    w_ref,
    wo_ref,
    gate_ref,
    x_ref,
    xh_ref,
    sh_ref,
    shh_ref,
    yt_ref,
    st_ref,
    rd_ref,
    px_ref,
    ps_ref,
    ph_ref,
    dall_ref,
    scaled_ref,
    p_ref,
    gx_ref,
    gs_ref,
    gh_ref,
    dstate,
    xpad,
    spad,
    dxpad,
    dspad,
    dsc,
    held_all,
    step,
    steps,
    here,
    there,
):
    columns = x_ref.shape[1]
    pairs = columns // LANES
    matmul_into(dsc, dr_ref[...], wo_ref, NN, columns, 2 * LANES)
    before = jnp.where(step < steps - 1, 1.0, 0.0).astype(f32)
    xpad[0:HALO, :] = xh_ref[...] * before
    spad[0:HALO, :] = shh_ref[:, : 2 * STATE] * before
    xpad[HALO:, :] = x_ref[...]
    spad[HALO:, :] = sh_ref[:, : 2 * STATE]
    first = HALO - KERNEL + 1
    pre_s = conv_of(spad, slice(None), ps_ref, first)
    sig_s = sigmoid(pre_s)
    bc = pre_s * sig_s
    b_low, c_low = bc[:, :STATE].astype(bf16), bc[:, STATE:].astype(bf16)
    raw, timestep, decay, log_decay, cumulative, lower = steps_of(sh_ref[:, 2 * STATE :], ph_ref)
    turned = cumulative.T
    grown = jnp.exp(cumulative)
    tail = jnp.exp(cumulative[SPAN - 1 : SPAN, :] - cumulative)
    upper = lower.T
    scores = dot(b_low, c_low, NT) * upper
    wide_step, wide_grown, wide_tail = (spread_heads(each, columns) for each in (timestep, grown, tail))
    low_half = lax.broadcasted_iota(jnp.int32, (SPAN, LANES), 1) < WIDTH
    inverse = rd_ref[:, 0:1]
    dots = rd_ref[:, 1:2] * (1.0 / INNER)
    head_row = lax.rem(lax.broadcasted_iota(jnp.int32, (2 * LANES, LANES), 0), LANES) // WIDTH
    head_col = lax.broadcasted_iota(jnp.int32, (2 * LANES, LANES), 1)

    half = SPAN // 2
    d_scores = [jnp.zeros((half, SPAN), f32), jnp.zeros((half, half), f32)]
    d_b = jnp.zeros((SPAN, STATE), f32)
    d_c = jnp.zeros((SPAN, STATE), f32)
    d_cum = jnp.zeros((SPAN, LANES), f32)
    d_step = jnp.zeros((SPAN, LANES), f32)
    d_last = jnp.zeros((8, LANES), f32)
    for pair in range(pairs):
        matmul_into(p_ref, held_all[there], w_ref, NT, (pair + 1) * D // pairs, 2 * LANES, pair * D // pairs)
        lanes = slice(pair * LANES, (pair + 1) * LANES)
        owner = jnp.where(head_row + 2 * pair == head_col, 1.0, 0.0).astype(bf16)
        pre = conv_of(xpad, lanes, px_ref, first)
        sig = sigmoid(pre)
        xc = pre * sig
        step_pair = wide_step[:, lanes]
        u = xc * step_pair
        u_low = u.astype(bf16)
        gate = gate_ref[:, lanes]
        sig_gate = sigmoid(gate)
        silu = gate * sig_gate
        total = yt_ref[:, lanes]
        gain = px_ref[5:6, lanes]
        sn = total * silu * inverse
        scaled_ref[:, lanes] = (sn * gain).astype(bf16)
        d_scaled = dsc[:, lanes]
        gx_ref[5:6, lanes] += jnp.sum(d_scaled * sn, 0, keepdims=True)
        d_mixed = inverse * (d_scaled * gain - sn * dots)
        held_all[here, :, lanes] = (
            d_mixed * total * (sig_gate * (1.0 + gate * (1.0 - sig_gate)))
        ).astype(bf16)
        dy = d_mixed * silu
        skip = px_ref[6:7, lanes]
        gx_ref[6:7, lanes] += jnp.sum(dy * xc, 0, keepdims=True)
        dy_low = dy.astype(bf16)
        mine = [jnp.where(low_half == (side == 0), dy_low, jnp.zeros_like(dy_low)) for side in range(2)]
        du = []
        for block, start in ((0, 0), (1, half)):
            rows = slice(start, start + half)
            mixing = []
            for side in range(2):
                head = 2 * pair + side
                spread = turned[head : head + 1, start:] - cumulative[rows, head : head + 1]
                mask = jnp.exp(jnp.minimum(spread, 0.0))
                mixing.append((scores[rows, start:] * mask).astype(bf16))
                d_scores[block] = d_scores[block] + dot(u_low[rows], mine[side][start:], NT) * mask
            du.append(dot(jnp.concatenate(mixing, 1), jnp.concatenate([mine[0][start:], mine[1][start:]], 0)))
        held_low = st_ref[0, :, lanes]
        grown_pair = wide_grown[:, lanes]
        last_pair = grown_pair[SPAN - 1 : SPAN, :]
        d_after = dstate[:, lanes]
        d_after_low = d_after.astype(bf16)
        grown_dy = (grown_pair * dy).astype(bf16)
        d_c = d_c + dot(grown_dy, held_low, NT)
        tail_pair = wide_tail[:, lanes]
        du_tail = tail_pair * dot(b_low, d_after_low)
        d_b = d_b + dot((tail_pair * u).astype(bf16), d_after_low, NT)
        dstate[:, lanes] = last_pair * d_after + dot(c_low, grown_dy, TN)
        du = jnp.concatenate(du, 0) + du_tail
        u_round = u_low.astype(f32)
        y = total - skip * xc
        d_cum = d_cum + head_sums(dy_low.astype(f32) * y - u_round * du, owner)
        d_step = d_step + head_sums(xc * du, owner)
        ends = jnp.sum(u_round * du_tail, 0, keepdims=True) + last_pair * jnp.sum(
            d_after * held_low.astype(f32), 0, keepdims=True
        )
        d_last = d_last + head_sums(jnp.broadcast_to(ends, (8, LANES)), owner)
        d_pre = (skip * dy + step_pair * du) * (sig * (1.0 + pre * (1.0 - sig)))
        dxpad[0:SPAN, lanes] = d_pre
        d_x = px_ref[KERNEL - 1 : KERNEL, lanes] * d_pre
        gx_ref[4:5, lanes] += jnp.sum(d_pre, 0, keepdims=True)
        for tap in range(KERNEL):
            gx_ref[tap : tap + 1, lanes] += jnp.sum(
                d_pre * xpad[first + tap : first + tap + SPAN, lanes], 0, keepdims=True
            )
            if tap < KERNEL - 1:
                ahead = KERNEL - 1 - tap
                d_x = d_x + px_ref[tap : tap + 1, lanes] * dxpad[ahead : ahead + SPAN, lanes]
        held_all[here, :, columns + pair * LANES : columns + (pair + 1) * LANES] = d_x.astype(bf16)
    d_log = dot_exact(upper, d_cum) + d_last[0:1, :]
    d_raw = (d_step + d_log * decay) * sigmoid(raw)
    gh_ref[0:1, :] += jnp.sum(d_log * log_decay, 0, keepdims=True)
    gh_ref[1:2, :] += jnp.sum(d_raw, 0, keepdims=True)
    d_scores = jnp.concatenate(
        [d_scores[0], jnp.concatenate([jnp.zeros((half, half), f32), d_scores[1]], 1)], 0
    )
    d_scores_low = (d_scores * upper).astype(bf16)
    d_b = d_b + dot(d_scores_low, c_low)
    d_c = d_c + dot(d_scores_low, b_low, TN)
    slope_s = sig_s * (1.0 + pre_s * (1.0 - sig_s))
    d_pre_s = jnp.concatenate([d_b, d_c], 1) * slope_s
    dspad[0:SPAN, :] = d_pre_s
    d_s = ps_ref[KERNEL - 1 : KERNEL, :] * d_pre_s
    gs_ref[4:5, :] += jnp.sum(d_pre_s, 0, keepdims=True)
    for tap in range(KERNEL):
        gs_ref[tap : tap + 1, :] += jnp.sum(
            d_pre_s * spad[first + tap : first + tap + SPAN, :], 0, keepdims=True
        )
        if tap < KERNEL - 1:
            ahead = KERNEL - 1 - tap
            d_s = d_s + ps_ref[tap : tap + 1, :] * dspad[ahead : ahead + SPAN, :]
    held_all[here, :, 2 * columns : 2 * columns + 2 * STATE] = d_s.astype(bf16)
    held_all[here, :, 2 * columns + 2 * STATE :] = d_raw.astype(bf16)
    dall_ref[...] = held_all[here]


def resident(shape):
    return pl.BlockSpec(shape, lambda i: (0, 0), pipeline_mode=pl.Buffered(1))


def mixer_forward(gathered, w_in, w_out, px, ps, ph):
    length, columns = gathered.shape[0], px.shape[1]
    spans = length // SPAN
    width = 2 * columns + SHARED_COLS
    at = lambda i: jnp.minimum(i, spans - 1)
    here = lambda i: (at(i), 0)
    return pl.pallas_call(
        forward_kernel,
        grid=(spans + 1,),
        in_specs=[
            pl.BlockSpec((SPAN, D), here),
            resident((D, width)),
            resident((D, columns)),
            resident((8, columns)),
            resident((8, 2 * STATE)),
            resident((8, LANES)),
        ],
        out_specs=[
            pl.BlockSpec((SPAN, width), here),
            pl.BlockSpec((SPAN, columns), here),
            pl.BlockSpec((SPAN, D), lambda i: (jnp.maximum(i - 1, 0), 0)),
            pl.BlockSpec((1, 8, SPAN), lambda i: (at(i), 0, 0)),
            pl.BlockSpec((1, STATE, columns), lambda i: (at(i), 0, 0)),
        ],
        out_shape=[
            jax.ShapeDtypeStruct((length, width), f32),
            jax.ShapeDtypeStruct((length, columns), f32),
            jax.ShapeDtypeStruct((length, D), bf16),
            jax.ShapeDtypeStruct((spans, 8, SPAN), f32),
            jax.ShapeDtypeStruct((spans, STATE, columns), bf16),
        ],
        scratch_shapes=[
            pltpu.VMEM((STATE, columns), f32),
            pltpu.VMEM((SPAN + HALO, columns), f32),
            pltpu.VMEM((SPAN + HALO, 2 * STATE), f32),
            pltpu.VMEM((2, SPAN, columns), bf16),
        ],
        compiler_params=pltpu.CompilerParams(vmem_limit_bytes=56 * 2**20),
        cost_estimate=pl.CostEstimate(flops=10 * 10**9, bytes_accessed=32 * 2**20, transcendentals=0),
    )(gathered, w_in, w_out, px, ps, ph)


def mixer_backward(d_rows, w_in, w_out, projected, total, states, rd, px, ps, ph):
    length, columns = total.shape
    spans = length // SPAN
    width = 2 * columns + SHARED_COLS
    at = lambda i: jnp.maximum(spans - 1 - i, 0)
    here = lambda i: (at(i), 0)
    blocks = SPAN // HALO
    halo = lambda i: jnp.maximum(at(i) * blocks - 1, 0)
    tail_block = 2 * columns // SHARED_COLS
    return pl.pallas_call(
        backward_kernel,
        grid=(spans + 1,),
        in_specs=[
            pl.BlockSpec((SPAN, D), here),
            resident((D, width)),
            resident((D, columns)),
            pl.BlockSpec((SPAN, columns), here),
            pl.BlockSpec((SPAN, columns), lambda i: (at(i), 1)),
            pl.BlockSpec((HALO, columns), lambda i: (halo(i), 1)),
            pl.BlockSpec((SPAN, SHARED_COLS), lambda i: (at(i), tail_block)),
            pl.BlockSpec((HALO, SHARED_COLS), lambda i: (halo(i), tail_block)),
            pl.BlockSpec((SPAN, columns), here),
            pl.BlockSpec((1, STATE, columns), lambda i: (at(i), 0, 0)),
            pl.BlockSpec((SPAN, 2), here),
            resident((8, columns)),
            resident((8, 2 * STATE)),
            resident((8, LANES)),
        ],
        out_specs=[
            pl.BlockSpec((SPAN, width), here),
            pl.BlockSpec((SPAN, columns), here),
            pl.BlockSpec((SPAN, D), lambda i: (jnp.minimum(spans - i, spans - 1), 0)),
            pl.BlockSpec((8, columns), lambda i: (0, 0)),
            pl.BlockSpec((8, 2 * STATE), lambda i: (0, 0)),
            pl.BlockSpec((8, LANES), lambda i: (0, 0)),
        ],
        out_shape=[
            jax.ShapeDtypeStruct((length, width), bf16),
            jax.ShapeDtypeStruct((length, columns), bf16),
            jax.ShapeDtypeStruct((length, D), bf16),
            jax.ShapeDtypeStruct((8, columns), f32),
            jax.ShapeDtypeStruct((8, 2 * STATE), f32),
            jax.ShapeDtypeStruct((8, LANES), f32),
        ],
        scratch_shapes=[
            pltpu.VMEM((STATE, columns), f32),
            pltpu.VMEM((SPAN + HALO, columns), f32),
            pltpu.VMEM((SPAN + HALO, 2 * STATE), f32),
            pltpu.VMEM((SPAN + HALO, columns), f32),
            pltpu.VMEM((SPAN + HALO, 2 * STATE), f32),
            pltpu.VMEM((SPAN, columns), f32),
            pltpu.VMEM((2, SPAN, width), bf16),
        ],
        compiler_params=pltpu.CompilerParams(vmem_limit_bytes=56 * 2**20),
        cost_estimate=pl.CostEstimate(flops=16 * 10**9, bytes_accessed=48 * 2**20, transcendentals=0),
    )(
        d_rows,
        w_in,
        w_out,
        projected,
        projected,
        projected,
        projected,
        projected,
        total,
        states,
        rd,
        px,
        ps,
        ph,
    )


def kernels_fit():
    return lax.axis_size("tensor") == 4 and lax.axis_size("dp") == 8


def neighbours():
    index = lax.axis_index("dp")
    core = lax.rem(index, 2)
    across = lax.rem(lax.div(index, 2), 2)
    along = lax.div(index, 4)
    return index, core, index + 1 - 2 * core, index + 2 - 4 * across, index + 4 - 8 * along


def greet(others):
    barrier = pltpu.get_barrier_semaphore()
    for other in others:
        pl.semaphore_signal(barrier, inc=1, device_id=other, device_id_type=MESH)
    pl.semaphore_wait(barrier, len(others))


def remote(source, target, send_sem, recv_sem, slot, where):
    return pltpu.make_async_remote_copy(
        src_ref=source,
        dst_ref=target,
        send_sem=send_sem.at[slot],
        recv_sem=recv_sem.at[slot],
        device_id=where,
        device_id_type=MESH,
    )


class Line:
    def __init__(self, side):
        me = lax.axis_index("tensor")
        self.side = side
        self.me = me
        self.pos = me if side == 0 else 3 - me
        self.next = {"tensor": lax.rem(me + (1 if side == 0 else 3), 4)}

    def chunk(self, ahead):
        return self.me + ahead if self.side == 0 else self.me - ahead


def rows_at(ref, chunk, count):
    return ref.at[pl.ds(pl.multiple_of(chunk * count, count), count), :]


class LineCopy:
    def __init__(self, lines, source, place, local_sem, send_sem, recv_sem):
        self.lines, self.source, self.place = lines, source, place
        self.send_sem, self.recv_sem = send_sem, recv_sem
        self.own = pltpu.make_async_copy(source, place(lines[0].me), local_sem)

    def outgoing(self, line, time):
        place = self.place(line.chunk(-time))
        source = self.source if time == 0 else place
        return remote(source, place, self.send_sem, self.recv_sem, 3 * line.side + time, line.next)

    def start(self):
        for line in self.lines:

            @pl.when(line.pos < 3)
            def _(line=line):
                self.outgoing(line, 0).start()

        self.own.start()

    def step(self, time):
        for line in self.lines:

            @pl.when(line.pos >= time)
            def _(line=line):
                place = self.place(line.chunk(-time))
                slot = 3 * line.side + time - 1
                remote(place, place, self.send_sem, self.recv_sem, slot, line.next).wait_recv()

            if time < 3:

                @pl.when(jnp.logical_and(line.pos >= time, line.pos < 3))
                def _(line=line):
                    self.outgoing(line, time).start()

    def finish(self):
        for time in range(3):
            for line in self.lines:

                @pl.when(jnp.logical_and(line.pos >= time, line.pos < 3))
                def _(line=line):
                    self.outgoing(line, time).wait_send()

        self.own.wait()


class SquareCopy:
    def __init__(self, source, result, local_sem, send_sem, recv_sem):
        self.source, self.result = source, result
        self.send_sem, self.recv_sem = send_sem, recv_sem
        self.rows = source.shape[0]
        self.split = near_rows(self.rows)
        self.index, core, self.sibling, self.by_x, self.by_y = neighbours()
        self.own = pltpu.make_async_copy(source, self.place(self.index, None), local_sem)

    def place(self, owner, side):
        start, count = {None: (0, self.rows), 0: (0, self.split), 1: (self.split, self.rows - self.split)}[side]
        return self.result.at[pl.ds(pl.multiple_of(owner * self.rows + start, 16), count), :]

    def copy(self, slot):
        near, far = self.source.at[pl.ds(0, self.split), :], self.source.at[pl.ds(self.split, self.rows - self.split), :]
        by_x, by_y = self.by_x, self.by_y
        source, owner, side, where = {
            0: (near, self.index, 0, by_x),
            1: (far, self.index, 1, by_y),
            2: (far, self.index, 1, by_x),
            3: (near, self.index, 0, by_y),
            4: (None, by_x, 0, by_y),
            5: (None, by_y, 1, by_x),
            6: (self.source, self.index, None, self.sibling),
            7: (None, by_x, None, self.sibling),
            8: (None, by_y, None, self.sibling),
            9: (None, by_x + by_y - self.index, None, self.sibling),
        }[slot]
        target = self.place(owner, side)
        return remote(target if source is None else source, target, self.send_sem, self.recv_sem, slot, {"dp": where})

    def start(self):
        for slot in (0, 1, 2, 3, 6):
            self.copy(slot).start()
        self.own.start()

    def relay(self):
        self.copy(0).wait_recv()
        self.copy(4).start()
        self.copy(1).wait_recv()
        self.copy(5).start()

    def forward(self):
        self.copy(2).wait_recv()
        self.copy(7).start()
        self.copy(3).wait_recv()
        self.copy(8).start()

    def last(self):
        self.copy(4).wait_recv()
        self.copy(5).wait_recv()
        self.copy(9).start()

    def finish(self):
        for slot in range(6, 10):
            self.copy(slot).wait_recv()
        for slot in range(10):
            self.copy(slot).wait_send()
        self.own.wait()


def first_kernel(x_ref, w_ref, v_ref, ox_ref, ow_ref, ov_ref, *sems):
    lines = (Line(0), Line(1))
    rows = x_ref.shape[0]
    me = lax.axis_index("tensor")
    index, core, sibling, by_x, by_y = neighbours()
    greet([{"tensor": lax.rem(me + 1, 4)}, {"tensor": lax.rem(me + 3, 4)}, {"dp": sibling}, {"dp": by_x}, {"dp": by_y}])
    tokens = LineCopy(lines, x_ref, lambda chunk: rows_at(ox_ref, chunk, rows), *sems[:3])
    weights = [SquareCopy(w_ref, ow_ref, *sems[3:6]), SquareCopy(v_ref, ov_ref, *sems[6:])]
    tokens.start()
    for each in weights:
        each.start()
    for each in weights:
        each.relay()
    tokens.step(1)
    for each in weights:
        each.forward()
    tokens.step(2)
    for each in weights:
        each.last()
    tokens.step(3)
    for each in weights:
        each.finish()
    tokens.finish()


def gather_first(rows, w_rows, v_rows):
    if not kernels_fit():
        return (
            lax.all_gather(rows, "tensor", axis=0, tiled=True),
            lax.all_gather(w_rows, "dp", axis=0, tiled=True),
            lax.all_gather(v_rows, "dp", axis=0, tiled=True),
        )
    anywhere = pl.BlockSpec(memory_space=pl.ANY)
    larger = lambda v, times: jax.ShapeDtypeStruct((times * v.shape[0], v.shape[1]), v.dtype)
    sems = lambda count: [
        pltpu.SemaphoreType.DMA,
        pltpu.SemaphoreType.DMA((count,)),
        pltpu.SemaphoreType.DMA((count,)),
    ]
    return pl.pallas_call(
        first_kernel,
        out_shape=(larger(rows, 4), larger(w_rows, 8), larger(v_rows, 8)),
        in_specs=[anywhere] * 3,
        out_specs=(anywhere,) * 3,
        scratch_shapes=[*sems(6), *sems(10), *sems(10)],
        compiler_params=pltpu.CompilerParams(collective_id=6, has_side_effects=True),
        cost_estimate=pl.CostEstimate(flops=0, bytes_accessed=150 * 2**20, transcendentals=0),
    )(rows, w_rows, v_rows)


def gather_tokens(rows, small):
    if not kernels_fit():
        return lax.all_gather(rows, "tensor", axis=0, tiled=True), lax.all_gather(small, "tensor", axis=0)
    count, columns = rows.shape
    vmem = pl.BlockSpec(memory_space=pltpu.VMEM)
    anywhere = pl.BlockSpec(memory_space=pl.ANY)
    return pl.pallas_call(
        gather_kernel,
        out_shape=(
            jax.ShapeDtypeStruct((4 * count, columns), rows.dtype),
            jax.ShapeDtypeStruct((4, *small.shape), small.dtype),
        ),
        in_specs=[anywhere, vmem],
        out_specs=(anywhere, vmem),
        scratch_shapes=[
            pltpu.SemaphoreType.DMA,
            pltpu.SemaphoreType.DMA,
            pltpu.SemaphoreType.DMA((6,)),
            pltpu.SemaphoreType.DMA((6,)),
            pltpu.SemaphoreType.DMA((6,)),
            pltpu.SemaphoreType.DMA((6,)),
        ],
        compiler_params=pltpu.CompilerParams(collective_id=0, has_side_effects=True),
        cost_estimate=pl.CostEstimate(flops=0, bytes_accessed=150 * 2**20, transcendentals=0),
    )(rows, small)


class LineSum:
    def __init__(self, lines, p_ref, o_ref, came, send_sem, recv_sem, first_row=0):
        self.lines, self.p_ref, self.o_ref, self.came = lines, p_ref, o_ref, came
        self.send_sem, self.recv_sem = send_sem, recv_sem
        self.first_row, self.count = first_row, came.shape[1]
        self.rows = p_ref.shape[0] // 4

    def part(self, chunk):
        start = pl.multiple_of(chunk * self.rows + self.first_row, self.count)
        return self.p_ref.at[pl.ds(start, self.count), :]

    def copy(self, line, time, first):
        slot = 3 * line.side + time
        target = self.came.at[slot]
        source = self.part(line.chunk(3 - time)) if first else self.came.at[slot - 1]
        return remote(source, target, self.send_sem, self.recv_sem, slot, line.next)

    def start(self, times=(0, 1, 2)):
        for line in self.lines:

            @pl.when(line.pos == 0)
            def _(line=line):
                for time in times:
                    self.copy(line, time, True).start()

    def step(self, time):
        for line in self.lines:

            @pl.when(jnp.logical_and(line.pos > 0, line.pos <= time))
            def _(line=line):
                slot = 3 * line.side + time - 1
                place = self.came.at[slot]
                remote(place, place, self.send_sem, self.recv_sem, slot, line.next).wait_recv()

            if time < 3:

                @pl.when(jnp.logical_and(line.pos > 0, line.pos <= time))
                def _(line=line):
                    slot = 3 * line.side + time - 1
                    mine = self.part(line.chunk(3 - time))[...]
                    self.came[slot] = (self.came[slot].astype(f32) + mine.astype(f32)).astype(bf16)
                    self.copy(line, time, False).start()

    def own(self):
        place = pl.ds(self.first_row, self.count)
        self.o_ref[place, :] = self.part(self.lines[0].me)[...].astype(f32)
        for line in self.lines:

            @pl.when(line.pos > 0)
            def _(line=line):
                self.o_ref[place, :] += self.came[3 * line.side + 2].astype(f32)

    def finish(self):
        for line in self.lines:

            @pl.when(line.pos == 0)
            def _(line=line):
                for time in range(3):
                    self.copy(line, time, True).wait_send()

            for time in range(1, 3):

                @pl.when(jnp.logical_and(line.pos > 0, line.pos <= time))
                def _(line=line):
                    self.copy(line, time, False).wait_send()


class Pass:
    def __init__(self, lines, p_ref, o_ref, came, x_ref, ox_ref, sems, work):
        half = came.shape[2]
        self.work = work
        self.sums, self.copies = [], []
        for part in range(2):
            sum_send, sum_recv, copy_local, copy_send, copy_recv = sems[5 * part : 5 * part + 5]
            first_row = part * half
            self.sums.append(LineSum(lines, p_ref, o_ref, came.at[part], sum_send, sum_recv, first_row))
            place = lambda chunk, first_row=first_row: ox_ref.at[
                pl.ds(pl.multiple_of(chunk * 2 * half + first_row, half), half), :
            ]
            source = x_ref.at[pl.ds(first_row, half), :]
            self.copies.append(LineCopy(lines, source, place, copy_local, copy_send, copy_recv))

    def start(self):
        self.sums[0].start()
        self.sums[1].start((0,))

    def turn(self, part):
        self.sums[part].step(3)
        self.sums[part].own()
        self.work(part)
        self.copies[part].start()

    def between(self):
        self.sums[1].start((1, 2))
        self.sums[1].step(1)

    def across(self):
        self.copies[0].step(1)
        self.sums[1].step(2)
        self.copies[0].step(2)

    def last(self):
        self.copies[0].step(3)
        for time in range(1, 4):
            self.copies[1].step(time)

    def finish(self):
        for each in (*self.sums, *self.copies):
            each.finish()


def pass_sems():
    line = pltpu.SemaphoreType.DMA((6,))
    return [line, line, pltpu.SemaphoreType.DMA, line, line] * 2


def column_of(row, count):
    return jnp.broadcast_to(row, (LANES, count)).T[:, 0:1]


def forward_pass_kernel(
    p_any,
    q_ref,
    r_ref,
    gain_ref,
    or_ref,
    ob_ref,
    oi_ref,
    ox_ref,
    p_ref,
    normed,
    came,
    came_q,
    fetch_sem,
    small_send,
    small_recv,
    *sems,
):
    lines = (Line(0), Line(1))
    me = lax.axis_index("tensor")
    others = [{"tensor": lax.rem(me + ahead, 4)} for ahead in (1, 2, 3)]
    fetch = pltpu.make_async_copy(p_any, p_ref, fetch_sem)
    fetch.start()
    greet(others)
    small = [
        remote(q_ref.at[lax.rem(me + slot + 1, 4)], came_q.at[slot], small_send, small_recv, slot, other)
        for slot, other in enumerate(others)
    ]
    for copy in small:
        copy.start()
    count = r_ref.shape[0]
    half = count // 2

    def work(part):
        rows = slice(part * half, (part + 1) * half)
        branch = ob_ref[rows, :] * column_of(oi_ref[0:1, rows], half)
        ob_ref[rows, :] = branch
        fresh = r_ref[rows, :] + branch
        or_ref[rows, :] = fresh
        inverse = lax.rsqrt(jnp.mean(fresh * fresh, -1, keepdims=True) + epsilon)
        normed[rows, :] = (fresh * inverse * gain_ref[0:1, :]).astype(bf16)

    line_pass = Pass(lines, p_ref, ob_ref, came, normed, ox_ref, sems, work)
    fetch.wait()
    line_pass.start()
    for copy in small:
        copy.wait_recv()
    oi_ref[...] = lax.rsqrt((q_ref[me] + came_q[0] + came_q[1] + came_q[2]) * (1.0 / INNER) + epsilon)
    line_pass.sums[0].step(1)
    line_pass.sums[0].step(2)
    line_pass.turn(0)
    line_pass.between()
    line_pass.across()
    line_pass.turn(1)
    line_pass.last()
    line_pass.finish()
    for copy in small:
        copy.wait_send()


def forward_pass(partial, squares, residual, in_gain):
    count, columns = residual.shape
    if not kernels_fit():
        summed, scale = plain_scatter(partial, squares)
        branch = summed * scale[0][:, None]
        fresh = residual + branch
        inverse = lax.rsqrt(jnp.mean(fresh * fresh, -1, keepdims=True) + epsilon)
        normed = (fresh * inverse * in_gain).astype(bf16)
        return fresh, branch, scale, lax.all_gather(normed, "tensor", axis=0, tiled=True)
    vmem = pl.BlockSpec(memory_space=pltpu.VMEM)
    anywhere = pl.BlockSpec(memory_space=pl.ANY)
    return pl.pallas_call(
        forward_pass_kernel,
        out_shape=(
            jax.ShapeDtypeStruct((count, columns), f32),
            jax.ShapeDtypeStruct((count, columns), f32),
            jax.ShapeDtypeStruct((8, count), f32),
            jax.ShapeDtypeStruct((4 * count, columns), bf16),
        ),
        in_specs=[anywhere, vmem, vmem, vmem],
        out_specs=(vmem, vmem, vmem, anywhere),
        scratch_shapes=[
            pltpu.VMEM(partial.shape, bf16),
            pltpu.VMEM((count, columns), bf16),
            pltpu.VMEM((2, 6, count // 2, columns), bf16),
            pltpu.VMEM((3, 8, count), f32),
            pltpu.SemaphoreType.DMA,
            pltpu.SemaphoreType.DMA((3,)),
            pltpu.SemaphoreType.DMA((3,)),
            *pass_sems(),
        ],
        compiler_params=pltpu.CompilerParams(
            collective_id=2, has_side_effects=True, vmem_limit_bytes=40 * 2**20
        ),
        cost_estimate=pl.CostEstimate(flops=0, bytes_accessed=250 * 2**20, transcendentals=0),
    )(partial, squares, residual, jnp.broadcast_to(in_gain[None], (8, columns)))


def scatter_kernel(
    p_ref,
    q_ref,
    x_ref,
    r_ref,
    or_ref,
    ox_ref,
    rd_ref,
    o_ref,
    oq_ref,
    came,
    came_q,
    send_sem,
    recv_sem,
    small_send,
    small_recv,
    local_sem,
    copy_send,
    copy_recv,
    scalars,
    rd_local,
    rd_send,
    rd_recv,
):
    lines = (Line(0), Line(1))
    me = lax.axis_index("tensor")
    others = [{"tensor": lax.rem(me + ahead, 4)} for ahead in (1, 2, 3)]
    greet(others)
    small = [
        remote(q_ref.at[lax.rem(me + slot + 1, 4)], came_q.at[slot], small_send, small_recv, slot, other)
        for slot, other in enumerate(others)
    ]
    for copy in small:
        copy.start()
    rows = x_ref.shape[0]
    place = lambda chunk: rows_at(ox_ref, chunk, rows)
    total = LineSum(lines, p_ref, o_ref, came, send_sem, recv_sem)
    streams = [LineCopy(lines, x_ref, place, local_sem, copy_send, copy_recv), total]
    for stream in streams:
        stream.start()
    for copy in small:
        copy.wait_recv()
    oq_ref[...] = q_ref[me] + came_q[0] + came_q[1] + came_q[2]
    for time in range(1, 4):
        for stream in streams:
            stream.step(time)
    total.own()
    inverse = lax.rsqrt(oq_ref[...] * (1.0 / INNER) + epsilon)
    products = x_ref[...].astype(f32) * o_ref[...]
    dots = dot_exact(jnp.ones((8, products.shape[1]), f32), products, NT) * inverse
    first_row = lax.broadcasted_iota(jnp.int32, scalars.shape, 0) == 0
    scalars[...] = jnp.where(first_row, inverse, dots)
    copies = [remote(scalars, rd_ref.at[me], rd_send, rd_recv, slot, other) for slot, other in enumerate(others)]
    copies.append(pltpu.make_async_copy(scalars, rd_ref.at[me], rd_local))
    for copy in copies:
        copy.start()
    or_ref[...] = r_ref[...] + o_ref[...] * column_of(inverse[0:1, :], rows)
    for stream in streams:
        stream.finish()
    for copy in small:
        copy.wait_send()
    for copy in copies:
        copy.wait()


def plain_scatter(partial, extra):
    total = lax.psum_scatter(partial, "tensor", scatter_dimension=0, tiled=True).astype(f32)
    flat = jnp.transpose(extra, (0, 2, 1)).reshape(partial.shape[0], 8)
    side = lax.psum_scatter(flat, "tensor", scatter_dimension=0, tiled=True).T
    return total, lax.rsqrt(side / INNER + epsilon)


def last_scatter(partial, extra, rows, residual):
    if not kernels_fit():
        total, inverse = plain_scatter(partial, extra)
        dots = jnp.sum(rows.astype(f32) * total, -1)[None] * inverse
        scalars = jnp.concatenate([inverse[:1], dots[1:]])
        return (
            residual + total * inverse[0][:, None],
            lax.all_gather(rows, "tensor", axis=0, tiled=True),
            lax.all_gather(scalars, "tensor", axis=0),
        )
    count, columns = partial.shape[0] // 4, partial.shape[1]
    vmem = pl.BlockSpec(memory_space=pltpu.VMEM)
    anywhere = pl.BlockSpec(memory_space=pl.ANY)
    return pl.pallas_call(
        scatter_kernel,
        out_shape=(
            jax.ShapeDtypeStruct((count, columns), f32),
            jax.ShapeDtypeStruct((4 * rows.shape[0], rows.shape[1]), rows.dtype),
            jax.ShapeDtypeStruct((4, 8, count), f32),
        ),
        in_specs=[vmem] * 4,
        out_specs=(vmem, anywhere, vmem),
        scratch_shapes=[
            pltpu.VMEM((count, columns), f32),
            pltpu.VMEM((8, count), f32),
            pltpu.VMEM((6, count, columns), bf16),
            pltpu.VMEM((3, 8, count), f32),
            pltpu.SemaphoreType.DMA((6,)),
            pltpu.SemaphoreType.DMA((6,)),
            pltpu.SemaphoreType.DMA((3,)),
            pltpu.SemaphoreType.DMA((3,)),
            pltpu.SemaphoreType.DMA,
            pltpu.SemaphoreType.DMA((6,)),
            pltpu.SemaphoreType.DMA((6,)),
            pltpu.VMEM((8, count), f32),
            pltpu.SemaphoreType.DMA,
            pltpu.SemaphoreType.DMA((3,)),
            pltpu.SemaphoreType.DMA((3,)),
        ],
        compiler_params=pltpu.CompilerParams(
            collective_id=5, has_side_effects=True, vmem_limit_bytes=32 * 2**20
        ),
        cost_estimate=pl.CostEstimate(flops=0, bytes_accessed=150 * 2**20, transcendentals=0),
    )(partial, extra, rows, residual)


def near_rows(rows):
    return -(-rows // 32) * 16


class Blocks:
    def __init__(self, source, result, owners, send_sem, recv_sem, local_sem):
        self.source, self.result, self.owners = source, result, owners
        self.send_sem, self.recv_sem, self.local_sem = send_sem, recv_sem, local_sem
        self.index = lax.axis_index("dp")

    def copy(self, slot):
        return pltpu.make_async_remote_copy(
            src_ref=self.source.at[slot],
            dst_ref=self.result.at[self.index],
            send_sem=self.send_sem.at[slot],
            recv_sem=self.recv_sem.at[self.index],
            device_id={"dp": self.owners[slot]},
            device_id_type=MESH,
        )

    def own(self, slot):
        return pltpu.make_async_copy(self.source.at[slot], self.result.at[self.owners[slot]], self.local_sem)

    def start(self):
        for slot, owner in enumerate(self.owners):

            @pl.when(self.index != owner)
            def _(slot=slot):
                self.copy(slot).start()

            @pl.when(self.index == owner)
            def _(slot=slot):
                self.own(slot).start()

    def arrive(self):
        for slot, owner in enumerate(self.owners):

            @pl.when(self.index == owner)
            def _(slot=slot, owner=owner):
                self.own(slot).wait()
                for sender in range(8):
                    if sender != owner:
                        place = self.result.at[sender]
                        where = {"dp": lax.rem(self.index + 1, 8)}
                        remote(place, place, self.recv_sem, self.recv_sem, sender, where).wait_recv()

    def finish(self):
        for slot, owner in enumerate(self.owners):

            @pl.when(self.index != owner)
            def _(slot=slot):
                self.copy(slot).wait_send()


def owners_of(layer):
    if not kernels_fit():
        return tuple(range(3 * layer, 3 * layer + 3))
    return ((1, 3, 6), (0, 2, 4))[layer]


class SquareSum:
    def __init__(self, g_ref, sib, relay, came, send_sem, recv_sem):
        self.g_ref, self.sib, self.relay, self.came = g_ref, sib, relay, came
        self.send_sem, self.recv_sem = send_sem, recv_sem
        self.rows = sib.shape[1]
        self.index, self.core, self.sibling, self.by_x, self.by_y = neighbours()
        self.chip = lax.div(self.index, 2)
        self.chip_x, self.chip_y = lax.div(self.by_x, 2), lax.div(self.by_y, 2)
        self.chip_far = 3 - self.chip
        split = near_rows(self.rows)
        self.near = pl.ds(0, split)
        self.far = pl.ds(split, self.rows - split)

    def send(self, source, target, slot, where):
        return remote(source, target, self.send_sem, self.recv_sem, slot, {"dp": where})

    def to_sibling(self, chip):
        theirs = 2 * chip + 1 - self.core
        return self.send(rows_at(self.g_ref, theirs, self.rows), self.sib.at[chip], chip, self.sibling)

    def start(self):
        for chip in range(4):
            self.to_sibling(chip).start()

    def add(self, chip):
        self.sib[chip] = (
            self.sib[chip].astype(f32) + rows_at(self.g_ref, 2 * chip + self.core, self.rows)[...].astype(f32)
        ).astype(bf16)

    def copy(self, slot):
        sib, far, near_half, far_half = self.sib, self.chip_far, self.near, self.far
        source, target, where = {
            4: (sib.at[far, near_half, :], self.relay.at[near_half, :], self.by_x),
            5: (sib.at[far, far_half, :], self.relay.at[far_half, :], self.by_y),
            6: (sib.at[self.chip_x, near_half, :], self.came.at[0, near_half, :], self.by_x),
            7: (sib.at[self.chip_y, far_half, :], self.came.at[1, far_half, :], self.by_y),
            8: (sib.at[self.chip_x, far_half, :], self.came.at[0, far_half, :], self.by_x),
            9: (sib.at[self.chip_y, near_half, :], self.came.at[1, near_half, :], self.by_y),
        }[slot]
        return self.send(source, target, slot, where)

    def cores(self):
        for chip in range(4):
            self.to_sibling(chip).wait_recv()
        self.add(self.chip_far)
        self.copy(4).start()
        self.copy(5).start()
        self.add(self.chip_x)
        self.copy(6).start()
        self.add(self.chip_y)
        self.copy(7).start()

    def join(self):
        self.copy(4).wait_recv()
        near = (self.sib[self.chip_y, self.near, :].astype(f32) + self.relay[self.near, :].astype(f32)).astype(bf16)
        self.sib[self.chip_y, self.near, :] = near
        self.copy(9).start()
        self.copy(5).wait_recv()
        far = (self.sib[self.chip_x, self.far, :].astype(f32) + self.relay[self.far, :].astype(f32)).astype(bf16)
        self.sib[self.chip_x, self.far, :] = far
        self.copy(8).start()

    def finish(self):
        for slot in range(6, 10):
            self.copy(slot).wait_recv()
        own = rows_at(self.g_ref, self.index, self.rows)[...].astype(f32) + self.sib[self.chip].astype(f32)
        for slot in range(4, 10):
            self.copy(slot).wait_send()
        for chip in range(4):
            self.to_sibling(chip).wait_send()
        return own + (self.came[0].astype(f32) + self.came[1].astype(f32))


def exchange_kernel(
    p_any,
    x_any,
    d_any,
    dr_any,
    sc_any,
    mi_ref,
    mo_ref,
    l_ref,
    r_ref,
    gain_ref,
    *refs,
    gathers,
):
    if gathers:
        (b_ref, i_ref), refs = refs[:2], refs[2:]
    (ni_ref, no_ref, slots_ref, os_ref, or_ref, og_ref), refs = refs[:6], refs[6:]
    if gathers:
        (ox_ref, rd_ref, early_ref), refs = refs[:3], refs[3:]
    o_ref, refs = refs[0], refs[1:]
    (p_ref, x_ref, d_ref, dr_ref, sc_ref, g_ref, h_ref, s_ref, fetch_sem), refs = refs[:9], refs[9:]
    square, refs = refs[:15], refs[15:]
    lines = (Line(0), Line(1))
    me = lax.axis_index("tensor")
    index, core, sibling, by_x, by_y = neighbours()
    fetches = [
        pltpu.make_async_copy(source, target, fetch_sem.at[slot])
        for slot, (source, target) in enumerate(
            ((p_any, p_ref), (x_any, x_ref), (d_any, d_ref), (dr_any, dr_ref), (sc_any, sc_ref))
        )
    ]
    for fetch in fetches:
        fetch.start()
    near_tensor = [{"tensor": lax.rem(me + 1, 4)}, {"tensor": lax.rem(me + 3, 4)}]
    if gathers:
        greet([*near_tensor, *[{"dp": lax.rem(index + ahead, 8)} for ahead in range(1, 8)]])
    else:
        greet([*near_tensor, {"dp": sibling}, {"dp": by_x}, {"dp": by_y}])
    sums = [SquareSum(ref, *square[5 * at : 5 * at + 5]) for at, ref in enumerate((g_ref, h_ref, s_ref))]
    og_ref[...] = jnp.zeros_like(og_ref)
    half = o_ref.shape[0] // 2

    def input_part(rows):
        d_normed = o_ref[rows, :]
        layer_in = l_ref[rows, :]
        inverse = lax.rsqrt(jnp.mean(layer_in * layer_in, -1, keepdims=True) + epsilon)
        scaled = layer_in * inverse
        og_ref[0:1, :] += jnp.sum(d_normed * scaled, 0, keepdims=True)
        d_scaled = d_normed * gain_ref[0:1, :]
        fresh = r_ref[rows, :] + inverse * (d_scaled - scaled * jnp.mean(d_scaled * scaled, -1, keepdims=True))
        or_ref[rows, :] = fresh
        return fresh

    if gathers:
        came, low_grad, scalars, rd_local, rd_send, rd_recv, *refs = refs
        blocks = Blocks(slots_ref, early_ref, owners_of(1), *refs[:3])
        line_sems = refs[3:]

        def work(part):
            rows = slice(part * half, (part + 1) * half)
            low = input_part(rows).astype(bf16)
            low_grad[rows, :] = low
            products = low.astype(f32) * b_ref[rows, :]
            dots = dot_exact(jnp.ones((8, products.shape[1]), f32), products, NT)
            first_row = lax.broadcasted_iota(jnp.int32, dots.shape, 0) == 0
            scalars[:, rows] = jnp.where(first_row, i_ref[:, rows], dots)

        line_pass = Pass(lines, p_ref, o_ref, came, low_grad, ox_ref, line_sems, work)
        total = line_pass.sums[0]
        small = LineCopy(lines, scalars, lambda chunk: rd_ref.at[chunk], rd_local, rd_send, rd_recv)
    else:
        total = LineSum(lines, p_ref, o_ref, *refs)
    fetches[0].wait()
    if gathers:
        line_pass.start()
    else:
        total.start()
    for fetch in fetches[1:]:
        fetch.wait()
    width = mo_ref.shape[1]
    share = x_ref.shape[1] // 4

    def grads(chip):
        rows = slice(chip * share, (chip + 1) * share)
        left = x_ref[:, rows]
        for at in range(0, 2 * width, 2 * LANES):
            cols = slice(at, at + 2 * LANES)
            g_ref[rows, cols] = dot(left, d_ref[:, cols], TN).astype(bf16)
        sums[0].to_sibling(chip).start()
        left = dr_ref[:, rows]
        for at in range(0, width, 2 * LANES):
            cols = slice(at, at + 2 * LANES)
            h_ref[rows, cols] = dot(left, sc_ref[:, cols], TN).astype(bf16)
        sums[1].to_sibling(chip).start()

    grads(0)
    grads(1)
    if gathers:
        total.step(1)
    grads(2)
    grads(3)
    heads = HEADS // 4
    to = lax.broadcasted_iota(jnp.int32, (LANES, LANES), 0)
    source = lax.broadcasted_iota(jnp.int32, (LANES, LANES), 1)
    moved = jnp.where(jnp.logical_and(to == source + me * heads, source < heads), 1.0, 0.0).astype(bf16)
    both = d_ref[:, 2 * width : 2 * width + 2 * STATE]
    steps = d_ref[:, 2 * width + 2 * STATE :]
    for at in range(0, s_ref.shape[1], 2 * LANES):
        cols = slice(at, at + 2 * LANES)
        s_ref[: 2 * STATE, cols] = dot(both, x_ref[:, cols], TN).astype(bf16)
        s_ref[2 * STATE :, cols] = dot(moved, dot(steps, x_ref[:, cols], TN).astype(bf16)).astype(bf16)
    sums[2].start()
    if gathers:
        total.step(2)
    for each in sums:
        each.cores()
    if gathers:
        line_pass.turn(0)
        line_pass.between()
    else:
        total.step(1)
    for each in sums:
        each.join()
    if gathers:
        line_pass.across()
        line_pass.turn(1)
        small.start()
    else:
        total.step(2)
    in_grad = sums[0].finish()
    for side in range(2):
        fresh = muon_decay * mi_ref[side] + in_grad[:, side * width : (side + 1) * width]
        ni_ref[side] = fresh
        slots_ref[side] = fresh.astype(bf16)
    fresh = muon_decay * mo_ref[...] + sums[1].finish()
    no_ref[...] = fresh
    slots_ref[2] = fresh.astype(bf16)
    if gathers:
        blocks.start()
    os_ref[...] = sums[2].finish()
    if gathers:
        line_pass.last()
        for time in range(1, 4):
            small.step(time)
        line_pass.finish()
        small.finish()
        blocks.arrive()
        blocks.finish()
    else:
        total.step(3)
        total.own()
        for part in range(2):
            input_part(slice(part * half, (part + 1) * half))
        total.finish()


def exchange(
    partial, gathered, d_all, d_rows, scaled_low, in_momentum, out_momentum, layer_in, grad_resid, in_gain, below=None
):
    rows, width = out_momentum.shape
    if not kernels_fit():
        heads = HEADS // lax.axis_size("tensor")
        in_grad = dot(gathered, d_all[:, : 2 * width], TN).astype(bf16)
        out_grad = dot(d_rows, scaled_low, TN).astype(bf16)
        shared_grad = dot(d_all[:, 2 * width :], gathered, TN).astype(bf16)
        steps_grad = lax.dynamic_update_slice_in_dim(
            jnp.zeros((LANES, D), bf16),
            shared_grad[2 * STATE : 2 * STATE + heads],
            lax.axis_index("tensor") * heads,
            0,
        )
        shared_grad = jnp.concatenate([shared_grad[: 2 * STATE], steps_grad], 0)
        add = lambda v: lax.psum_scatter(v, "dp", scatter_dimension=0, tiled=True).astype(f32)
        in_sum = add(in_grad)
        in_new = muon_decay * in_momentum + jnp.stack([in_sum[:, :width], in_sum[:, width:]])
        out_new = muon_decay * out_momentum + add(out_grad)
        d_normed = lax.psum_scatter(partial, "tensor", scatter_dimension=0, tiled=True).astype(f32)
        grad_resid, d_in_gain = input_step(d_normed, layer_in, grad_resid, in_gain)
        results = (
            in_new,
            out_new,
            jnp.concatenate([in_new, out_new[None]]).astype(bf16),
            add(shared_grad),
            grad_resid,
            d_in_gain,
        )
        if below is None:
            return results
        branch, scale = below
        d_branch = grad_resid.astype(bf16)
        dots = jnp.sum(d_branch.astype(f32) * branch, -1)
        scalars = jnp.concatenate([scale[:1], jnp.broadcast_to(dots[None], (7, dots.shape[0]))])
        return (
            *results,
            lax.all_gather(d_branch, "tensor", axis=0, tiled=True),
            lax.all_gather(scalars, "tensor", axis=0),
            None,
        )
    count, columns = partial.shape[0] // 4, partial.shape[1]
    vmem = pl.BlockSpec(memory_space=pltpu.VMEM)
    anywhere = pl.BlockSpec(memory_space=pl.ANY)
    fetched = (partial, gathered, d_all, d_rows, scaled_low)
    square = []
    shapes = ((D, 2 * width), (D, width), (SHARED_COLS, D))
    for tall, wide in shapes:
        square += [
            pltpu.VMEM((4, tall // 8, wide), bf16),
            pltpu.VMEM((tall // 8, wide), bf16),
            pltpu.VMEM((2, tall // 8, wide), bf16),
            pltpu.SemaphoreType.DMA((10,)),
            pltpu.SemaphoreType.DMA((10,)),
        ]
    line = pltpu.SemaphoreType.DMA((6,))
    out_shape = [
        jax.ShapeDtypeStruct((2, rows, width), f32),
        jax.ShapeDtypeStruct((rows, width), f32),
        jax.ShapeDtypeStruct((3, rows, width), bf16),
        jax.ShapeDtypeStruct((SHARED_COLS // 8, D), f32),
        jax.ShapeDtypeStruct((count, columns), f32),
        jax.ShapeDtypeStruct((8, columns), f32),
    ]
    out_specs = [vmem] * 6
    operands = [*fetched, in_momentum, out_momentum, layer_in, grad_resid, jnp.broadcast_to(in_gain[None], (8, columns))]
    if below is None:
        scratch = [pltpu.VMEM((6, count, columns), bf16), line, line]
    else:
        operands += below
        out_shape += [
            jax.ShapeDtypeStruct((4 * count, columns), bf16),
            jax.ShapeDtypeStruct((4, 8, count), f32),
            jax.ShapeDtypeStruct((8, rows, width), bf16),
        ]
        out_specs += [anywhere, vmem, anywhere]
        scratch = [
            pltpu.VMEM((2, 6, count // 2, columns), bf16),
            pltpu.VMEM((count, columns), bf16),
            pltpu.VMEM((8, count), f32),
            pltpu.SemaphoreType.DMA,
            line,
            line,
            pltpu.SemaphoreType.DMA((3,)),
            pltpu.SemaphoreType.DMA((8,)),
            pltpu.SemaphoreType.DMA,
            *pass_sems(),
        ]
    results = pl.pallas_call(
        functools.partial(exchange_kernel, gathers=below is not None),
        out_shape=tuple(out_shape),
        in_specs=[anywhere] * 5 + [vmem] * (len(operands) - 5),
        out_specs=tuple(out_specs),
        scratch_shapes=[
            pltpu.VMEM((count, columns), f32),
            *[pltpu.VMEM(each.shape, bf16) for each in fetched],
            *[pltpu.VMEM(shape, bf16) for shape in shapes],
            pltpu.SemaphoreType.DMA((5,)),
            *square,
            *scratch,
        ],
        compiler_params=pltpu.CompilerParams(
            collective_id=3 if below is None else 7, has_side_effects=True, vmem_limit_bytes=62 * 2**20
        ),
        cost_estimate=pl.CostEstimate(flops=10**10, bytes_accessed=150 * 2**20, transcendentals=0),
    )(*operands)
    return (*results[:5], results[5][0], *results[6:])


def input_step(d_normed, layer_in, grad_resid, in_gain):
    inverse = lax.rsqrt(jnp.mean(layer_in * layer_in, -1, keepdims=True) + epsilon)
    scaled_in = layer_in * inverse
    d_in_gain = jnp.sum(d_normed * scaled_in, 0)
    d_scaled_in = d_normed * in_gain
    grad_resid = grad_resid + inverse * (
        d_scaled_in - scaled_in * jnp.mean(d_scaled_in * scaled_in, -1, keepdims=True)
    )
    return grad_resid, d_in_gain


def tail_kernel(
    s0_ref,
    s1_ref,
    v0_ref,
    v1_ref,
    b_ref,
    early_ref,
    os_ref,
    ov_ref,
    t_ref,
    whole,
    low,
    next_low,
    shifted,
    mine,
    came,
    vsum,
    vcame,
    send_sem,
    recv_sem,
    small_send,
    small_recv,
    block_send,
    block_recv,
    block_local,
):
    me = lax.axis_index("tensor")
    index, core, sibling, by_x, by_y = neighbours()
    beside = me + 1 - 2 * lax.rem(me, 2)
    beyond = lax.rem(me + 2, 4)
    others_dp = [lax.rem(index + ahead, 8) for ahead in range(1, 8)]
    greet([{"tensor": beside}, {"tensor": beyond}, *[{"dp": other} for other in others_dp]])
    rows = b_ref.shape[1]
    blocks = Blocks(b_ref, whole, owners_of(0), block_send, block_recv, block_local.at[0])
    blocks.start()
    idle = index >= 0
    for owner in (*owners_of(0), *owners_of(1)):
        idle = jnp.logical_and(idle, index != owner)

    def stored():
        return pltpu.make_async_copy(early_ref, whole, block_local.at[0])

    def filler(place):
        return pltpu.make_async_copy(b_ref.at[place % 3], whole.at[place], block_local.at[place])

    for owner in owners_of(1):

        @pl.when(index == owner)
        def _():
            stored().start()

    @pl.when(idle)
    def _():
        for place in range(8):
            filler(place).start()

    share = s0_ref.shape[0]
    mine[0, :share, :] = s0_ref[...].astype(bf16)
    mine[0, share:, :] = s1_ref[...].astype(bf16)
    first = remote(mine.at[0], came.at[0], send_sem, recv_sem, 0, {"tensor": beside})
    first.start()
    first.wait()
    mine[1] = (mine[0].astype(f32) + came[0].astype(f32)).astype(bf16)
    second = remote(mine.at[1], came.at[1], send_sem, recv_sem, 1, {"tensor": beyond})
    second.start()
    second.wait()
    os_ref[index] = (mine[1].astype(f32) + came[1].astype(f32)).astype(bf16)

    blocks.arrive()
    for owner in owners_of(1):

        @pl.when(index == owner)
        def _():
            stored().wait()

    @pl.when(idle)
    def _():
        for place in range(8):
            filler(place).wait()

    half = share
    near, far, everything = pl.ds(0, half), pl.ds(half, half), pl.ds(0, 2 * half)

    def send(owner, part, slot, where):
        place = os_ref.at[owner, part, :]
        copy = remote(place, place, send_sem, recv_sem, slot, {"dp": where})
        copy.start()
        return copy

    def small(source, target, slot, where):
        copy = remote(source, target, small_send, small_recv, slot, where)
        copy.start()
        return copy

    width = v0_ref.shape[1]
    vsum[0, :, :width] = v0_ref[...]
    vsum[0, :, width:] = v1_ref[...]
    pending = small(vsum.at[0], vcame.at[0], 0, {"dp": sibling})
    copies = [
        send(index, near, 2, by_x),
        send(index, far, 3, by_y),
        send(index, far, 4, by_x),
        send(index, near, 5, by_y),
        send(index, everything, 8, sibling),
    ]
    squares = jnp.zeros((1, 1), f32)
    for at in range(8):
        part = whole[at].astype(f32)
        squares = squares + jnp.sum(part * part)
    scale = 1.0 / (jnp.sqrt(squares) + 1e-07)
    for at in range(0, 8, 2):
        part = jnp.concatenate([whole[at], whole[at + 1]], 0).astype(f32) * scale
        low[:, at * rows : (at + 2) * rows] = part.T.astype(bf16)
    chains = [(low, next_low, shifted)]
    advance(chains, 0)
    pending.wait()
    vsum[1] = vsum[0] + vcame[0]
    pending = small(vsum.at[1], vcame.at[1], 1, {"dp": by_x})
    copies[0].wait_recv()
    copies.append(send(by_x, near, 6, by_y))
    copies[1].wait_recv()
    copies.append(send(by_y, far, 7, by_x))
    advance(chains, 1)
    pending.wait()
    vsum[2] = vsum[1] + vcame[1]
    pending = small(vsum.at[2], vcame.at[2], 2, {"dp": by_y})
    copies[2].wait_recv()
    copies.append(send(by_x, everything, 9, sibling))
    copies[3].wait_recv()
    copies.append(send(by_y, everything, 10, sibling))
    advance(chains, 0)
    pending.wait()
    ov_ref[me] = vsum[2] + vcame[2]
    pending = small(ov_ref.at[me], ov_ref.at[me], 3, {"tensor": beside})
    copies[5].wait_recv()
    copies[6].wait_recv()
    copies.append(send(by_x + by_y - index, everything, 11, sibling))
    advance(chains, 1)
    pending.wait()
    base = pl.ds(2 * lax.div(me, 2), 2)
    pending = small(ov_ref.at[base], ov_ref.at[base], 4, {"tensor": beyond})
    advance(chains, 0)
    for at in range(0, 8, 2):
        t_ref[at * rows : (at + 2) * rows, :] = next_low[:, at * rows : (at + 2) * rows].astype(f32).T.astype(bf16)
    pending.wait()
    for at in (4, 7, 8, 9):
        copies[at].wait_recv()
    for copy in copies:
        copy.wait_send()
    blocks.finish()


def finish_blocks(shards, vectors, slots, early):
    rows, width = slots[0].shape[1:]
    if not kernels_fit():
        count = lax.axis_size("dp")
        total = lax.psum(jnp.concatenate(shards, 0), "tensor").astype(bf16)
        blocks = jnp.concatenate(slots, 0)
        padded = jnp.pad(blocks, ((0, count - blocks.shape[0]), (0, 0), (0, 0)))
        whole = lax.all_to_all(padded, "dp", split_axis=0, concat_axis=0, tiled=True)
        return (
            lax.all_gather(total, "dp", axis=0),
            lax.all_gather(lax.psum(jnp.concatenate(vectors, 1), "dp"), "tensor", axis=0),
            orthogonal(whole.reshape(D, width), bf16),
        )
    vmem = pl.BlockSpec(memory_space=pltpu.VMEM)
    anywhere = pl.BlockSpec(memory_space=pl.ANY)
    shard = (LAYERS * shards[0].shape[0], shards[0].shape[1])
    vector = (vectors[0].shape[0], LAYERS * vectors[0].shape[1])
    return pl.pallas_call(
        tail_kernel,
        out_shape=(
            jax.ShapeDtypeStruct((8, *shard), bf16),
            jax.ShapeDtypeStruct((4, *vector), f32),
            jax.ShapeDtypeStruct((D, width), bf16),
        ),
        in_specs=[vmem] * 4 + [anywhere] * 2,
        out_specs=(vmem, vmem, vmem),
        scratch_shapes=[
            pltpu.VMEM((8, rows, width), bf16),
            pltpu.VMEM((width, D), bf16),
            pltpu.VMEM((width, D), bf16),
            pltpu.VMEM((width, width), bf16),
            pltpu.VMEM((2, *shard), bf16),
            pltpu.VMEM((2, *shard), bf16),
            pltpu.VMEM((3, *vector), f32),
            pltpu.VMEM((3, *vector), f32),
            pltpu.SemaphoreType.DMA((12,)),
            pltpu.SemaphoreType.DMA((12,)),
            pltpu.SemaphoreType.DMA((5,)),
            pltpu.SemaphoreType.DMA((5,)),
            pltpu.SemaphoreType.DMA((3,)),
            pltpu.SemaphoreType.DMA((8,)),
            pltpu.SemaphoreType.DMA((8,)),
        ],
        compiler_params=pltpu.CompilerParams(
            collective_id=4, has_side_effects=True, vmem_limit_bytes=56 * 2**20
        ),
        cost_estimate=pl.CostEstimate(flops=2 * 10**10, bytes_accessed=100 * 2**20, transcendentals=0),
    )(*shards, *vectors, slots[0], early)


def advance(chains, flip):
    poly_zero = coef_first + coef_second + coef_third
    poly_one = coef_second + 2.0 * coef_third

    def unit(at, count, size):
        rows = lax.broadcasted_iota(jnp.int32, (count, size), 0) + at
        return jnp.where(rows == lax.broadcasted_iota(jnp.int32, (count, size), 1), 1.0, 0.0).astype(f32)

    for *buffers, shifted in chains:
        source = buffers[flip]
        size = source.shape[0]
        for at in range(0, size, 256):
            count = min(256, size - at)
            gram = dot(source[at : at + count, :], source[...], NT)
            shifted[at : at + count, :] = (gram - unit(at, count, size)).astype(bf16)
    for *buffers, shifted in chains:
        source, target = buffers[flip], buffers[1 - flip]
        size = source.shape[0]
        for at in range(0, size, 256):
            count = min(256, size - at)
            mine = shifted[at : at + count, :]
            poly = (
                poly_zero * unit(at, count, size)
                + poly_one * mine.astype(f32)
                + coef_third * dot(mine, shifted[...])
            )
            target[at : at + count, :] = dot(poly.astype(bf16), source[...]).astype(bf16)


def iterate(chains):
    def twice(_, carry):
        advance(chains, 0)
        advance(chains, 1)
        return carry

    lax.fori_loop(0, 2, twice, 0)
    advance(chains, 0)


def orthogonal_kernel(m_ref, o_ref, low, next_low, shifted):
    turned = m_ref[...].astype(f32).T
    scale = 1.0 / (jnp.sqrt(jnp.sum(turned * turned)) + 1e-07)
    low[...] = (turned * scale).astype(bf16)
    iterate([(low, next_low, shifted)])
    o_ref[...] = next_low[...].astype(f32).T.astype(o_ref.dtype)


def shared_step_kernel(m_ref, w_ref, o_ref, low, next_low, shifted):
    for layer in range(LAYERS):
        momentum = m_ref[layer]
        scale = 1.0 / (jnp.sqrt(jnp.sum(momentum * momentum)) + 1e-07)
        low[layer, :SSM_COLS, :] = (momentum * scale).astype(bf16)
        low[layer, SSM_COLS:, :] = jnp.zeros((low.shape[1] - SSM_COLS, D), bf16)
    iterate([(low.at[layer], next_low.at[layer], shifted.at[layer]) for layer in range(LAYERS)])
    rate = muon_rate * (D / SSM_COLS) ** 0.5
    for layer in range(LAYERS):
        o_ref[layer] = w_ref[layer].astype(f32) - rate * next_low[layer, :SSM_COLS, :].astype(f32)


def shared_pair_kernel(m_ref, w_ref, o_ref, low, next_low, shifted, both, send_sem, recv_sem):
    index, core, sibling, by_x, by_y = neighbours()
    greet([{"dp": sibling}])
    momentum = m_ref[core]
    scale = 1.0 / (jnp.sqrt(jnp.sum(momentum * momentum)) + 1e-07)
    low[:SSM_COLS, :] = (momentum * scale).astype(bf16)
    low[SSM_COLS:, :] = jnp.zeros((low.shape[0] - SSM_COLS, D), bf16)
    iterate([(low, next_low, shifted)])
    both[core] = next_low[...]
    copy = remote(both.at[core], both.at[core], send_sem, recv_sem, 0, {"dp": sibling})
    copy.start()
    copy.wait()
    rate = muon_rate * (D / SSM_COLS) ** 0.5
    for layer in range(2):
        o_ref[layer] = w_ref[layer].astype(f32) - rate * both[layer, :SSM_COLS, :].astype(f32)


def shared_step(momentum, weight):
    vmem = pl.BlockSpec(memory_space=pltpu.VMEM)
    padded = -(-SSM_COLS // LANES) * LANES
    pair = kernels_fit() and LAYERS == 2
    if pair:
        scratch = [
            pltpu.VMEM((padded, D), bf16),
            pltpu.VMEM((padded, D), bf16),
            pltpu.VMEM((padded, padded), bf16),
            pltpu.VMEM((2, padded, D), bf16),
            pltpu.SemaphoreType.DMA((1,)),
            pltpu.SemaphoreType.DMA((1,)),
        ]
        params = pltpu.CompilerParams(collective_id=0, has_side_effects=True, vmem_limit_bytes=56 * 2**20)
    else:
        scratch = [
            pltpu.VMEM((LAYERS, padded, D), bf16),
            pltpu.VMEM((LAYERS, padded, D), bf16),
            pltpu.VMEM((LAYERS, padded, padded), bf16),
        ]
        params = pltpu.CompilerParams(vmem_limit_bytes=56 * 2**20)
    return pl.pallas_call(
        shared_pair_kernel if pair else shared_step_kernel,
        out_shape=jax.ShapeDtypeStruct(momentum.shape, f32),
        in_specs=[vmem, vmem],
        out_specs=vmem,
        scratch_shapes=scratch,
        compiler_params=params,
        cost_estimate=pl.CostEstimate(
            flops=20 * padded * padded * (2 * D + padded), bytes_accessed=12 * D * padded, transcendentals=0
        ),
    )(momentum, weight)


def orthogonal(matrix, dtype):
    length, size = matrix.shape
    vmem = pl.BlockSpec(memory_space=pltpu.VMEM)
    return pl.pallas_call(
        orthogonal_kernel,
        out_shape=jax.ShapeDtypeStruct((length, size), dtype),
        in_specs=[vmem],
        out_specs=vmem,
        scratch_shapes=[
            pltpu.VMEM((size, length), bf16),
            pltpu.VMEM((size, length), bf16),
            pltpu.VMEM((size, size), bf16),
        ],
        compiler_params=pltpu.CompilerParams(vmem_limit_bytes=56 * 2**20),
        cost_estimate=pl.CostEstimate(
            flops=10 * size * size * (2 * length + size), bytes_accessed=6 * size * length, transcendentals=0
        ),
    )(matrix)


def body(
    resid_in,
    in_weight,
    out_weight,
    shared_weight,
    small_params,
    in_momentum,
    out_momentum,
    shared_momentum,
    small_first,
    small_second,
    resid_grad,
):
    tensor_index = lax.axis_index("tensor")
    tensor_count = lax.axis_size("tensor")
    local_cols = in_weight.shape[3]
    local_heads = HEADS // tensor_count
    col_start = tensor_index * local_cols
    head_start = tensor_index * local_heads
    shard_rows = in_weight.shape[1]
    own_tokens = resid_in.shape[0]
    length = own_tokens * tensor_count

    row_start = lax.axis_index("dp") * shard_rows
    channels = small_params[:, : (KERNEL + 2) * INNER].reshape(LAYERS, KERNEL + 2, INNER)
    channels = lax.dynamic_slice_in_dim(channels, col_start, local_cols, 2)
    states_at = (KERNEL + 2) * INNER
    heads_at = states_at + (KERNEL + 1) * 2 * STATE
    by_state = small_params[:, states_at:heads_at].reshape(LAYERS, KERNEL + 1, 2 * STATE)
    by_head = small_params[:, heads_at : heads_at + 3 * HEADS].reshape(LAYERS, 3, HEADS)
    by_head = lax.dynamic_slice_in_dim(by_head, head_start, local_heads, 2)
    in_gains = small_params[:, heads_at + 3 * HEADS :]
    skips = jnp.repeat(by_head[:, 2:], WIDTH, axis=2)
    px_all = jnp.concatenate([channels, skips, jnp.zeros((LAYERS, 1, local_cols), f32)], 1)
    ps_all = jnp.pad(by_state, ((0, 0), (0, 8 - KERNEL - 1), (0, 0)))
    ph_all = jnp.pad(by_head[:, :2], ((0, 0), (0, 6), (0, LANES - local_heads)))

    w_in, w_out = [], []
    for layer in range(LAYERS):
        shared_rows = lax.dynamic_slice_in_dim(shared_weight[layer], row_start, shard_rows, 0)
        steps_weight = lax.dynamic_slice_in_dim(shared_rows, 2 * STATE + head_start, local_heads, 1)
        w_rows = jnp.concatenate(
            [
                in_weight[layer, :, 0],
                in_weight[layer, :, 1],
                shared_rows[:, : 2 * STATE],
                jnp.pad(steps_weight, ((0, 0), (0, LANES - local_heads))),
            ],
            1,
        )
        w_in.append(w_rows)
        w_out.append(out_weight[layer])
    in_momentum_planes = jnp.transpose(in_momentum, (0, 2, 1, 3))

    residual = resid_in
    inverse_in = lax.rsqrt(jnp.mean(residual * residual, -1, keepdims=True) + epsilon)
    normed_low = (residual * inverse_in * in_gains[0]).astype(bf16)
    gathered, w_in[0], w_out[0] = gather_first(normed_low, w_in[0], w_out[0])
    held = lax.optimization_barrier((gathered, *w_in[1:], *w_out[1:]))
    gathered = held[0]
    for later in range(1, LAYERS):
        w_in[later] = lax.all_gather(held[later], "dp", axis=0, tiled=True)
        w_out[later] = lax.all_gather(held[LAYERS - 1 + later], "dp", axis=0, tiled=True)
    saved = []
    branches = [None] * LAYERS
    for layer in range(LAYERS):
        projected, total, partial, squares, states = mixer_forward(
            gathered, w_in[layer], w_out[layer], px_all[layer], ps_all[layer], ph_all[layer]
        )
        saved.append((residual, gathered, projected, total, states))
        squares = squares[:, 0, :].reshape(tensor_count, 1, own_tokens)
        squares = jnp.broadcast_to(squares, (tensor_count, 8, own_tokens))
        if layer < LAYERS - 1:
            residual, branch, scale, gathered = forward_pass(partial, squares, residual, in_gains[layer + 1])
            branches[layer] = (branch, scale)
    residual, d_rows, rd = last_scatter(partial, squares, resid_grad.astype(bf16), residual)

    grad_resid = resid_grad
    in_new = [None] * LAYERS
    out_new = [None] * LAYERS
    slots = [None] * LAYERS
    shared_shards = [None] * LAYERS
    small_grads = [None] * LAYERS
    for layer in reversed(range(LAYERS)):
        layer_in, gathered, projected, total, states = saved[layer]
        rd = jnp.transpose(rd[:, :2], (0, 2, 1)).reshape(length, 2)
        d_all, scaled_low, partial, grad_x, grad_s, grad_h = mixer_backward(
            d_rows, w_in[layer], w_out[layer], projected, total, states, rd, px_all[layer], ps_all[layer], ph_all[layer]
        )
        results = exchange(
            partial,
            gathered,
            d_all,
            d_rows,
            scaled_low,
            in_momentum_planes[layer],
            out_momentum[layer],
            layer_in,
            grad_resid,
            in_gains[layer],
            branches[layer - 1] if layer > 0 else None,
        )
        in_new[layer], out_new[layer], slots[layer], shared_shards[layer], grad_resid, d_in_gain = results[:6]
        if layer > 0:
            d_rows, rd, early = results[6:]
        small_grads[layer] = jnp.concatenate([grad_x, grad_s, grad_h, d_in_gain.reshape(8, D // 8)], 1)

    in_momentum_new = jnp.transpose(jnp.stack(in_new), (0, 2, 1, 3))
    out_momentum_new = jnp.stack(out_new)
    dp_count = lax.axis_size("dp")
    shared_total, vectors, turned = finish_blocks(shared_shards, small_grads, slots, early)
    turned = turned.reshape(dp_count, shard_rows, local_cols)
    returned = lax.all_to_all(turned, "dp", split_axis=0, concat_axis=0, tiled=True)
    scale = muon_rate * (D / local_cols) ** 0.5
    in_weight_new, out_weight_new = [], []
    for layer in range(LAYERS):
        gate, x, out = (returned[owner].astype(f32) * scale for owner in owners_of(layer))
        in_weight_new.append(in_weight[layer].astype(f32) - jnp.stack([gate, x], 1))
        out_weight_new.append(out_weight[layer].astype(f32) - out)
    in_weight_new, out_weight_new = jnp.stack(in_weight_new), jnp.stack(out_weight_new)

    share = SHARED_COLS // dp_count
    shared_total = shared_total.reshape(dp_count, LAYERS, share, D)
    shared_total = jnp.transpose(shared_total, (1, 0, 2, 3)).reshape(LAYERS, SHARED_COLS, D)[:, :SSM_COLS]
    turned_momentum = muon_decay * jnp.transpose(shared_momentum, (0, 2, 1)) + shared_total.astype(f32)
    shared_momentum_new = jnp.transpose(turned_momentum, (0, 2, 1))
    shared_weight_new = jnp.transpose(
        shared_step(turned_momentum, jnp.transpose(shared_weight, (0, 2, 1))), (0, 2, 1)
    )
    small_rows = []
    for layer in range(LAYERS):
        width = local_cols + 2 * STATE + LANES + D // 8
        mine = vectors[:, :, layer * width : (layer + 1) * width]
        channel_grads = jnp.transpose(mine[:, :7, :local_cols], (1, 0, 2)).reshape(7, INNER)
        head_grads = jnp.transpose(mine[:, :2, local_cols + 2 * STATE :][:, :, :local_heads], (1, 0, 2))
        common = jnp.sum(mine, 0)
        state_grads = common[: KERNEL + 1, local_cols : local_cols + 2 * STATE]
        small_rows.append(
            jnp.concatenate(
                [
                    channel_grads[: KERNEL + 2].reshape(-1),
                    state_grads.reshape(-1),
                    head_grads.reshape(-1),
                    channel_grads[6].reshape(HEADS, WIDTH).sum(1),
                    common[:, local_cols + 2 * STATE + LANES :].reshape(-1),
                ]
            )
        )
    small_grad = jnp.stack(small_rows)
    first_new = beta_first * small_first + (1.0 - beta_first) * small_grad
    small_second_new = beta_second * small_second + (1.0 - beta_second) * small_grad * small_grad
    small_new = small_params - adam_rate * (first_new / (1.0 - beta_first**STEP)) / (
        jnp.sqrt(small_second_new / (1.0 - beta_second**STEP)) + 1e-08
    )
    return (
        residual,
        grad_resid,
        small_grad,
        small_second_new,
        small_new,
        in_momentum_new,
        in_weight_new,
        out_momentum_new,
        out_weight_new,
        shared_momentum_new,
        shared_weight_new,
    )


def solution(mesh):
    placed = (
        P(("dp", "tensor"), None),
        P(None, "dp", None, "tensor"),
        P(None, "dp", "tensor"),
        P(),
        P(),
        P(None, "dp", None, "tensor"),
        P(None, "dp", "tensor"),
        P(),
        P(),
        P(),
        P(("dp", "tensor"), None),
    )
    return jax.shard_map(
        body,
        mesh=mesh,
        in_specs=placed,
        out_specs=(
            P(("dp", "tensor"), None),
            P(("dp", "tensor"), None),
            P(),
            P(),
            P(),
            P(None, "dp", None, "tensor"),
            P(None, "dp", None, "tensor"),
            P(None, "dp", "tensor"),
            P(None, "dp", "tensor"),
            P(),
            P(),
        ),
        check_vma=False,
    )
```
